32 devices in a mesh: dp: 4 (over y, core), pool: 8 (over z, x).
Axes of the slice: x: 2, y: 2, z: 4, core: 2. Of those that a mesh axis runs over, the one named last changes fastest.
Arguments:
- feats: bfloat16 [8192, 2048], P(('dp', 'pool')), may hold values from -6 to 6
- tower_w: bfloat16 [2048, 256], replicated, may hold values from -0.125 to 0.125
- partners: int32 [8192], P(('dp', 'pool')), may hold values from 0 to 2047, as said below
- popularity_buckets: int32 [8192], P(('dp', 'pool')), may hold values from 0 to 31
- row_counts: int32 [4, 8], replicated, may hold values from 64 to 256, as said below
Outputs:
- grad_w: float32 [2048, 256], P(('dp', 'pool'))
The draws below stay inside these ranges and needn't reach their ends.
Inputs may be any that keep to these rules, and one draw needn't show every extreme that they name: row_counts[d, p] valid slots stand first in the block of 256 slots of pool member p in data group d; in every data group some member has all 256 slots valid. `partners`: each slot's partner is the position, within its data group's 2048 slots, of a valid slot other than itself.
All inputs are finite; a program needn't handle non-finite values.
Results may differ from the reference program's by a relative error of at most 0.0038.
The reference program's roundings to bfloat16 on the way count: a program that leaves them out, or rounds other values in their place, can miss the bound.
Values may be sent and summed in bfloat16 or wider, within the bound.
No kernel may reach another device: no remote copies, remote signals or barrier semaphores. Data moves between devices by JAX's collectives and lax.ppermute only.
A program may use at most 64 MiB of HBM per device.

```python
import jax
import jax.numpy as jnp
from jax import lax

DIN = 2048
DE = 256
ROWS_DEV = 256
NBINS = 32
VIEWS = 2048
ROWS = 8192
N_DP = 4
N_POOL = 8


def tally_matrix(key):
    base_key = jax.random.fold_in(key, 7001)
    lowest = ROWS_DEV // 4
    counts = jax.random.randint(jax.random.fold_in(base_key, 1), (N_DP, N_POOL), lowest, ROWS_DEV + 1)
    full_at = jax.random.randint(jax.random.fold_in(base_key, 2), (N_DP,), 0, N_POOL)
    full_at = jnp.where(jnp.arange(N_DP) == 0, N_POOL - 1, full_at)
    members = jnp.arange(N_POOL)[None, :]
    counts = jnp.where(members == full_at[:, None], ROWS_DEV, counts)
    empty_at = (full_at[0] + 1) % N_POOL
    first_group = jnp.arange(N_DP)[:, None] == 0
    counts = jnp.where(first_group & (members == empty_at), lowest, counts)
    return counts.astype(jnp.int32)


def draw_row_counts(key, part):
    return tally_matrix(key)


def draw_partners(key, part):
    counts = tally_matrix(key)
    base_key = jax.random.fold_in(key, 7002)
    owner_index = jax.random.randint(jax.random.fold_in(base_key, 1), (N_DP, VIEWS), 0, N_POOL)
    available = jnp.take_along_axis(counts, owner_index, axis=1)
    raw_bits = jax.random.randint(jax.random.fold_in(base_key, 2), (N_DP, VIEWS), 0, 1 << 30)
    local_row = raw_bits % available
    picked = owner_index * ROWS_DEV + local_row
    own_index = jnp.arange(VIEWS)[None, :]
    picked = jnp.where(picked == own_index, owner_index * ROWS_DEV + (local_row + 1) % available, picked)
    group_rows = jnp.arange(N_DP)[:, None]
    picked = jnp.where((group_rows == 0) & (own_index == 0), VIEWS - 1, picked)
    picked = jnp.where((group_rows == 0) & (own_index == VIEWS - 1), 0, picked)
    return picked.reshape(N_DP * VIEWS).astype(jnp.int32)


def set_ends(result, stream_key, least, high):
    extent = result.shape
    index_at = [jax.random.randint(jax.random.fold_in(stream_key, axis), (), 0, extent[axis]) for axis in range(len(extent))]
    result = result.at[tuple(index_at)].set(least)
    longest = extent.index(max(extent))
    index_at[longest] = (index_at[longest] + 1) % extent[longest]
    return result.at[tuple(index_at)].set(high)


def raised(entries, key, source, target, blocks, factor):
    def block_of(axis_at):
        return (jnp.arange(entries.shape[axis_at]) // (entries.shape[axis_at] // blocks)).reshape((-1,) + (1,) * (entries.ndim - 1 - axis_at))

    one_side = jax.random.permutation(key, blocks)[block_of(target)]
    second = (block_of(target) + blocks // 2) % blocks
    return jnp.where((block_of(source) == one_side) | (block_of(source) == second), factor * entries, entries)


def block_levels(stream_key, dims, split, least, high):
    def one(axis_at, blocks):
        steps = jax.random.uniform(jax.random.fold_in(jax.random.fold_in(stream_key, 6), axis_at), (blocks,), jnp.float32, least / len(split), high / len(split))
        return jnp.repeat(jnp.exp(steps), dims[axis_at] // blocks).reshape((-1,) + (1,) * (len(dims) - axis_at - 1))

    gain = one(*split[0])
    for cut in split[1:]:
        gain = gain * one(*cut)
    return gain


def scatter_about(rng, shape, spread, most, shards=(), kind=jnp.bfloat16):
    values = spread * jax.random.normal(rng, shape, jnp.float32)
    if shards:
        values = values * block_levels(rng, shape, shards, -0.22, 0.18)
    return jnp.clip(values, -most, most).astype(kind)


def heavy_noise(own_key, shape, deviation, most, cuts, heavy, held_as=jnp.bfloat16):
    array = deviation * jax.random.normal(own_key, shape, jnp.float32)
    if cuts:
        array = array * block_levels(own_key, shape, cuts, -0.22, 0.18)
    return jnp.clip(raised(array, jax.random.fold_in(own_key, 3), *heavy), -most, most).astype(held_as)


def setup_inputs(seed: int = 0) -> dict:
    streams_of = jax.random.split(jax.random.key(seed), 6)
    return {
        "feats": heavy_noise(streams_of[0], (ROWS, DIN), 1.0, 6.0, ((0, 32),), (0, 1, 32, 2.75)),
        "tower_w": scatter_about(streams_of[1], (DIN, DE), DIN ** -0.5, 0.125),
        "partners": draw_partners(jax.random.fold_in(streams_of[5], 71), 0),
        "popularity_buckets": set_ends(jax.random.randint(streams_of[3], (ROWS,), 0, NBINS), jax.random.fold_in(streams_of[3], 1), 0, NBINS - 1).astype(jnp.int32),
        "row_counts": draw_row_counts(jax.random.fold_in(streams_of[5], 71), 0),
    }


sharpness_scaler = 0.05
epsilon = 1e-06

def group_grad(embedded, prior_occurrence_correction, partners, perspective_usable):
    group_rows = embedded.shape[0]
    emb_float = embedded.astype(jnp.float32)
    angular_affinities = jnp.dot(emb_float, emb_float.T, preferred_element_type=jnp.float32)
    position = jnp.arange(group_rows, dtype=jnp.int32)
    admitted_flags = perspective_usable[None, :] & (position[:, None] != position[None, :])
    natural_powers = jnp.where(admitted_flags, jnp.exp(angular_affinities / sharpness_scaler - prior_occurrence_correction.astype(jnp.float32)[None, :]), 0.0)
    normalizer_sums = lax.optimization_barrier(jnp.sum(natural_powers, axis=1, keepdims=True))
    matched_partner = (partners[:, None] == position[None, :]).astype(jnp.float32)
    pair_multiplier = jnp.where(perspective_usable[:, None], natural_powers / normalizer_sums - matched_partner, 0.0).astype(jnp.bfloat16)
    pair_multiplier = lax.optimization_barrier(pair_multiplier).astype(jnp.float32)
    return jnp.dot(pair_multiplier, emb_float, preferred_element_type=jnp.float32) + jnp.dot(pair_multiplier.T, emb_float, preferred_element_type=jnp.float32)

def reference(feats, tower_w, partners, popularity_buckets, row_counts):
    projected = jnp.dot(feats, tower_w, preferred_element_type=jnp.float32)
    inv_norm = lax.rsqrt(lax.optimization_barrier(jnp.sum(projected * projected, axis=1, keepdims=True)) + epsilon)
    normed = projected * inv_norm
    embedded = normed.astype(jnp.bfloat16)
    prior_occurrence_correction = (-(popularity_buckets.astype(jnp.float32) + 0.5) / 4.0).astype(jnp.bfloat16)
    position_index = jnp.arange(VIEWS, dtype=jnp.int32) % ROWS_DEV
    owner_index = jnp.arange(VIEWS, dtype=jnp.int32) // ROWS_DEV
    perspective_usable = position_index[None, :] < row_counts[:, owner_index]
    packed = (embedded.reshape(N_DP, VIEWS, DE), prior_occurrence_correction.reshape(N_DP, VIEWS), partners.reshape(N_DP, VIEWS), perspective_usable)
    group_grads = lax.map(lambda operand_tensors: group_grad(*operand_tensors), packed)
    grad_emb = group_grads.reshape(ROWS, DE)
    grad_proj = ((grad_emb - normed * lax.optimization_barrier(jnp.sum(normed * grad_emb, axis=1, keepdims=True))) * inv_norm).astype(jnp.bfloat16)
    return lax.dot_general(feats, grad_proj, (((0,), (0,)), ((), ())), preferred_element_type=jnp.float32)
```

```python
import functools
import math

import jax
import jax.numpy as jnp
from jax import lax
from jax.experimental import pallas as pl
from jax.experimental.pallas import tpu as pltpu
from jax.sharding import PartitionSpec as P

sharpness_scaler = 0.05
epsilon = 1e-06
META = 16
DIGIT_BITS = 8
DIGIT = 1 << DIGIT_BITS
EXP2_SCALE = math.log2(math.e) / sharpness_scaler
LOG2E = math.log2(math.e)
VMEM_LIMIT = 48 * 1024 * 1024

VMEM = pl.BlockSpec(memory_space=pltpu.VMEM)
SMEM = pl.BlockSpec(memory_space=pltpu.SMEM)
ANY = pl.BlockSpec(memory_space=pl.ANY)


def f32_dot(left, right, dims):
    return lax.dot_general(left, right, (dims, ((), ())), preferred_element_type=jnp.float32)


def column_of(row):
    return jnp.transpose(jnp.broadcast_to(row, (128, row.shape[1])))


def project_kernel(chunks, feats_hbm, w_hbm, partners_ref, buckets_ref, msg_ref, normed_ref, inv_ref,
                   feats_v, w_v, sems):
    rows, din = feats_v.shape
    width = w_v.shape[1]
    step = din // chunks
    copies = []
    for c in range(chunks):
        cut = pl.ds(c * step, step)
        pair = (
            pltpu.make_async_copy(feats_hbm.at[:, cut], feats_v.at[:, cut], sems.at[0, c]),
            pltpu.make_async_copy(w_hbm.at[cut, :], w_v.at[cut, :], sems.at[1, c]),
        )
        pair[0].start()
        pair[1].start()
        copies.append(pair)
    partners = partners_ref[...]
    logq = -(buckets_ref[...].astype(jnp.float32) + 0.5) / 4.0
    high = (partners >> DIGIT_BITS).astype(jnp.float32)
    low = (partners & (DIGIT - 1)).astype(jnp.float32)
    kinds = lax.broadcasted_iota(jnp.int32, (META, rows), 0)
    meta = jnp.where(kinds == 0, logq, jnp.where(kinds == 1, high, jnp.where(kinds == 2, low, 0.0)))
    msg_ref[pl.ds(rows, META), :] = meta.astype(jnp.bfloat16)
    projected = jnp.zeros((rows, width), jnp.float32)
    for c in range(chunks):
        copies[c][0].wait()
        copies[c][1].wait()
        cut = pl.ds(c * step, step)
        projected = projected + jnp.dot(feats_v[:, cut], w_v[cut, :], preferred_element_type=jnp.float32)
    inv_norm = lax.rsqrt(jnp.sum(projected * projected, axis=1, keepdims=True) + epsilon)
    normed = projected * inv_norm
    normed_ref[...] = normed
    inv_ref[...] = jnp.broadcast_to(inv_norm, inv_ref.shape)
    msg_ref[pl.ds(0, rows), :] = normed.astype(jnp.bfloat16)


def project(feats, tower_w, partners, buckets):
    rows, din = feats.shape
    width = tower_w.shape[1]
    chunks = 4
    return pl.pallas_call(
        functools.partial(project_kernel, chunks),
        out_shape=(
            jax.ShapeDtypeStruct((rows + META, width), jnp.bfloat16),
            jax.ShapeDtypeStruct((rows, width), jnp.float32),
            jax.ShapeDtypeStruct((rows, 128), jnp.float32),
        ),
        in_specs=[ANY, ANY, VMEM, VMEM],
        out_specs=(VMEM, VMEM, VMEM),
        scratch_shapes=[
            pltpu.VMEM((rows, din), jnp.bfloat16),
            pltpu.VMEM((din, width), jnp.bfloat16),
            pltpu.SemaphoreType.DMA((2, chunks)),
        ],
        compiler_params=pltpu.CompilerParams(vmem_limit_bytes=VMEM_LIMIT),
        cost_estimate=pl.CostEstimate(
            flops=2 * rows * din * width, bytes_accessed=2 * din * (rows + width), transcendentals=rows
        ),
        name="project",
    )(feats, tower_w, partners, buckets)


def cut_kernel(feats_hbm, msg_hbm, *refs):
    outs, sems = refs[:-1], refs[-1]
    width = outs[0].shape[1]
    me = lax.axis_index("dp")
    copies = []
    for k, out in enumerate(outs):
        first = pl.multiple_of((me ^ k) * width, width)
        copies.append(pltpu.make_async_copy(feats_hbm.at[:, pl.ds(first, width)], out, sems.at[k]))
    for copy in copies:
        copy.start()
    for copy in copies:
        copy.wait()


def cut_feats(feats, msg, parts):
    rows, din = feats.shape
    return pl.pallas_call(
        cut_kernel,
        out_shape=tuple(jax.ShapeDtypeStruct((rows, din // parts), feats.dtype) for _ in range(parts)),
        in_specs=[ANY, ANY],
        out_specs=tuple(ANY for _ in range(parts)),
        scratch_shapes=[pltpu.SemaphoreType.DMA((parts,))],
        cost_estimate=pl.CostEstimate(flops=0, bytes_accessed=4 * rows * din, transcendentals=0),
        name="cut_feats",
    )(feats, msg)


def grad_kernel(members, counts_ref, *refs):
    msgs = refs[:members]
    normed_ref, inv_ref, out_ref, emb, weight, recip, partner, kept = refs[members:]
    rows, width = normed_ref.shape
    group = lax.axis_index("dp")
    me = lax.axis_index("pool")
    lanes = lax.broadcasted_iota(jnp.int32, (1, rows), 1)
    for k in range(members):
        emb[k] = msgs[k][pl.ds(0, rows), :]
        meta = msgs[k][pl.ds(rows, META), :].astype(jnp.float32)
        valid = lanes < counts_ref[group, me ^ k]
        weight[k] = jnp.where(valid, jnp.exp2(meta[0:1] * -LOG2E), 0.0)
        partner[k] = jnp.where(valid, meta[1:2] * DIGIT + meta[2:3], -1.0)

    def exps(left, k):
        return jnp.exp2(f32_dot(left, emb[k], ((1,), (1,))) * EXP2_SCALE)

    def folded(terms):
        total = terms[:, 0:128]
        for at in range(128, rows, 128):
            total = total + terms[:, at:at + 128]
        return total

    off_diagonal = lax.broadcasted_iota(jnp.int32, (rows, rows), 0) != lax.broadcasted_iota(
        jnp.int32, (rows, rows), 1
    )

    def store_recip(block, sums):
        totals = jnp.sum(jnp.transpose(sums), axis=0, keepdims=True)
        recip[block] = jnp.where(weight[block] > 0.0, 1.0 / totals, 0.0)

    own_emb = emb[0]
    own_sums = jnp.zeros((rows, 128), jnp.float32)
    for k in range(members):
        powers = exps(own_emb, k)
        if k == 0:
            powers = jnp.where(off_diagonal, powers, 0.0)
        kept[k] = powers
        own_sums = own_sums + folded(powers * weight[k])
    store_recip(0, own_sums)

    def other_totals(block, carry):
        left = emb[block]
        sums = folded(jnp.where(off_diagonal, exps(left, block), 0.0) * weight[block])
        for k in range(1, members):
            sums = sums + folded(exps(left, block ^ k) * weight[block ^ k])
        store_recip(block, sums)
        return carry

    lax.fori_loop(1, members, other_totals, 0)

    own_recip = column_of(recip[0])[:, 0:1]
    own_weight = column_of(weight[0])[:, 0:1]
    own_partner = column_of(partner[0])[:, 0:1].astype(jnp.int32)
    own_rows = me * rows + lax.broadcasted_iota(jnp.int32, (rows, 1), 0)
    grad = jnp.zeros((rows, width), jnp.float32)
    for k in range(members):
        columns = (me ^ k) * rows + lanes
        powers = kept[k]
        along = powers * weight[k] * own_recip - jnp.where(own_partner == columns, 1.0, 0.0)
        across = powers * own_weight * recip[k] - jnp.where(
            partner[k].astype(jnp.int32) == own_rows, 1.0, 0.0
        )
        grad = grad + f32_dot(along.astype(jnp.bfloat16), emb[k], ((1,), (0,)))
        grad = grad + f32_dot(across.astype(jnp.bfloat16), emb[k], ((1,), (0,)))
    normed = normed_ref[...]
    inward = jnp.sum(normed * grad, axis=1, keepdims=True)
    out_ref[...] = ((grad - normed * inward) * inv_ref[:, 0:1]).astype(jnp.bfloat16)


def group_grad(counts, msgs, normed, inv):
    members = len(msgs)
    rows, width = normed.shape
    pairs = members * members * rows * rows
    return pl.pallas_call(
        functools.partial(grad_kernel, members),
        out_shape=jax.ShapeDtypeStruct((rows, width), jnp.bfloat16),
        in_specs=[SMEM] + [VMEM] * (members + 2),
        out_specs=VMEM,
        scratch_shapes=[
            pltpu.VMEM((members, rows, width), jnp.bfloat16),
            pltpu.VMEM((members, 1, rows), jnp.float32),
            pltpu.VMEM((members, 1, rows), jnp.float32),
            pltpu.VMEM((members, 1, rows), jnp.float32),
            pltpu.VMEM((members, rows, rows), jnp.float32),
        ],
        compiler_params=pltpu.CompilerParams(vmem_limit_bytes=VMEM_LIMIT),
        cost_estimate=pl.CostEstimate(
            flops=2 * pairs * width, bytes_accessed=2 * members * rows * width, transcendentals=pairs
        ),
        name="group_grad",
    )(counts, *msgs, normed, inv)


def weight_kernel(parts, members, *refs):
    feats, grads = refs[:parts], refs[parts:2 * parts]
    own_ref, outs, total = refs[2 * parts], refs[2 * parts + 1:-1], refs[-1]
    piece = own_ref.shape[0]
    me = lax.axis_index("pool")
    result = f32_dot(feats[0][...], grads[0][...], ((0,), (0,)))
    for k in range(1, parts):
        result = result + f32_dot(feats[k][...], grads[k][...], ((0,), (0,)))
    total[...] = result
    for k, out in enumerate((own_ref,) + outs):
        first = pl.multiple_of((me ^ k) * piece, piece)
        out[...] = total[pl.ds(first, piece), :].astype(out.dtype)


def weight_grad(feats, grads, members):
    parts = len(feats)
    rows, cols = feats[0].shape
    width = grads[0].shape[1]
    piece = (cols // members, width)
    return pl.pallas_call(
        functools.partial(weight_kernel, parts, members),
        out_shape=(jax.ShapeDtypeStruct(piece, jnp.float32),)
        + tuple(jax.ShapeDtypeStruct(piece, jnp.float32) for _ in range(1, members)),
        in_specs=[VMEM] * (2 * parts),
        out_specs=tuple(VMEM for _ in range(members)),
        scratch_shapes=[pltpu.VMEM((cols, width), jnp.float32)],
        compiler_params=pltpu.CompilerParams(vmem_limit_bytes=VMEM_LIMIT),
        cost_estimate=pl.CostEstimate(
            flops=2 * parts * rows * cols * width, bytes_accessed=2 * parts * rows * cols, transcendentals=0
        ),
        name="weight_grad",
    )(*feats, *grads)


def swap(value, axis, flip):
    size = lax.axis_size(axis)
    return lax.ppermute(value, axis, [(at, at ^ flip) for at in range(size)])


def per_device(feats, tower_w, partners, popularity_buckets, row_counts):
    members = lax.axis_size("pool")
    parts = lax.axis_size("dp")
    minor = 1 << ((members.bit_length() - 1) // 2)
    msg, normed, inv = project(feats, tower_w, partners[None, :], popularity_buckets[None, :])
    msgs = [msg] + [None] * (members - 1)
    for far in range(minor, members, minor):
        msgs[far] = swap(msg, "pool", far)
    for near in range(1, minor):
        for far in range(0, members, minor):
            msgs[far + near] = swap(msgs[far], "pool", near)
    cuts = cut_feats(feats, msg, parts)
    cuts = [cuts[0]] + [swap(cuts[k], "dp", k) for k in range(1, parts)]
    grad_proj = group_grad(row_counts, msgs, normed, inv)
    grads = [grad_proj] + [swap(grad_proj, "dp", k) for k in range(1, parts)]
    pieces = weight_grad(cuts, grads, members)
    total = pieces[0]
    for k in range(1, members):
        total = total + swap(pieces[k], "pool", k)
    return total


def solution(mesh):
    return jax.shard_map(
        per_device,
        mesh=mesh,
        in_specs=(P(("dp", "pool"), None), P(), P(("dp", "pool")), P(("dp", "pool")), P()),
        out_specs=P(("dp", "pool"), None),
        check_vma=False,
    )
```

```python
import functools
import math

import jax
import jax.numpy as jnp
from jax import lax
from jax.experimental import pallas as pl
from jax.experimental.pallas import tpu as pltpu
from jax.sharding import PartitionSpec as P

sharpness_scaler = 0.05
epsilon = 1e-06
META = 16
DIGIT_BITS = 8
DIGIT = 1 << DIGIT_BITS
EXP2_SCALE = math.log2(math.e) / sharpness_scaler
LOG2E = math.log2(math.e)
VMEM_LIMIT = 48 * 1024 * 1024

VMEM = pl.BlockSpec(memory_space=pltpu.VMEM)
SMEM = pl.BlockSpec(memory_space=pltpu.SMEM)
HBM = pl.BlockSpec(memory_space=pltpu.HBM)


def f32_dot(left, right, dims):
    return lax.dot_general(left, right, (dims, ((), ())), preferred_element_type=jnp.float32)


def column_of(row):
    return jnp.transpose(jnp.broadcast_to(row, (128, row.shape[1])))


def project_kernel(parts, feats_hbm, w_hbm, partners_ref, buckets_ref, msg_ref, normed_ref, inv_ref, *rest):
    cuts, w_v, sems = rest[:parts], rest[parts], rest[parts + 1]
    width = w_v.shape[1]
    rows, step = cuts[0].shape
    me = lax.axis_index("dp")
    copies = []
    for k in range(parts):
        first = pl.multiple_of((me ^ k) * step, step)
        cut = pl.ds(first, step)
        pair = (
            pltpu.make_async_copy(feats_hbm.at[:, cut], cuts[k], sems.at[0, k]),
            pltpu.make_async_copy(w_hbm.at[cut, :], w_v.at[pl.ds(k * step, step), :], sems.at[1, k]),
        )
        pair[0].start()
        pair[1].start()
        copies.append(pair)
    partners = partners_ref[...]
    logq = -(buckets_ref[...].astype(jnp.float32) + 0.5) / 4.0
    high = (partners >> DIGIT_BITS).astype(jnp.float32)
    low = (partners & (DIGIT - 1)).astype(jnp.float32)
    kinds = lax.broadcasted_iota(jnp.int32, (META, rows), 0)
    meta = jnp.where(kinds == 0, logq, jnp.where(kinds == 1, high, jnp.where(kinds == 2, low, 0.0)))
    msg_ref[pl.ds(rows, META), :] = meta.astype(jnp.bfloat16)
    projected = jnp.zeros((rows, width), jnp.float32)
    for k in range(parts):
        copies[k][0].wait()
        copies[k][1].wait()
        projected = projected + f32_dot(cuts[k][...], w_v[pl.ds(k * step, step), :], ((1,), (0,)))
    inv_norm = lax.rsqrt(jnp.sum(projected * projected, axis=1, keepdims=True) + epsilon)
    normed = projected * inv_norm
    normed_ref[...] = normed
    inv_ref[...] = jnp.broadcast_to(inv_norm, inv_ref.shape)
    msg_ref[pl.ds(0, rows), :] = normed.astype(jnp.bfloat16)


def project(feats, tower_w, partners, buckets, parts):
    rows, din = feats.shape
    width = tower_w.shape[1]
    return pl.pallas_call(
        functools.partial(project_kernel, parts),
        out_shape=(
            jax.ShapeDtypeStruct((rows + META, width), jnp.bfloat16),
            jax.ShapeDtypeStruct((rows, width), jnp.float32),
            jax.ShapeDtypeStruct((rows, 128), jnp.float32),
        )
        + tuple(jax.ShapeDtypeStruct((rows, din // parts), feats.dtype) for _ in range(parts)),
        in_specs=[HBM, HBM, VMEM, VMEM],
        out_specs=(VMEM,) * (3 + parts),
        scratch_shapes=[
            pltpu.VMEM((din, width), jnp.bfloat16),
            pltpu.SemaphoreType.DMA((2, parts)),
        ],
        compiler_params=pltpu.CompilerParams(vmem_limit_bytes=VMEM_LIMIT),
        cost_estimate=pl.CostEstimate(
            flops=2 * rows * din * width, bytes_accessed=2 * din * (rows + width), transcendentals=rows
        ),
        name="project",
    )(feats, tower_w, partners, buckets)


def grad_kernel(members, counts_ref, *refs):
    msgs = refs[:members]
    normed_ref, inv_ref, out_ref, emb, weight, recip, partner, kept = refs[members:]
    rows, width = normed_ref.shape
    group = lax.axis_index("dp")
    me = lax.axis_index("pool")
    lanes = lax.broadcasted_iota(jnp.int32, (1, rows), 1)
    for k in range(members):
        emb[k] = msgs[k][pl.ds(0, rows), :]
        meta = msgs[k][pl.ds(rows, META), :].astype(jnp.float32)
        valid = lanes < counts_ref[group, me ^ k]
        weight[k] = jnp.where(valid, jnp.exp2(meta[0:1] * -LOG2E), 0.0)
        partner[k] = jnp.where(valid, meta[1:2] * DIGIT + meta[2:3], -1.0)

    def exps(left, k):
        return jnp.exp2(f32_dot(left, emb[k], ((1,), (1,))) * EXP2_SCALE)

    def folded(terms):
        total = terms[:, 0:128]
        for at in range(128, rows, 128):
            total = total + terms[:, at:at + 128]
        return total

    off_diagonal = lax.broadcasted_iota(jnp.int32, (rows, rows), 0) != lax.broadcasted_iota(
        jnp.int32, (rows, rows), 1
    )

    def store_recip(block, sums):
        totals = jnp.sum(jnp.transpose(sums), axis=0, keepdims=True)
        recip[block] = jnp.where(weight[block] > 0.0, 1.0 / totals, 0.0)

    own_emb = emb[0]
    own_sums = jnp.zeros((rows, 128), jnp.float32)
    for k in range(members):
        powers = exps(own_emb, k)
        if k == 0:
            powers = jnp.where(off_diagonal, powers, 0.0)
        kept[k] = powers
        own_sums = own_sums + folded(powers * weight[k])
    store_recip(0, own_sums)

    def other_totals(block, carry):
        left = emb[block]
        sums = folded(jnp.where(off_diagonal, exps(left, block), 0.0) * weight[block])
        for k in range(1, members):
            sums = sums + folded(exps(left, block ^ k) * weight[block ^ k])
        store_recip(block, sums)
        return carry

    lax.fori_loop(1, members, other_totals, 0)

    own_recip = column_of(recip[0])[:, 0:1]
    own_weight = column_of(weight[0])[:, 0:1]
    own_partner = column_of(partner[0])[:, 0:1].astype(jnp.int32)
    own_rows = me * rows + lax.broadcasted_iota(jnp.int32, (rows, 1), 0)
    grad = jnp.zeros((rows, width), jnp.float32)
    for k in range(members):
        columns = (me ^ k) * rows + lanes
        powers = kept[k]
        along = powers * weight[k] * own_recip - jnp.where(own_partner == columns, 1.0, 0.0)
        across = powers * own_weight * recip[k] - jnp.where(
            partner[k].astype(jnp.int32) == own_rows, 1.0, 0.0
        )
        grad = grad + f32_dot(along.astype(jnp.bfloat16), emb[k], ((1,), (0,)))
        grad = grad + f32_dot(across.astype(jnp.bfloat16), emb[k], ((1,), (0,)))
    normed = normed_ref[...]
    inward = jnp.sum(normed * grad, axis=1, keepdims=True)
    out_ref[...] = ((grad - normed * inward) * inv_ref[:, 0:1]).astype(jnp.bfloat16)


def group_grad(counts, msgs, normed, inv):
    members = len(msgs)
    rows, width = normed.shape
    pairs = members * members * rows * rows
    return pl.pallas_call(
        functools.partial(grad_kernel, members),
        out_shape=jax.ShapeDtypeStruct((rows, width), jnp.bfloat16),
        in_specs=[SMEM] + [VMEM] * (members + 2),
        out_specs=VMEM,
        scratch_shapes=[
            pltpu.VMEM((members, rows, width), jnp.bfloat16),
            pltpu.VMEM((members, 1, rows), jnp.float32),
            pltpu.VMEM((members, 1, rows), jnp.float32),
            pltpu.VMEM((members, 1, rows), jnp.float32),
            pltpu.VMEM((members, rows, rows), jnp.float32),
        ],
        compiler_params=pltpu.CompilerParams(vmem_limit_bytes=VMEM_LIMIT),
        cost_estimate=pl.CostEstimate(
            flops=2 * pairs * width, bytes_accessed=2 * members * rows * width, transcendentals=pairs
        ),
        name="group_grad",
    )(counts, *msgs, normed, inv)


def weight_kernel(parts, *refs):
    feats, grads, out_ref = refs[:parts], refs[parts:2 * parts], refs[2 * parts]
    result = f32_dot(feats[0][...], grads[0][...], ((0,), (0,)))
    for k in range(1, parts):
        result = result + f32_dot(feats[k][...], grads[k][...], ((0,), (0,)))
    out_ref[...] = result.astype(out_ref.dtype)


def weight_grad(feats, grads):
    parts = len(feats)
    rows, cols = feats[0].shape
    width = grads[0].shape[1]
    return pl.pallas_call(
        functools.partial(weight_kernel, parts),
        out_shape=jax.ShapeDtypeStruct((cols, width), jnp.bfloat16),
        in_specs=[VMEM] * (2 * parts),
        out_specs=VMEM,
        compiler_params=pltpu.CompilerParams(vmem_limit_bytes=VMEM_LIMIT),
        cost_estimate=pl.CostEstimate(
            flops=2 * parts * rows * cols * width, bytes_accessed=2 * parts * rows * cols, transcendentals=0
        ),
        name="weight_grad",
    )(*feats, *grads)


def swap(value, axis, flip):
    size = lax.axis_size(axis)
    return lax.ppermute(value, axis, [(at, at ^ flip) for at in range(size)])


def per_device(feats, tower_w, partners, popularity_buckets, row_counts):
    members = lax.axis_size("pool")
    parts = lax.axis_size("dp")
    minor = 1 << ((members.bit_length() - 1) // 2)
    msg, normed, inv, *cuts = project(feats, tower_w, partners[None, :], popularity_buckets[None, :], parts)
    msgs = [msg] + [None] * (members - 1)
    for far in range(minor, members, minor):
        msgs[far] = swap(msg, "pool", far)
    for near in range(1, minor):
        for far in range(0, members, minor):
            msgs[far + near] = swap(msgs[far], "pool", near)
    cuts = [cuts[0]] + [swap(cuts[k], "dp", k) for k in range(1, parts)]
    grad_proj = group_grad(row_counts, msgs, normed, inv)
    grads = [grad_proj] + [swap(grad_proj, "dp", k) for k in range(1, parts)]
    partial = weight_grad(cuts, grads)
    pieces = partial.reshape(members, partial.shape[0] // members, partial.shape[1])
    pieces = lax.all_to_all(pieces, "pool", split_axis=0, concat_axis=0)
    return jnp.sum(pieces.astype(jnp.float32), axis=0)


def solution(mesh):
    return jax.shard_map(
        per_device,
        mesh=mesh,
        in_specs=(P(("dp", "pool"), None), P(), P(("dp", "pool")), P(("dp", "pool")), P()),
        out_specs=P(("dp", "pool"), None),
        check_vma=False,
    )
```

```python
import functools
import math

import jax
import jax.numpy as jnp
from jax import lax
from jax.experimental import pallas as pl
from jax.experimental.pallas import tpu as pltpu
from jax.sharding import PartitionSpec as P

sharpness_scaler = 0.05
epsilon = 1e-06
META = 16
DIGIT_BITS = 8
DIGIT = 1 << DIGIT_BITS
EXP2_SCALE = math.log2(math.e) / sharpness_scaler
LOG2E = math.log2(math.e)
VMEM_LIMIT = 48 * 1024 * 1024

VMEM = pl.BlockSpec(memory_space=pltpu.VMEM)
SMEM = pl.BlockSpec(memory_space=pltpu.SMEM)
HBM = pl.BlockSpec(memory_space=pltpu.HBM)


def f32_dot(left, right, dims):
    return lax.dot_general(left, right, (dims, ((), ())), preferred_element_type=jnp.float32)


def column_of(row):
    return jnp.transpose(jnp.broadcast_to(row, (128, row.shape[1])))


def project_kernel(parts, feats_hbm, w_hbm, partners_hbm, buckets_hbm, msg_ref, normed_ref, inv_ref, *rest):
    cuts = rest[:parts]
    w_v, partners_ref, buckets_ref, sems, small_sems = rest[parts:]
    width = w_v.shape[1]
    rows, step = cuts[0].shape
    me = lax.axis_index("dp")
    copies = []
    for k in range(parts):
        first = pl.multiple_of((me ^ k) * step, step)
        cut = pl.ds(first, step)
        pair = (
            pltpu.make_async_copy(feats_hbm.at[:, cut], cuts[k], sems.at[0, k]),
            pltpu.make_async_copy(w_hbm.at[cut, :], w_v.at[pl.ds(k * step, step), :], sems.at[1, k]),
        )
        pair[0].start()
        pair[1].start()
        copies.append(pair)
    small = (
        pltpu.make_async_copy(partners_hbm, partners_ref, small_sems.at[0]),
        pltpu.make_async_copy(buckets_hbm, buckets_ref, small_sems.at[1]),
    )
    for copy in small:
        copy.start()
    for copy in small:
        copy.wait()
    partners = partners_ref[...]
    logq = -(buckets_ref[...].astype(jnp.float32) + 0.5) / 4.0
    high = (partners >> DIGIT_BITS).astype(jnp.float32)
    low = (partners & (DIGIT - 1)).astype(jnp.float32)
    kinds = lax.broadcasted_iota(jnp.int32, (META, rows), 0)
    meta = jnp.where(kinds == 0, logq, jnp.where(kinds == 1, high, jnp.where(kinds == 2, low, 0.0)))
    msg_ref[pl.ds(rows, META), :] = meta.astype(jnp.bfloat16)
    projected = jnp.zeros((rows, width), jnp.float32)
    for k in range(parts):
        copies[k][0].wait()
        copies[k][1].wait()
        projected = projected + f32_dot(cuts[k][...], w_v[pl.ds(k * step, step), :], ((1,), (0,)))
    inv_norm = lax.rsqrt(jnp.sum(projected * projected, axis=1, keepdims=True) + epsilon)
    normed = projected * inv_norm
    normed_ref[...] = normed
    inv_ref[...] = jnp.broadcast_to(inv_norm, inv_ref.shape)
    msg_ref[pl.ds(0, rows), :] = normed.astype(jnp.bfloat16)


def project(feats, tower_w, partners, buckets, parts):
    rows, din = feats.shape
    width = tower_w.shape[1]
    return pl.pallas_call(
        functools.partial(project_kernel, parts),
        out_shape=(
            jax.ShapeDtypeStruct((rows + META, width), jnp.bfloat16),
            jax.ShapeDtypeStruct((rows, width), jnp.float32),
            jax.ShapeDtypeStruct((rows, 128), jnp.float32),
        )
        + tuple(jax.ShapeDtypeStruct((rows, din // parts), feats.dtype) for _ in range(parts)),
        in_specs=[HBM, HBM, HBM, HBM],
        out_specs=(VMEM,) * (3 + parts),
        scratch_shapes=[
            pltpu.VMEM((din, width), jnp.bfloat16),
            pltpu.VMEM((1, rows), jnp.int32),
            pltpu.VMEM((1, rows), jnp.int32),
            pltpu.SemaphoreType.DMA((2, parts)),
            pltpu.SemaphoreType.DMA((2,)),
        ],
        compiler_params=pltpu.CompilerParams(vmem_limit_bytes=VMEM_LIMIT),
        cost_estimate=pl.CostEstimate(
            flops=2 * rows * din * width, bytes_accessed=2 * din * (rows + width), transcendentals=rows
        ),
        name="project",
    )(*(pltpu.with_memory_space_constraint(each, pltpu.HBM) for each in (feats, tower_w, partners, buckets)))


def folded(terms):
    total = terms[:, 0:128]
    for at in range(128, terms.shape[1], 128):
        total = total + terms[:, at:at + 128]
    return total


def rows_to_lanes(sums):
    return jnp.sum(jnp.transpose(sums), axis=0, keepdims=True)


def weight_of(msg_ref, counts_ref, flip):
    rows = msg_ref.shape[0] - META
    meta = msg_ref[pl.ds(rows, META), :].astype(jnp.float32)
    lanes = lax.broadcasted_iota(jnp.int32, (1, rows), 1)
    valid = lanes < counts_ref[lax.axis_index("dp"), lax.axis_index("pool") ^ flip]
    return jnp.where(valid, jnp.exp2(meta[0:1] * -LOG2E), 0.0)


def pair_sums(seen, fresh, counts_ref, msgs, sums_ref, own_ref, sums_out, kept_at):
    rows = own_ref.shape[0] if own_ref is not None else msgs[0].shape[0] - META
    emb = {k: msgs[k][pl.ds(0, rows), :] for k in seen + fresh}
    weight = {k: weight_of(msgs[k], counts_ref, k) for k in seen + fresh}
    sums = {k: sums_ref[k] for k in seen if k}
    own_sums = own_ref[...] if own_ref is not None else jnp.zeros((rows, 128), jnp.float32)
    off_diagonal = lax.broadcasted_iota(jnp.int32, (rows, rows), 0) != lax.broadcasted_iota(
        jnp.int32, (rows, rows), 1
    )

    def powers_of(left, right):
        return jnp.exp2(f32_dot(emb[left], emb[right], ((1,), (1,))) * EXP2_SCALE)

    def down(powers, column):
        return jnp.sum(powers * column, axis=0, keepdims=True)

    own_column = column_of(weight[0])[:, 0:1]
    for k in fresh:
        powers = powers_of(0, k)
        if k == 0:
            powers = jnp.where(off_diagonal, powers, 0.0)
        else:
            sums[k] = down(powers, own_column)
        kept_at(k)[...] = powers
        own_sums = own_sums + folded(powers * weight[k])
    others = [k for k in seen if k]
    for k in fresh:
        if k == 0:
            continue
        column = column_of(weight[k])[:, 0:1]
        mine = folded(jnp.where(off_diagonal, powers_of(k, k), 0.0) * weight[k])
        for other in others:
            powers = powers_of(k, other)
            mine = mine + folded(powers * weight[other])
            sums[other] = sums[other] + down(powers, column)
        sums[k] = sums[k] + rows_to_lanes(mine)
        others.append(k)
    return sums, own_sums, weight, own_column


def pairs_kernel(seen, fresh, *refs):
    known = seen + fresh
    counts_ref, refs = refs[0], refs[1:]
    msgs, refs = dict(zip(known, refs)), refs[len(known):]
    before = {}
    own_ref = None
    if seen:
        sums_ref, own_ref, refs = refs[0], refs[1], refs[2:]
        before = {k: sums_ref[at:at + 1, :] for at, k in enumerate(seen)}
    sums_out, own_out, kept_out = refs
    sums, own_sums, _, _ = pair_sums(
        seen, fresh, counts_ref, msgs, before, own_ref, sums_out, lambda k: kept_out.at[fresh.index(k)]
    )
    own_out[...] = own_sums
    for at, k in enumerate(known):
        sums_out[at:at + 1, :] = sums[k] if k else jnp.zeros_like(sums_out[0:1, :])


def pairs_cost(seen, fresh, rows, width):
    pairs = len(fresh) * len(seen) + len(fresh) * (len(fresh) + 1) // 2
    return pl.CostEstimate(
        flops=2 * pairs * rows * rows * width,
        bytes_accessed=2 * (len(seen) + len(fresh)) * rows * width + 4 * len(fresh) * rows * rows,
        transcendentals=pairs * rows * rows,
    )


def add_pairs(seen, fresh, counts, msgs, state):
    known = seen + fresh
    rows, width = msgs[0].shape[0] - META, msgs[0].shape[1]
    return pl.pallas_call(
        functools.partial(pairs_kernel, seen, fresh),
        out_shape=(
            jax.ShapeDtypeStruct((len(known), rows), jnp.float32),
            jax.ShapeDtypeStruct((rows, 128), jnp.float32),
            jax.ShapeDtypeStruct((len(fresh), rows, rows), jnp.float32),
        ),
        in_specs=[SMEM] + [VMEM] * (len(known) + len(state)),
        out_specs=(VMEM,) * 3,
        compiler_params=pltpu.CompilerParams(vmem_limit_bytes=VMEM_LIMIT),
        cost_estimate=pairs_cost(seen, fresh, rows, width),
        name="add_pairs",
    )(counts, *(msgs[k] for k in known), *state)


def grad_kernel(stages, fresh, *refs):
    seen = [k for stage in stages for k in stage]
    known = seen + fresh
    counts_ref, refs = refs[0], refs[1:]
    msgs, refs = dict(zip(known, refs)), refs[len(known):]
    sums_ref, own_ref, refs = refs[0], refs[1], refs[2:]
    stage_refs, refs = refs[:len(stages)], refs[len(stages):]
    normed_ref, inv_ref, out_ref, kept = refs
    rows, width = normed_ref.shape
    before = {k: sums_ref[at:at + 1, :] for at, k in enumerate(seen)}
    sums, own_sums, weight, own_weight = pair_sums(
        seen, fresh, counts_ref, msgs, before, own_ref, None, lambda k: kept.at[fresh.index(k)]
    )
    sums[0] = rows_to_lanes(own_sums)
    places = {k: kept.at[at] for at, k in enumerate(fresh)}
    for stage, ref in zip(stages, stage_refs):
        for at, k in enumerate(stage):
            places[k] = ref.at[at]

    me = lax.axis_index("pool")
    lanes = lax.broadcasted_iota(jnp.int32, (1, rows), 1)
    own_rows = me * rows + lax.broadcasted_iota(jnp.int32, (rows, 1), 0)

    def partner_of(k):
        meta = msgs[k][pl.ds(rows, META), :].astype(jnp.float32)
        return jnp.where(weight[k] > 0.0, meta[1:2] * DIGIT + meta[2:3], -1.0)

    recip = {k: jnp.where(weight[k] > 0.0, 1.0 / sums[k], 0.0) for k in known}
    own_recip = column_of(recip[0])[:, 0:1]
    own_partner = column_of(partner_of(0))[:, 0:1].astype(jnp.int32)
    both = jnp.zeros((2 * rows, width), jnp.float32)
    for k in known:
        columns = (me ^ k) * rows + lanes
        powers = places[k][...]
        along = powers * weight[k] * own_recip - jnp.where(own_partner == columns, 1.0, 0.0)
        across = powers * own_weight * recip[k] - jnp.where(
            partner_of(k).astype(jnp.int32) == own_rows, 1.0, 0.0
        )
        coefficients = jnp.concatenate([along.astype(jnp.bfloat16), across.astype(jnp.bfloat16)], axis=0)
        both = both + f32_dot(coefficients, msgs[k][pl.ds(0, rows), :], ((1,), (0,)))
    grad = both[:rows] + both[rows:]
    normed = normed_ref[...]
    inward = jnp.sum(normed * grad, axis=1, keepdims=True)
    out_ref[...] = ((grad - normed * inward) * inv_ref[:, 0:1]).astype(jnp.bfloat16)


def group_grad(stages, fresh, counts, msgs, state, kept, normed, inv):
    seen = [k for stage in stages for k in stage]
    known = seen + fresh
    rows, width = normed.shape
    return pl.pallas_call(
        functools.partial(grad_kernel, stages, fresh),
        out_shape=jax.ShapeDtypeStruct((rows, width), jnp.bfloat16),
        in_specs=[SMEM] + [VMEM] * (len(known) + len(state) + len(kept) + 2),
        out_specs=VMEM,
        scratch_shapes=[pltpu.VMEM((len(fresh), rows, rows), jnp.float32)],
        compiler_params=pltpu.CompilerParams(vmem_limit_bytes=VMEM_LIMIT),
        cost_estimate=pairs_cost(seen, fresh, rows, width),
        name="group_grad",
    )(counts, *(msgs[k] for k in known), *state, *kept, normed, inv)


def weight_kernel(parts, *refs):
    feats, grads, out_ref = refs[:parts], refs[parts:2 * parts], refs[2 * parts]
    result = f32_dot(feats[0][...], grads[0][...], ((0,), (0,)))
    for k in range(1, parts):
        result = result + f32_dot(feats[k][...], grads[k][...], ((0,), (0,)))
    out_ref[...] = result.astype(out_ref.dtype)


def weight_grad(feats, grads):
    parts = len(feats)
    rows, cols = feats[0].shape
    width = grads[0].shape[1]
    return pl.pallas_call(
        functools.partial(weight_kernel, parts),
        out_shape=jax.ShapeDtypeStruct((cols, width), jnp.bfloat16),
        in_specs=[VMEM] * (2 * parts),
        out_specs=VMEM,
        compiler_params=pltpu.CompilerParams(vmem_limit_bytes=VMEM_LIMIT),
        cost_estimate=pl.CostEstimate(
            flops=2 * parts * rows * cols * width, bytes_accessed=2 * parts * rows * cols, transcendentals=0
        ),
        name="weight_grad",
    )(*feats, *grads)


def swap(value, axis, flip):
    size = lax.axis_size(axis)
    return lax.ppermute(value, axis, [(at, at ^ flip) for at in range(size)])


def per_device(feats, tower_w, partners, popularity_buckets, row_counts):
    members = lax.axis_size("pool")
    parts = lax.axis_size("dp")
    minor = 1 << ((members.bit_length() - 1) // 2)
    msg, normed, inv, *cuts = project(feats, tower_w, partners[None, :], popularity_buckets[None, :], parts)

    msgs = {0: msg}
    bit = members // 2
    while bit >= minor:
        for k in list(msgs):
            msgs[k ^ bit] = swap(msgs[k], "pool", bit)
        bit //= 2
    majors = sorted(msgs)
    for near in range(1, minor):
        for far in majors:
            msgs[far + near] = swap(msgs[far], "pool", near)
    cuts = [cuts[0]] + [swap(cuts[k], "dp", k) for k in range(1, parts)]

    columns = [[far + near for near in range(minor)] for far in majors]
    stages = [sum(columns[:-2], []), columns[-2]]
    seen, state, kept = [], (), []
    for fresh in stages:
        *state, powers = add_pairs(seen, fresh, row_counts, msgs, state)
        kept.append(powers)
        seen = seen + fresh
    grad_proj = group_grad(stages, columns[-1], row_counts, msgs, state, kept, normed, inv)

    grads = {0: grad_proj}
    bit = parts // 2
    while bit:
        for k in list(grads):
            grads[k ^ bit] = swap(grads[k], "dp", bit)
        bit //= 2
    partial = weight_grad(cuts, [grads[k] for k in range(parts)])
    pieces = partial.reshape(members, partial.shape[0] // members, partial.shape[1])
    pieces = lax.all_to_all(pieces, "pool", split_axis=0, concat_axis=0)
    return jnp.sum(pieces.astype(jnp.float32), axis=0)


def solution(mesh):
    return jax.shard_map(
        per_device,
        mesh=mesh,
        in_specs=(P(("dp", "pool"), None), P(), P(("dp", "pool")), P(("dp", "pool")), P()),
        out_specs=P(("dp", "pool"), None),
        check_vma=False,
    )
```

```python
import functools
import math

import jax
import jax.numpy as jnp
from jax import lax
from jax.experimental import pallas as pl
from jax.experimental.pallas import tpu as pltpu
from jax.sharding import PartitionSpec as P

sharpness_scaler = 0.05
epsilon = 1e-06
META = 16
DIGIT_BITS = 8
DIGIT = 1 << DIGIT_BITS
EXP2_SCALE = math.log2(math.e) / sharpness_scaler
LOG2E = math.log2(math.e)
VMEM_LIMIT = 48 * 1024 * 1024

VMEM = pl.BlockSpec(memory_space=pltpu.VMEM)
SMEM = pl.BlockSpec(memory_space=pltpu.SMEM)
ANY = pl.BlockSpec(memory_space=pl.ANY)
HBM = pl.BlockSpec(memory_space=pltpu.HBM)


def f32_dot(left, right, dims):
    return lax.dot_general(left, right, (dims, ((), ())), preferred_element_type=jnp.float32)


def column_of(row):
    return jnp.transpose(jnp.broadcast_to(row, (128, row.shape[1])))


def project_kernel(parts, feats_hbm, w_hbm, partners_hbm, buckets_hbm, msg_ref, normed_ref, inv_ref, *rest):
    cuts = rest[:parts]
    w_v, partners_ref, buckets_ref, sems, small_sems = rest[parts:]
    width = w_v.shape[1]
    rows, step = cuts[0].shape
    me = lax.axis_index("dp")
    copies = []
    for k in range(parts):
        first = pl.multiple_of((me ^ k) * step, step)
        cut = pl.ds(first, step)
        pair = (
            pltpu.make_async_copy(feats_hbm.at[:, cut], cuts[k], sems.at[0, k]),
            pltpu.make_async_copy(w_hbm.at[cut, :], w_v.at[pl.ds(k * step, step), :], sems.at[1, k]),
        )
        pair[0].start()
        pair[1].start()
        copies.append(pair)
    small = (
        pltpu.make_async_copy(partners_hbm, partners_ref, small_sems.at[0]),
        pltpu.make_async_copy(buckets_hbm, buckets_ref, small_sems.at[1]),
    )
    for copy in small:
        copy.start()
    for copy in small:
        copy.wait()
    partners = partners_ref[...]
    logq = -(buckets_ref[...].astype(jnp.float32) + 0.5) / 4.0
    high = (partners >> DIGIT_BITS).astype(jnp.float32)
    low = (partners & (DIGIT - 1)).astype(jnp.float32)
    kinds = lax.broadcasted_iota(jnp.int32, (META, rows), 0)
    meta = jnp.where(kinds == 0, logq, jnp.where(kinds == 1, high, jnp.where(kinds == 2, low, 0.0)))
    msg_ref[pl.ds(rows, META), :] = meta.astype(jnp.bfloat16)
    projected = jnp.zeros((rows, width), jnp.float32)
    for k in range(parts):
        copies[k][0].wait()
        copies[k][1].wait()
        projected = projected + f32_dot(cuts[k][...], w_v[pl.ds(k * step, step), :], ((1,), (0,)))
    inv_norm = lax.rsqrt(jnp.sum(projected * projected, axis=1, keepdims=True) + epsilon)
    normed = projected * inv_norm
    normed_ref[...] = normed
    inv_ref[...] = jnp.broadcast_to(inv_norm, inv_ref.shape)
    msg_ref[pl.ds(0, rows), :] = normed.astype(jnp.bfloat16)


def project(feats, tower_w, partners, buckets, parts):
    rows, din = feats.shape
    width = tower_w.shape[1]
    return pl.pallas_call(
        functools.partial(project_kernel, parts),
        out_shape=(
            jax.ShapeDtypeStruct((rows + META, width), jnp.bfloat16),
            jax.ShapeDtypeStruct((rows, width), jnp.float32),
            jax.ShapeDtypeStruct((rows, 128), jnp.float32),
        )
        + tuple(jax.ShapeDtypeStruct((rows, din // parts), feats.dtype) for _ in range(parts)),
        in_specs=[HBM, HBM, HBM, HBM],
        out_specs=(VMEM,) * (3 + parts),
        scratch_shapes=[
            pltpu.VMEM((din, width), jnp.bfloat16),
            pltpu.VMEM((1, rows), jnp.int32),
            pltpu.VMEM((1, rows), jnp.int32),
            pltpu.SemaphoreType.DMA((2, parts)),
            pltpu.SemaphoreType.DMA((2,)),
        ],
        compiler_params=pltpu.CompilerParams(vmem_limit_bytes=VMEM_LIMIT),
        cost_estimate=pl.CostEstimate(
            flops=2 * rows * din * width, bytes_accessed=2 * din * (rows + width), transcendentals=rows
        ),
        name="project",
    )(*(pltpu.with_memory_space_constraint(each, pltpu.HBM) for each in (feats, tower_w, partners, buckets)))


def folded(terms):
    total = terms[:, 0:128]
    for at in range(128, terms.shape[1], 128):
        total = total + terms[:, at:at + 128]
    return total


def rows_to_lanes(sums):
    return jnp.sum(jnp.transpose(sums), axis=0, keepdims=True)


def weight_of(msg_ref, counts_ref, flip):
    rows = msg_ref.shape[0] - META
    meta = msg_ref[pl.ds(rows, META), :].astype(jnp.float32)
    lanes = lax.broadcasted_iota(jnp.int32, (1, rows), 1)
    valid = lanes < counts_ref[lax.axis_index("dp"), lax.axis_index("pool") ^ flip]
    return jnp.where(valid, jnp.exp2(meta[0:1] * -LOG2E), 0.0)


def pair_sums(seen, fresh, counts_ref, msgs, sums_ref, own_ref, sums_out, kept_at):
    rows = own_ref.shape[0] if own_ref is not None else msgs[0].shape[0] - META
    emb = {k: msgs[k][pl.ds(0, rows), :] for k in seen + fresh}
    weight = {k: weight_of(msgs[k], counts_ref, k) for k in seen + fresh}
    sums = {k: sums_ref[k] for k in seen if k}
    own_sums = own_ref[...] if own_ref is not None else jnp.zeros((rows, 128), jnp.float32)
    off_diagonal = lax.broadcasted_iota(jnp.int32, (rows, rows), 0) != lax.broadcasted_iota(
        jnp.int32, (rows, rows), 1
    )

    def powers_of(left, right):
        return jnp.exp2(f32_dot(emb[left], emb[right], ((1,), (1,))) * EXP2_SCALE)

    def down(powers, column):
        return jnp.sum(powers * column, axis=0, keepdims=True)

    own_column = column_of(weight[0])[:, 0:1]
    for k in fresh:
        powers = powers_of(0, k)
        if k == 0:
            powers = jnp.where(off_diagonal, powers, 0.0)
        else:
            sums[k] = down(powers, own_column)
        kept_at(k)[...] = powers
        own_sums = own_sums + folded(powers * weight[k])
    others = [k for k in seen if k]
    for k in fresh:
        if k == 0:
            continue
        column = column_of(weight[k])[:, 0:1]
        mine = folded(jnp.where(off_diagonal, powers_of(k, k), 0.0) * weight[k])
        for other in others:
            powers = powers_of(k, other)
            mine = mine + folded(powers * weight[other])
            sums[other] = sums[other] + down(powers, column)
        sums[k] = sums[k] + rows_to_lanes(mine)
        others.append(k)
    return sums, own_sums, weight, own_column


def pairs_kernel(seen, fresh, *refs):
    known = seen + fresh
    counts_ref, refs = refs[0], refs[1:]
    msgs, refs = dict(zip(known, refs)), refs[len(known):]
    before = {}
    own_ref = None
    if seen:
        sums_ref, own_ref, refs = refs[0], refs[1], refs[2:]
        before = {k: sums_ref[at:at + 1, :] for at, k in enumerate(seen)}
    sums_out, own_out, kept_out = refs
    sums, own_sums, _, _ = pair_sums(
        seen, fresh, counts_ref, msgs, before, own_ref, sums_out, lambda k: kept_out.at[fresh.index(k)]
    )
    own_out[...] = own_sums
    for at, k in enumerate(known):
        sums_out[at:at + 1, :] = sums[k] if k else jnp.zeros_like(sums_out[0:1, :])


def pairs_cost(seen, fresh, rows, width):
    pairs = len(fresh) * len(seen) + len(fresh) * (len(fresh) + 1) // 2
    return pl.CostEstimate(
        flops=2 * pairs * rows * rows * width,
        bytes_accessed=2 * (len(seen) + len(fresh)) * rows * width + 4 * len(fresh) * rows * rows,
        transcendentals=pairs * rows * rows,
    )


def add_pairs(seen, fresh, counts, msgs, state):
    known = seen + fresh
    rows, width = msgs[0].shape[0] - META, msgs[0].shape[1]
    return pl.pallas_call(
        functools.partial(pairs_kernel, seen, fresh),
        out_shape=(
            jax.ShapeDtypeStruct((len(known), rows), jnp.float32),
            jax.ShapeDtypeStruct((rows, 128), jnp.float32),
            jax.ShapeDtypeStruct((len(fresh), rows, rows), jnp.float32),
        ),
        in_specs=[SMEM] + [VMEM] * (len(known) + len(state)),
        out_specs=(VMEM,) * 3,
        compiler_params=pltpu.CompilerParams(vmem_limit_bytes=VMEM_LIMIT),
        cost_estimate=pairs_cost(seen, fresh, rows, width),
        name="add_pairs",
    )(counts, *(msgs[k] for k in known), *state)


def grad_kernel(stages, fresh, *refs):
    seen = [k for stage in stages for k in stage]
    known = seen + fresh
    counts_ref, refs = refs[0], refs[1:]
    msgs, refs = dict(zip(known, refs)), refs[len(known):]
    sums_ref, own_ref, refs = refs[0], refs[1], refs[2:]
    stage_refs, refs = refs[:len(stages)], refs[len(stages):]
    normed_ref, inv_ref, out_ref, kept = refs
    rows, width = normed_ref.shape
    before = {k: sums_ref[at:at + 1, :] for at, k in enumerate(seen)}
    sums, own_sums, weight, own_weight = pair_sums(
        seen, fresh, counts_ref, msgs, before, own_ref, None, lambda k: kept.at[fresh.index(k)]
    )
    sums[0] = rows_to_lanes(own_sums)
    places = {k: kept.at[at] for at, k in enumerate(fresh)}
    for stage, ref in zip(stages, stage_refs):
        for at, k in enumerate(stage):
            places[k] = ref.at[at]

    me = lax.axis_index("pool")
    lanes = lax.broadcasted_iota(jnp.int32, (1, rows), 1)
    own_rows = me * rows + lax.broadcasted_iota(jnp.int32, (rows, 1), 0)

    def partner_of(k):
        meta = msgs[k][pl.ds(rows, META), :].astype(jnp.float32)
        return jnp.where(weight[k] > 0.0, meta[1:2] * DIGIT + meta[2:3], -1.0)

    recip = {k: jnp.where(weight[k] > 0.0, 1.0 / sums[k], 0.0) for k in known}
    own_recip = column_of(recip[0])[:, 0:1]
    own_partner = column_of(partner_of(0))[:, 0:1].astype(jnp.int32)
    both = jnp.zeros((2 * rows, width), jnp.float32)
    for k in known:
        columns = (me ^ k) * rows + lanes
        powers = places[k][...]
        along = powers * weight[k] * own_recip - jnp.where(own_partner == columns, 1.0, 0.0)
        across = powers * own_weight * recip[k] - jnp.where(
            partner_of(k).astype(jnp.int32) == own_rows, 1.0, 0.0
        )
        coefficients = jnp.concatenate([along.astype(jnp.bfloat16), across.astype(jnp.bfloat16)], axis=0)
        both = both + f32_dot(coefficients, msgs[k][pl.ds(0, rows), :], ((1,), (0,)))
    grad = both[:rows] + both[rows:]
    normed = normed_ref[...]
    inward = jnp.sum(normed * grad, axis=1, keepdims=True)
    out_ref[...] = ((grad - normed * inward) * inv_ref[:, 0:1]).astype(jnp.bfloat16)


def group_grad(stages, fresh, counts, msgs, state, kept, normed, inv):
    seen = [k for stage in stages for k in stage]
    known = seen + fresh
    rows, width = normed.shape
    return pl.pallas_call(
        functools.partial(grad_kernel, stages, fresh),
        out_shape=jax.ShapeDtypeStruct((rows, width), jnp.bfloat16),
        in_specs=[SMEM] + [VMEM] * (len(known) + len(state) + len(kept) + 2),
        out_specs=VMEM,
        scratch_shapes=[pltpu.VMEM((len(fresh), rows, rows), jnp.float32)],
        compiler_params=pltpu.CompilerParams(vmem_limit_bytes=VMEM_LIMIT),
        cost_estimate=pairs_cost(seen, fresh, rows, width),
        name="group_grad",
    )(counts, *(msgs[k] for k in known), *state, *kept, normed, inv)


def weight_kernel(parts, *refs):
    feats, grads, out_ref = refs[:parts], refs[parts:2 * parts], refs[2 * parts]
    result = f32_dot(feats[0][...], grads[0][...], ((0,), (0,)))
    for k in range(1, parts):
        result = result + f32_dot(feats[k][...], grads[k][...], ((0,), (0,)))
    out_ref[...] = result.astype(out_ref.dtype)


def weight_grad(feats, grads):
    parts = len(feats)
    rows, cols = feats[0].shape
    width = grads[0].shape[1]
    return pl.pallas_call(
        functools.partial(weight_kernel, parts),
        out_shape=jax.ShapeDtypeStruct((cols, width), jnp.bfloat16),
        in_specs=[VMEM] * (2 * parts),
        out_specs=VMEM,
        compiler_params=pltpu.CompilerParams(vmem_limit_bytes=VMEM_LIMIT),
        cost_estimate=pl.CostEstimate(
            flops=2 * parts * rows * cols * width, bytes_accessed=2 * parts * rows * cols, transcendentals=0
        ),
        name="weight_grad",
    )(*feats, *grads)


def swap(value, axis, flip):
    size = lax.axis_size(axis)
    return lax.ppermute(value, axis, [(at, at ^ flip) for at in range(size)])


def order_kernel(*refs):
    pass


def after(value, *earlier):
    return pl.pallas_call(
        order_kernel,
        out_shape=jax.ShapeDtypeStruct(value.shape, value.dtype),
        in_specs=[ANY] * (1 + len(earlier)),
        out_specs=ANY,
        input_output_aliases={0: 0},
        name="after",
    )(value, *earlier)


def per_device(feats, tower_w, partners, popularity_buckets, row_counts):
    members = lax.axis_size("pool")
    parts = lax.axis_size("dp")
    minor = 1 << ((members.bit_length() - 1) // 2)
    msg, normed, inv, *cuts = project(feats, tower_w, partners[None, :], popularity_buckets[None, :], parts)

    msgs = {0: msg}
    for near in range(1, minor):
        msgs[near] = swap(msg, "pool", near)
    bits = []
    bit = minor
    while bit < members:
        bits.append(bit)
        msgs[bit] = swap(msg, "pool", bit)
        bit *= 2
    first = bits[0]
    for near in range(1, minor):
        msgs[first + near] = swap(msgs[first], "pool", near)
    msgs[bits[-1]] = after(msgs[bits[-1]], *(msgs[base + near] for base in (0, first) for near in range(1, minor)))
    for at, bit in enumerate(bits):
        for k in range(bit + minor, 2 * bit, minor):
            msgs[k] = swap(msgs[bit], "pool", k ^ bit) if k ^ bit in bits else swap(msgs[k ^ bit], "pool", bit)
    majors = sorted(k for k in msgs if k % minor == 0)
    for far in majors[2:]:
        for near in range(1, minor):
            msgs[far + near] = swap(msgs[far], "pool", near)
    cuts = [cuts[0]] + [swap(cuts[k], "dp", k) for k in range(1, parts)]

    columns = [[far + near for near in range(minor)] for far in majors]
    stages = [sum(columns[:-2], []), columns[-2]]
    seen, state, kept = [], (), []
    for fresh in stages:
        *state, powers = add_pairs(seen, fresh, row_counts, msgs, state)
        kept.append(powers)
        seen = seen + fresh
    grad_proj = group_grad(stages, columns[-1], row_counts, msgs, state, kept, normed, inv)

    grads = {0: grad_proj}
    bit = parts // 2
    while bit:
        for k in list(grads):
            grads[k ^ bit] = swap(grads[k], "dp", bit)
        bit //= 2
    partial = weight_grad(cuts, [grads[k] for k in range(parts)])
    pieces = partial.reshape(members, partial.shape[0] // members, partial.shape[1])
    pieces = lax.all_to_all(pieces, "pool", split_axis=0, concat_axis=0)
    return jnp.sum(pieces.astype(jnp.float32), axis=0)


def solution(mesh):
    return jax.shard_map(
        per_device,
        mesh=mesh,
        in_specs=(P(("dp", "pool"), None), P(), P(("dp", "pool")), P(("dp", "pool")), P()),
        out_specs=P(("dp", "pool"), None),
        check_vma=False,
    )
```

```python
import functools
import math

import jax
import jax.numpy as jnp
from jax import lax
from jax.experimental import pallas as pl
from jax.experimental.pallas import tpu as pltpu
from jax.sharding import PartitionSpec as P

sharpness_scaler = 0.05
epsilon = 1e-06
META = 16
DIGIT_BITS = 8
DIGIT = 1 << DIGIT_BITS
EXP2_SCALE = math.log2(math.e) / sharpness_scaler
LOG2E = math.log2(math.e)
VMEM_LIMIT = 48 * 1024 * 1024

VMEM = pl.BlockSpec(memory_space=pltpu.VMEM)
SMEM = pl.BlockSpec(memory_space=pltpu.SMEM)
HBM = pl.BlockSpec(memory_space=pltpu.HBM)


def f32_dot(left, right, dims):
    return lax.dot_general(left, right, (dims, ((), ())), preferred_element_type=jnp.float32)


def column_of(row):
    return jnp.transpose(jnp.broadcast_to(row, (128, row.shape[1])))


def project_kernel(parts, feats_hbm, w_hbm, partners_hbm, buckets_hbm, msg_ref, normed_ref, inv_ref,
                   near_ref, far_ref, w_v, partners_ref, buckets_ref, sems, small_sems):
    half, rows, step = near_ref.shape
    cuts = [near_ref.at[k] for k in range(half)] + [far_ref.at[k] for k in range(half)]
    width = w_v.shape[1]
    me = lax.axis_index("dp")
    copies = []
    for k in range(parts):
        first = pl.multiple_of((me ^ k) * step, step)
        cut = pl.ds(first, step)
        pair = (
            pltpu.make_async_copy(feats_hbm.at[:, cut], cuts[k], sems.at[0, k]),
            pltpu.make_async_copy(w_hbm.at[cut, :], w_v.at[pl.ds(k * step, step), :], sems.at[1, k]),
        )
        pair[0].start()
        pair[1].start()
        copies.append(pair)
    small = (
        pltpu.make_async_copy(partners_hbm, partners_ref, small_sems.at[0]),
        pltpu.make_async_copy(buckets_hbm, buckets_ref, small_sems.at[1]),
    )
    for copy in small:
        copy.start()
    for copy in small:
        copy.wait()
    partners = partners_ref[...]
    logq = -(buckets_ref[...].astype(jnp.float32) + 0.5) / 4.0
    high = (partners >> DIGIT_BITS).astype(jnp.float32)
    low = (partners & (DIGIT - 1)).astype(jnp.float32)
    kinds = lax.broadcasted_iota(jnp.int32, (META, rows), 0)
    meta = jnp.where(kinds == 0, logq, jnp.where(kinds == 1, high, jnp.where(kinds == 2, low, 0.0)))
    msg_ref[pl.ds(rows, META), :] = meta.astype(jnp.bfloat16)
    projected = jnp.zeros((rows, width), jnp.float32)
    for k in range(parts):
        copies[k][0].wait()
        copies[k][1].wait()
        projected = projected + f32_dot(cuts[k][...], w_v[pl.ds(k * step, step), :], ((1,), (0,)))
    inv_norm = lax.rsqrt(jnp.sum(projected * projected, axis=1, keepdims=True) + epsilon)
    normed = projected * inv_norm
    normed_ref[...] = normed
    inv_ref[...] = jnp.broadcast_to(inv_norm, inv_ref.shape)
    msg_ref[pl.ds(0, rows), :] = normed.astype(jnp.bfloat16)


def project(feats, tower_w, partners, buckets, parts):
    rows, din = feats.shape
    width = tower_w.shape[1]
    return pl.pallas_call(
        functools.partial(project_kernel, parts),
        out_shape=(
            jax.ShapeDtypeStruct((rows + META, width), jnp.bfloat16),
            jax.ShapeDtypeStruct((rows, width), jnp.float32),
            jax.ShapeDtypeStruct((rows, 128), jnp.float32),
        )
        + (jax.ShapeDtypeStruct((parts // 2, rows, din // parts), feats.dtype),) * 2,
        in_specs=[HBM, HBM, HBM, HBM],
        out_specs=(VMEM,) * 5,
        scratch_shapes=[
            pltpu.VMEM((din, width), jnp.bfloat16),
            pltpu.VMEM((1, rows), jnp.int32),
            pltpu.VMEM((1, rows), jnp.int32),
            pltpu.SemaphoreType.DMA((2, parts)),
            pltpu.SemaphoreType.DMA((2,)),
        ],
        compiler_params=pltpu.CompilerParams(vmem_limit_bytes=VMEM_LIMIT),
        cost_estimate=pl.CostEstimate(
            flops=2 * rows * din * width, bytes_accessed=2 * din * (rows + width), transcendentals=rows
        ),
        name="project",
    )(*(pltpu.with_memory_space_constraint(each, pltpu.HBM) for each in (feats, tower_w, partners, buckets)))


def folded(terms):
    total = terms[:, 0:128]
    for at in range(128, terms.shape[1], 128):
        total = total + terms[:, at:at + 128]
    return total


def rows_to_lanes(sums):
    return jnp.sum(jnp.transpose(sums), axis=0, keepdims=True)


def weight_of(msg_ref, counts_ref, flip):
    rows = msg_ref.shape[0] - META
    meta = msg_ref[pl.ds(rows, META), :].astype(jnp.float32)
    lanes = lax.broadcasted_iota(jnp.int32, (1, rows), 1)
    valid = lanes < counts_ref[lax.axis_index("dp"), lax.axis_index("pool") ^ flip]
    return jnp.where(valid, jnp.exp2(meta[0:1] * -LOG2E), 0.0)


def pair_sums(seen, fresh, counts_ref, msgs, sums_ref, own_ref, sums_out, kept_at):
    rows = own_ref.shape[0] if own_ref is not None else msgs[0].shape[0] - META
    emb = {k: msgs[k][pl.ds(0, rows), :] for k in seen + fresh}
    weight = {k: weight_of(msgs[k], counts_ref, k) for k in seen + fresh}
    sums = {k: sums_ref[k] for k in seen if k}
    own_sums = own_ref[...] if own_ref is not None else jnp.zeros((rows, 128), jnp.float32)
    off_diagonal = lax.broadcasted_iota(jnp.int32, (rows, rows), 0) != lax.broadcasted_iota(
        jnp.int32, (rows, rows), 1
    )

    def powers_of(left, right):
        return jnp.exp2(f32_dot(emb[left], emb[right], ((1,), (1,))) * EXP2_SCALE)

    def down(powers, column):
        return jnp.sum(powers * column, axis=0, keepdims=True)

    own_column = column_of(weight[0])[:, 0:1]
    for k in fresh:
        powers = powers_of(0, k)
        if k == 0:
            powers = jnp.where(off_diagonal, powers, 0.0)
        else:
            sums[k] = down(powers, own_column)
        kept_at(k)[...] = powers
        own_sums = own_sums + folded(powers * weight[k])
    others = [k for k in seen if k]
    for k in fresh:
        if k == 0:
            continue
        column = column_of(weight[k])[:, 0:1]
        mine = folded(jnp.where(off_diagonal, powers_of(k, k), 0.0) * weight[k])
        for other in others:
            powers = powers_of(k, other)
            mine = mine + folded(powers * weight[other])
            sums[other] = sums[other] + down(powers, column)
        sums[k] = sums[k] + rows_to_lanes(mine)
        others.append(k)
    return sums, own_sums, weight, own_column


def pairs_kernel(seen, fresh, *refs):
    known = seen + fresh
    counts_ref, refs = refs[0], refs[1:]
    msgs, refs = dict(zip(known, refs)), refs[len(known):]
    before = {}
    own_ref = None
    if seen:
        sums_ref, own_ref, refs = refs[0], refs[1], refs[2:]
        before = {k: sums_ref[at:at + 1, :] for at, k in enumerate(seen)}
    sums_out, own_out, kept_out = refs
    sums, own_sums, _, _ = pair_sums(
        seen, fresh, counts_ref, msgs, before, own_ref, sums_out, lambda k: kept_out.at[fresh.index(k)]
    )
    own_out[...] = own_sums
    for at, k in enumerate(known):
        sums_out[at:at + 1, :] = sums[k] if k else jnp.zeros_like(sums_out[0:1, :])


def pairs_cost(seen, fresh, rows, width):
    pairs = len(fresh) * len(seen) + len(fresh) * (len(fresh) + 1) // 2
    return pl.CostEstimate(
        flops=2 * pairs * rows * rows * width,
        bytes_accessed=2 * (len(seen) + len(fresh)) * rows * width + 4 * len(fresh) * rows * rows,
        transcendentals=pairs * rows * rows,
    )


def add_pairs(seen, fresh, counts, msgs, state):
    known = seen + fresh
    rows, width = msgs[0].shape[0] - META, msgs[0].shape[1]
    return pl.pallas_call(
        functools.partial(pairs_kernel, seen, fresh),
        out_shape=(
            jax.ShapeDtypeStruct((len(known), rows), jnp.float32),
            jax.ShapeDtypeStruct((rows, 128), jnp.float32),
            jax.ShapeDtypeStruct((len(fresh), rows, rows), jnp.float32),
        ),
        in_specs=[SMEM] + [VMEM] * (len(known) + len(state)),
        out_specs=(VMEM,) * 3,
        compiler_params=pltpu.CompilerParams(vmem_limit_bytes=VMEM_LIMIT),
        cost_estimate=pairs_cost(seen, fresh, rows, width),
        name="add_pairs",
    )(counts, *(msgs[k] for k in known), *state)


def grad_kernel(stages, fresh, *refs):
    seen = [k for stage in stages for k in stage]
    known = seen + fresh
    counts_ref, refs = refs[0], refs[1:]
    msgs, refs = dict(zip(known, refs)), refs[len(known):]
    sums_ref, own_ref, refs = refs[0], refs[1], refs[2:]
    stage_refs, refs = refs[:len(stages)], refs[len(stages):]
    normed_ref, inv_ref, out_ref, kept = refs[-4:]
    rows, width = normed_ref.shape
    before = {k: sums_ref[at:at + 1, :] for at, k in enumerate(seen)}
    sums, own_sums, weight, own_weight = pair_sums(
        seen, fresh, counts_ref, msgs, before, own_ref, None, lambda k: kept.at[fresh.index(k)]
    )
    sums[0] = rows_to_lanes(own_sums)
    places = {k: kept.at[at] for at, k in enumerate(fresh)}
    for stage, ref in zip(stages, stage_refs):
        for at, k in enumerate(stage):
            places[k] = ref.at[at]

    me = lax.axis_index("pool")
    lanes = lax.broadcasted_iota(jnp.int32, (1, rows), 1)
    own_rows = me * rows + lax.broadcasted_iota(jnp.int32, (rows, 1), 0)

    def partner_of(k):
        meta = msgs[k][pl.ds(rows, META), :].astype(jnp.float32)
        return jnp.where(weight[k] > 0.0, meta[1:2] * DIGIT + meta[2:3], -1.0)

    recip = {k: jnp.where(weight[k] > 0.0, 1.0 / sums[k], 0.0) for k in known}
    own_recip = column_of(recip[0])[:, 0:1]
    own_partner = column_of(partner_of(0))[:, 0:1].astype(jnp.int32)
    both = jnp.zeros((2 * rows, width), jnp.float32)
    for k in known:
        columns = (me ^ k) * rows + lanes
        powers = places[k][...]
        along = powers * weight[k] * own_recip - jnp.where(own_partner == columns, 1.0, 0.0)
        across = powers * own_weight * recip[k] - jnp.where(
            partner_of(k).astype(jnp.int32) == own_rows, 1.0, 0.0
        )
        coefficients = jnp.concatenate([along.astype(jnp.bfloat16), across.astype(jnp.bfloat16)], axis=0)
        both = both + f32_dot(coefficients, msgs[k][pl.ds(0, rows), :], ((1,), (0,)))
    grad = both[:rows] + both[rows:]
    normed = normed_ref[...]
    inward = jnp.sum(normed * grad, axis=1, keepdims=True)
    out_ref[...] = ((grad - normed * inward) * inv_ref[:, 0:1]).astype(jnp.bfloat16)


def group_grad(stages, fresh, counts, msgs, state, kept, earlier, normed, inv):
    seen = [k for stage in stages for k in stage]
    known = seen + fresh
    rows, width = normed.shape
    return pl.pallas_call(
        functools.partial(grad_kernel, stages, fresh),
        out_shape=jax.ShapeDtypeStruct((rows, width), jnp.bfloat16),
        in_specs=[SMEM] + [VMEM] * (len(known) + len(state) + len(kept) + len(earlier) + 2),
        out_specs=VMEM,
        scratch_shapes=[pltpu.VMEM((len(fresh), rows, rows), jnp.float32)],
        compiler_params=pltpu.CompilerParams(vmem_limit_bytes=VMEM_LIMIT),
        cost_estimate=pairs_cost(seen, fresh, rows, width),
        name="group_grad",
    )(counts, *(msgs[k] for k in known), *state, *kept, *earlier, normed, inv)


def distinct(arrays):
    found = []
    for array in arrays:
        if all(array is not other for other in found):
            found.append(array)
    return found, [next(at for at, other in enumerate(found) if array is other) for array in arrays]


def pack_kernel(places, *refs):
    for at, (array, row) in enumerate(places):
        refs[-1][at] = refs[array][row]


def pack(pieces, earlier):
    arrays, which = distinct([array for array, _ in pieces])
    shape = (len(pieces),) + arrays[0].shape[1:]
    return pl.pallas_call(
        functools.partial(pack_kernel, [(at, piece[1]) for at, piece in zip(which, pieces)]),
        out_shape=jax.ShapeDtypeStruct(shape, arrays[0].dtype),
        in_specs=[VMEM] * len(arrays) + [VMEM],
        out_specs=VMEM,
        compiler_params=pltpu.CompilerParams(vmem_limit_bytes=VMEM_LIMIT),
        cost_estimate=pl.CostEstimate(flops=0, bytes_accessed=4 * math.prod(shape), transcendentals=0),
        name="pack",
    )(*arrays, earlier)


def weight_kernel(places, order, *refs):
    own_ref, outs, total = refs[-2 - len(order)], refs[-1 - len(order):-1], refs[-1]
    piece = own_ref.shape[0]
    me = lax.axis_index("pool")
    result = None
    for array, row, grad in places:
        term = f32_dot(refs[array][row], refs[grad][...], ((0,), (0,)))
        result = term if result is None else result + term
    total[...] = result
    for k, out in zip([0] + order, (own_ref,) + outs):
        first = pl.multiple_of((me ^ k) * piece, piece)
        out[...] = total[pl.ds(first, piece), :].astype(out.dtype)


def weight_grad(blocks, grads, order):
    arrays, which = distinct([array for _, array, _ in blocks])
    places = [(at, row, len(arrays) + source) for at, (source, _, row) in zip(which, blocks)]
    parts = len(grads)
    _, rows, cols = arrays[0].shape
    width = grads[0].shape[1]
    piece = (cols // (1 + len(order)), width)
    return pl.pallas_call(
        functools.partial(weight_kernel, places, order),
        out_shape=(jax.ShapeDtypeStruct(piece, jnp.float32),)
        + tuple(jax.ShapeDtypeStruct(piece, jnp.bfloat16) for _ in order),
        in_specs=[VMEM] * (len(arrays) + parts),
        out_specs=(VMEM,) * (1 + len(order)),
        scratch_shapes=[pltpu.VMEM((cols, width), jnp.float32)],
        compiler_params=pltpu.CompilerParams(vmem_limit_bytes=VMEM_LIMIT),
        cost_estimate=pl.CostEstimate(
            flops=2 * parts * rows * cols * width, bytes_accessed=2 * parts * rows * cols, transcendentals=0
        ),
        name="weight_grad",
    )(*arrays, *grads)


def swap(value, axis, flip):
    size = lax.axis_size(axis)
    return lax.ppermute(value, axis, [(at, at ^ flip) for at in range(size)])


def order_kernel(value_ref, *refs):
    refs[-1][...] = value_ref[...]


def after(value, *earlier):
    return pl.pallas_call(
        order_kernel,
        out_shape=jax.ShapeDtypeStruct(value.shape, value.dtype),
        in_specs=[VMEM] * (1 + len(earlier)),
        out_specs=VMEM,
        name="after",
    )(value, *earlier)


def per_device(feats, tower_w, partners, popularity_buckets, row_counts):
    members = lax.axis_size("pool")
    parts = lax.axis_size("dp")
    minor = 1 << ((members.bit_length() - 1) // 2)
    msg, normed, inv, near_cuts, far_cuts = project(feats, tower_w, partners[None, :], popularity_buckets[None, :], parts)

    came = swap(far_cuts, "dp", parts // 2)

    msgs = {0: msg}
    for near in range(1, minor):
        msgs[near] = swap(msg, "pool", near)
    bits = []
    bit = minor
    while bit < members:
        bits.append(bit)
        msgs[bit] = swap(msg, "pool", bit)
        bit *= 2
    first = bits[0]
    for near in range(1, minor):
        msgs[first + near] = swap(msgs[first], "pool", near)
    relayed = after(msgs[bits[-1]], *(msgs[base + near] for base in (0, first) for near in range(1, minor)))
    for at, bit in enumerate(bits):
        for k in range(bit + minor, 2 * bit, minor):
            msgs[k] = swap(relayed if bit == bits[-1] else msgs[bit], "pool", k ^ bit)
    majors = sorted(k for k in msgs if k % minor == 0)
    for far in majors[2:]:
        for near in range(1, minor):
            msgs[far + near] = swap(msgs[far], "pool", near)
    columns = [[far + near for near in range(minor)] for far in majors]
    stages = [sum(columns[:-2], []), majors[-2:], columns[-2][1:]]
    seen, state, kept = [], (), []
    for fresh in stages:
        *state, powers = add_pairs(seen, fresh, row_counts, msgs, state)
        kept.append(powers)
        seen = seen + fresh
    grad_proj = group_grad(stages, columns[-1][1:], row_counts, msgs, state, kept, [], normed, inv)

    grads = {0: grad_proj}
    bit = parts // 2
    while bit:
        for k in list(grads):
            grads[k ^ bit] = swap(grads[k], "dp", bit)
        bit //= 2
    blocks = {k: [(0, near_cuts, k), (parts // 2, came, k)] for k in range(parts // 2)}
    bit = parts // 4
    while bit:
        moving = [(k ^ bit, source ^ bit, array, at) for k in blocks if k & bit for source, array, at in blocks[k]]
        passed = swap(pack([each[2:] for each in moving], grads[parts // 2]), "dp", bit)
        blocks = {k: blocks[k] for k in blocks if not k & bit}
        for at, (k, source, _, _) in enumerate(moving):
            blocks[k].append((source, passed, at))
        bit //= 2

    order = sorted(range(1, members), key=lambda k: (k < members // 2, k))
    total, *pieces = weight_grad(blocks[0], [grads[k] for k in range(parts)], order)
    for k, piece in zip(order, pieces):
        total = total + swap(piece, "pool", k).astype(jnp.float32)
    return total


def solution(mesh):
    return jax.shard_map(
        per_device,
        mesh=mesh,
        in_specs=(P(("dp", "pool"), None), P(), P(("dp", "pool")), P(("dp", "pool")), P()),
        out_specs=P(("dp", "pool"), None),
        check_vma=False,
    )
```

```python
import functools
import math

import jax
import jax.numpy as jnp
from jax import lax
from jax.experimental import pallas as pl
from jax.experimental.pallas import tpu as pltpu
from jax.sharding import PartitionSpec as P

sharpness_scaler = 0.05
epsilon = 1e-06
META = 16
DIGIT_BITS = 8
DIGIT = 1 << DIGIT_BITS
EXP2_SCALE = math.log2(math.e) / sharpness_scaler
LOG2E = math.log2(math.e)
VMEM_LIMIT = 40 * 1024 * 1024
SMALL_VMEM_LIMIT = 8 * 1024 * 1024

VMEM = pl.BlockSpec(memory_space=pltpu.VMEM)
SMEM = pl.BlockSpec(memory_space=pltpu.SMEM)
HBM = pl.BlockSpec(memory_space=pltpu.HBM)


def f32_dot(left, right, dims):
    return lax.dot_general(left, right, (dims, ((), ())), preferred_element_type=jnp.float32)


def column_of(row):
    return jnp.transpose(jnp.broadcast_to(row, (128, row.shape[1])))


def project_kernel(parts, feats_hbm, w_hbm, partners_hbm, buckets_hbm, msg_ref, normed_ref, inv_ref,
                   near_ref, far_ref, w_v, partners_ref, buckets_ref, sems, small_sems):
    half, rows, step = near_ref.shape
    cuts = [near_ref.at[k] for k in range(half)] + [far_ref.at[k] for k in range(half)]
    width = w_v.shape[1]
    me = lax.axis_index("dp")
    copies = []
    for k in range(parts):
        first = pl.multiple_of((me ^ k) * step, step)
        cut = pl.ds(first, step)
        pair = (
            pltpu.make_async_copy(feats_hbm.at[:, cut], cuts[k], sems.at[0, k]),
            pltpu.make_async_copy(w_hbm.at[cut, :], w_v.at[pl.ds(k * step, step), :], sems.at[1, k]),
        )
        pair[0].start()
        pair[1].start()
        copies.append(pair)
    small = (
        pltpu.make_async_copy(partners_hbm, partners_ref, small_sems.at[0]),
        pltpu.make_async_copy(buckets_hbm, buckets_ref, small_sems.at[1]),
    )
    for copy in small:
        copy.start()
    for copy in small:
        copy.wait()
    partners = partners_ref[...]
    logq = -(buckets_ref[...].astype(jnp.float32) + 0.5) / 4.0
    high = (partners >> DIGIT_BITS).astype(jnp.float32)
    low = (partners & (DIGIT - 1)).astype(jnp.float32)
    kinds = lax.broadcasted_iota(jnp.int32, (META, rows), 0)
    meta = jnp.where(kinds == 0, logq, jnp.where(kinds == 1, high, jnp.where(kinds == 2, low, 0.0)))
    msg_ref[pl.ds(rows, META), :] = meta.astype(jnp.bfloat16)
    projected = jnp.zeros((rows, width), jnp.float32)
    for k in range(parts):
        copies[k][0].wait()
        copies[k][1].wait()
        projected = projected + f32_dot(cuts[k][...], w_v[pl.ds(k * step, step), :], ((1,), (0,)))
    inv_norm = lax.rsqrt(jnp.sum(projected * projected, axis=1, keepdims=True) + epsilon)
    normed = projected * inv_norm
    normed_ref[...] = normed
    inv_ref[...] = jnp.broadcast_to(inv_norm, inv_ref.shape)
    msg_ref[pl.ds(0, rows), :] = normed.astype(jnp.bfloat16)


def project(feats, tower_w, partners, buckets, parts):
    rows, din = feats.shape
    width = tower_w.shape[1]
    return pl.pallas_call(
        functools.partial(project_kernel, parts),
        out_shape=(
            jax.ShapeDtypeStruct((rows + META, width), jnp.bfloat16),
            jax.ShapeDtypeStruct((rows, width), jnp.float32),
            jax.ShapeDtypeStruct((rows, 128), jnp.float32),
        )
        + (jax.ShapeDtypeStruct((parts // 2, rows, din // parts), feats.dtype),) * 2,
        in_specs=[HBM, HBM, HBM, HBM],
        out_specs=(VMEM,) * 5,
        scratch_shapes=[
            pltpu.VMEM((din, width), jnp.bfloat16),
            pltpu.VMEM((1, rows), jnp.int32),
            pltpu.VMEM((1, rows), jnp.int32),
            pltpu.SemaphoreType.DMA((2, parts)),
            pltpu.SemaphoreType.DMA((2,)),
        ],
        compiler_params=pltpu.CompilerParams(vmem_limit_bytes=VMEM_LIMIT),
        cost_estimate=pl.CostEstimate(
            flops=2 * rows * din * width, bytes_accessed=2 * din * (rows + width), transcendentals=rows
        ),
        name="project",
    )(*(pltpu.with_memory_space_constraint(each, pltpu.HBM) for each in (feats, tower_w, partners, buckets)))


def folded(terms):
    total = terms[:, 0:128]
    for at in range(128, terms.shape[1], 128):
        total = total + terms[:, at:at + 128]
    return total


def rows_to_lanes(sums):
    return jnp.sum(jnp.transpose(sums), axis=0, keepdims=True)


def weight_of(msg_ref, counts_ref, flip):
    rows = msg_ref.shape[0] - META
    meta = msg_ref[pl.ds(rows, META), :].astype(jnp.float32)
    lanes = lax.broadcasted_iota(jnp.int32, (1, rows), 1)
    valid = lanes < counts_ref[lax.axis_index("dp"), lax.axis_index("pool") ^ flip]
    return jnp.where(valid, jnp.exp2(meta[0:1] * -LOG2E), 0.0)


def pair_sums(seen, fresh, counts_ref, msgs, sums_ref, own_ref, sums_out, kept_at):
    rows = own_ref.shape[0] if own_ref is not None else msgs[0].shape[0] - META
    emb = {k: msgs[k][pl.ds(0, rows), :] for k in seen + fresh}
    weight = {k: weight_of(msgs[k], counts_ref, k) for k in seen + fresh}
    sums = {k: sums_ref[k] for k in seen if k}
    own_sums = own_ref[...] if own_ref is not None else jnp.zeros((rows, 128), jnp.float32)
    off_diagonal = lax.broadcasted_iota(jnp.int32, (rows, rows), 0) != lax.broadcasted_iota(
        jnp.int32, (rows, rows), 1
    )

    def powers_of(left, right):
        return jnp.exp2(f32_dot(emb[left], emb[right], ((1,), (1,))) * EXP2_SCALE)

    def down(powers, column):
        return jnp.sum(powers * column, axis=0, keepdims=True)

    own_column = column_of(weight[0])[:, 0:1]
    for k in fresh:
        powers = powers_of(0, k)
        if k == 0:
            powers = jnp.where(off_diagonal, powers, 0.0)
        else:
            sums[k] = down(powers, own_column)
        kept_at(k)[...] = powers
        own_sums = own_sums + folded(powers * weight[k])
    others = [k for k in seen if k]
    for k in fresh:
        if k == 0:
            continue
        column = column_of(weight[k])[:, 0:1]
        mine = folded(jnp.where(off_diagonal, powers_of(k, k), 0.0) * weight[k])
        for other in others:
            powers = powers_of(k, other)
            mine = mine + folded(powers * weight[other])
            sums[other] = sums[other] + down(powers, column)
        sums[k] = sums[k] + rows_to_lanes(mine)
        others.append(k)
    return sums, own_sums, weight, own_column


def pairs_kernel(seen, fresh, *refs):
    known = seen + fresh
    counts_ref, refs = refs[0], refs[1:]
    msgs, refs = dict(zip(known, refs)), refs[len(known):]
    before = {}
    own_ref = None
    if seen:
        sums_ref, own_ref, refs = refs[0], refs[1], refs[2:]
        before = {k: sums_ref[at:at + 1, :] for at, k in enumerate(seen)}
    sums_out, own_out, kept_out = refs
    sums, own_sums, _, _ = pair_sums(
        seen, fresh, counts_ref, msgs, before, own_ref, sums_out, lambda k: kept_out.at[fresh.index(k)]
    )
    own_out[...] = own_sums
    for at, k in enumerate(known):
        sums_out[at:at + 1, :] = sums[k] if k else jnp.zeros_like(sums_out[0:1, :])


def pairs_cost(seen, fresh, rows, width):
    pairs = len(fresh) * len(seen) + len(fresh) * (len(fresh) + 1) // 2
    return pl.CostEstimate(
        flops=2 * pairs * rows * rows * width,
        bytes_accessed=2 * (len(seen) + len(fresh)) * rows * width + 4 * len(fresh) * rows * rows,
        transcendentals=pairs * rows * rows,
    )


def add_pairs(seen, fresh, counts, msgs, state):
    known = seen + fresh
    rows, width = msgs[0].shape[0] - META, msgs[0].shape[1]
    return pl.pallas_call(
        functools.partial(pairs_kernel, seen, fresh),
        out_shape=(
            jax.ShapeDtypeStruct((len(known), rows), jnp.float32),
            jax.ShapeDtypeStruct((rows, 128), jnp.float32),
            jax.ShapeDtypeStruct((len(fresh), rows, rows), jnp.float32),
        ),
        in_specs=[SMEM] + [VMEM] * (len(known) + len(state)),
        out_specs=(VMEM,) * 3,
        compiler_params=pltpu.CompilerParams(vmem_limit_bytes=VMEM_LIMIT),
        cost_estimate=pairs_cost(seen, fresh, rows, width),
        name="add_pairs",
    )(counts, *(msgs[k] for k in known), *state)


def grad_kernel(stages, fresh, *refs):
    seen = [k for stage in stages for k in stage]
    known = seen + fresh
    counts_ref, refs = refs[0], refs[1:]
    msgs, refs = dict(zip(known, refs)), refs[len(known):]
    sums_ref, own_ref, refs = refs[0], refs[1], refs[2:]
    stage_refs, refs = refs[:len(stages)], refs[len(stages):]
    normed_ref, inv_ref, out_ref, kept = refs[-4:]
    rows, width = normed_ref.shape
    before = {k: sums_ref[at:at + 1, :] for at, k in enumerate(seen)}
    sums, own_sums, weight, own_weight = pair_sums(
        seen, fresh, counts_ref, msgs, before, own_ref, None, lambda k: kept.at[fresh.index(k)]
    )
    sums[0] = rows_to_lanes(own_sums)
    places = {k: kept.at[at] for at, k in enumerate(fresh)}
    for stage, ref in zip(stages, stage_refs):
        for at, k in enumerate(stage):
            places[k] = ref.at[at]

    me = lax.axis_index("pool")
    lanes = lax.broadcasted_iota(jnp.int32, (1, rows), 1)
    own_rows = me * rows + lax.broadcasted_iota(jnp.int32, (rows, 1), 0)

    def partner_of(k):
        meta = msgs[k][pl.ds(rows, META), :].astype(jnp.float32)
        return jnp.where(weight[k] > 0.0, meta[1:2] * DIGIT + meta[2:3], -1.0)

    recip = {k: jnp.where(weight[k] > 0.0, 1.0 / sums[k], 0.0) for k in known}
    own_recip = column_of(recip[0])[:, 0:1]
    own_partner = column_of(partner_of(0))[:, 0:1].astype(jnp.int32)
    both = jnp.zeros((2 * rows, width), jnp.float32)
    for k in known:
        columns = (me ^ k) * rows + lanes
        powers = places[k][...]
        along = powers * weight[k] * own_recip - jnp.where(own_partner == columns, 1.0, 0.0)
        across = powers * own_weight * recip[k] - jnp.where(
            partner_of(k).astype(jnp.int32) == own_rows, 1.0, 0.0
        )
        coefficients = jnp.concatenate([along.astype(jnp.bfloat16), across.astype(jnp.bfloat16)], axis=0)
        both = both + f32_dot(coefficients, msgs[k][pl.ds(0, rows), :], ((1,), (0,)))
    grad = both[:rows] + both[rows:]
    normed = normed_ref[...]
    inward = jnp.sum(normed * grad, axis=1, keepdims=True)
    out_ref[0] = ((grad - normed * inward) * inv_ref[:, 0:1]).astype(jnp.bfloat16)


def group_grad(stages, fresh, counts, msgs, state, kept, earlier, normed, inv):
    seen = [k for stage in stages for k in stage]
    known = seen + fresh
    rows, width = normed.shape
    return pl.pallas_call(
        functools.partial(grad_kernel, stages, fresh),
        out_shape=jax.ShapeDtypeStruct((1, rows, width), jnp.bfloat16),
        in_specs=[SMEM] + [VMEM] * (len(known) + len(state) + len(kept) + len(earlier) + 2),
        out_specs=VMEM,
        scratch_shapes=[pltpu.VMEM((len(fresh), rows, rows), jnp.float32)],
        compiler_params=pltpu.CompilerParams(vmem_limit_bytes=VMEM_LIMIT),
        cost_estimate=pairs_cost(seen, fresh, rows, width),
        name="group_grad",
    )(counts, *(msgs[k] for k in known), *state, *kept, *earlier, normed, inv)


def distinct(arrays):
    found = []
    for array in arrays:
        if all(array is not other for other in found):
            found.append(array)
    return found, [next(at for at, other in enumerate(found) if array is other) for array in arrays]


def pack_kernel(places, *refs):
    for at, (array, row) in enumerate(places):
        refs[-1][at] = refs[array][row]


def pack(pieces, earlier=()):
    arrays, which = distinct([array for array, _ in pieces])
    shape = (len(pieces),) + arrays[0].shape[1:]
    return pl.pallas_call(
        functools.partial(pack_kernel, [(at, piece[1]) for at, piece in zip(which, pieces)]),
        out_shape=jax.ShapeDtypeStruct(shape, arrays[0].dtype),
        in_specs=[VMEM] * (len(arrays) + len(earlier)),
        out_specs=VMEM,
        compiler_params=pltpu.CompilerParams(vmem_limit_bytes=VMEM_LIMIT),
        cost_estimate=pl.CostEstimate(flops=0, bytes_accessed=4 * math.prod(shape), transcendentals=0),
        name="pack",
    )(*arrays, *earlier)


def weight_kernel(places, *refs):
    result = None
    for array, row, grad_array, grad_row in places:
        term = f32_dot(refs[array][row], refs[grad_array][grad_row], ((0,), (0,)))
        result = term if result is None else result + term
    refs[-1][...] = result.astype(jnp.bfloat16)


def weight_grad(blocks, grads):
    blocks, grads = sorted(blocks, key=lambda each: each[0]), sorted(grads, key=lambda each: each[0])
    arrays, which = distinct([array for _, array, _ in blocks + grads])
    parts = len(blocks)
    places = [
        (which[at], blocks[at][2], which[parts + at], grads[at][2]) for at in range(parts)
    ]
    _, rows, cols = blocks[0][1].shape
    width = grads[0][1].shape[2]
    return pl.pallas_call(
        functools.partial(weight_kernel, places),
        out_shape=jax.ShapeDtypeStruct((cols, width), jnp.bfloat16),
        in_specs=[VMEM] * len(arrays),
        out_specs=VMEM,
        compiler_params=pltpu.CompilerParams(vmem_limit_bytes=VMEM_LIMIT),
        cost_estimate=pl.CostEstimate(
            flops=2 * parts * rows * cols * width, bytes_accessed=2 * parts * rows * cols, transcendentals=0
        ),
        name="weight_grad",
    )(*arrays)


def swap(value, axis, flip):
    size = lax.axis_size(axis)
    return lax.ppermute(value, axis, [(at, at ^ flip) for at in range(size)])


def order_kernel(value_ref, *refs):
    refs[-1][...] = value_ref[...]


def after(value, *earlier):
    return pl.pallas_call(
        order_kernel,
        out_shape=jax.ShapeDtypeStruct(value.shape, value.dtype),
        in_specs=[VMEM] * (1 + len(earlier)),
        out_specs=VMEM,
        compiler_params=pltpu.CompilerParams(vmem_limit_bytes=SMALL_VMEM_LIMIT),
        name="after",
    )(value, *earlier)


def per_device(feats, tower_w, partners, popularity_buckets, row_counts):
    members = lax.axis_size("pool")
    parts = lax.axis_size("dp")
    minor = 1 << ((members.bit_length() - 1) // 2)
    msg, normed, inv, near_cuts, far_cuts = project(feats, tower_w, partners[None, :], popularity_buckets[None, :], parts)

    came = swap(far_cuts, "dp", parts // 2)

    msgs = {0: msg}
    for near in range(1, minor):
        msgs[near] = swap(msg, "pool", near)
    bits = []
    bit = minor
    while bit < members:
        bits.append(bit)
        msgs[bit] = swap(msg, "pool", bit)
        bit *= 2
    first = bits[0]
    for near in range(1, minor):
        msgs[first + near] = swap(msgs[first], "pool", near)
    majors = list(range(0, members, minor))
    early = [far + near for far in majors[:-2] for near in range(minor)]
    held = early[1 - minor:]
    early = early[:1 - minor]
    state, kept, stages = (), [], []

    def add(fresh):
        nonlocal state
        *state, powers = add_pairs(sum(stages, []), fresh, row_counts, msgs, state)
        kept.append(powers)
        stages.append(fresh)

    add(early)
    last = bits[-1]
    for k in range(first + minor, last, minor):
        msgs[k] = swap(msgs[first], "pool", k ^ first)
    relayed = after(msgs[last], state[1], *(msgs[k] for k in held))
    for k in range(last + minor, members, minor):
        msgs[k] = swap(relayed, "pool", k ^ last)
    for far in majors[2:-1]:
        for near in range(1, minor):
            msgs[far + near] = swap(msgs[far], "pool", near)
    add(held + majors[2:-1])
    relayed = after(msgs[majors[-1]], state[1])
    for near in range(1, minor):
        msgs[majors[-1] + near] = swap(relayed, "pool", near)
    add([majors[-1]])
    add([far + near for far in majors[2:-1] for near in range(1, minor)])
    grad_proj = group_grad(
        stages, [majors[-1] + near for near in range(1, minor)], row_counts, msgs, state, kept, [], normed, inv
    )

    bit = parts // 2
    grads = [(0, grad_proj, 0), (bit, swap(grad_proj, "dp", bit), 0)]
    blocks = {k: [(0, near_cuts, k), (bit, came, k)] for k in range(bit)}
    bit //= 2
    while bit:
        moving = [(k ^ bit, source ^ bit, array, at) for k in blocks if k & bit for source, array, at in blocks[k]]
        blocks = {k: blocks[k] for k in blocks if not k & bit}
        passed = swap(pack([each[2:] for each in moving], [grads[-1][1]]), "dp", bit)
        for at, (k, source, _, _) in enumerate(moving):
            blocks[k].append((source, passed, at))
        sent = swap(pack([each[1:] for each in grads]), "dp", bit)
        grads += [(each[0] ^ bit, sent, at) for at, each in enumerate(grads)]
        bit //= 2

    partial = weight_grad(blocks[0], grads)
    pieces = partial.reshape(members, partial.shape[0] // members, partial.shape[1])
    pieces = lax.all_to_all(pieces, "pool", split_axis=0, concat_axis=0)
    return jnp.sum(pieces.astype(jnp.float32), axis=0)


def solution(mesh):
    return jax.shard_map(
        per_device,
        mesh=mesh,
        in_specs=(P(("dp", "pool"), None), P(), P(("dp", "pool")), P(("dp", "pool")), P()),
        out_specs=P(("dp", "pool"), None),
        check_vma=False,
    )
```

```python
import functools
import math

import jax
import jax.numpy as jnp
from jax import lax
from jax.experimental import pallas as pl
from jax.experimental.pallas import tpu as pltpu
from jax.sharding import PartitionSpec as P

sharpness_scaler = 0.05
epsilon = 1e-06
META = 16
DIGIT_BITS = 8
DIGIT = 1 << DIGIT_BITS
EXP2_SCALE = math.log2(math.e) / sharpness_scaler
LOG2E = math.log2(math.e)
VMEM_LIMIT = 40 * 1024 * 1024
SMALL_VMEM_LIMIT = 8 * 1024 * 1024

VMEM = pl.BlockSpec(memory_space=pltpu.VMEM)
SMEM = pl.BlockSpec(memory_space=pltpu.SMEM)
HBM = pl.BlockSpec(memory_space=pltpu.HBM)


def f32_dot(left, right, dims):
    return lax.dot_general(left, right, (dims, ((), ())), preferred_element_type=jnp.float32)


def column_of(row):
    return jnp.transpose(jnp.broadcast_to(row, (128, row.shape[1])))


def project_kernel(parts, feats_hbm, w_hbm, partners_hbm, buckets_hbm, msg_ref, normed_ref, inv_ref,
                   near_ref, far_ref, w_v, partners_ref, buckets_ref, sems, small_sems):
    half, rows, step = near_ref.shape
    cuts = [near_ref.at[k] for k in range(half)] + [far_ref.at[k] for k in range(half)]
    width = w_v.shape[1]
    me = lax.axis_index("dp")
    small = (
        pltpu.make_async_copy(partners_hbm, partners_ref, small_sems.at[0]),
        pltpu.make_async_copy(buckets_hbm, buckets_ref, small_sems.at[1]),
    )
    for copy in small:
        copy.start()
    copies = []
    for k in range(parts):
        first = pl.multiple_of((me ^ k) * step, step)
        cut = pl.ds(first, step)
        pair = (
            pltpu.make_async_copy(feats_hbm.at[:, cut], cuts[k], sems.at[0, k]),
            pltpu.make_async_copy(w_hbm.at[cut, :], w_v.at[pl.ds(k * step, step), :], sems.at[1, k]),
        )
        pair[0].start()
        pair[1].start()
        copies.append(pair)
    projected = jnp.zeros((rows, width), jnp.float32)
    for k in range(parts):
        copies[k][0].wait()
        copies[k][1].wait()
        projected = projected + f32_dot(cuts[k][...], w_v[pl.ds(k * step, step), :], ((1,), (0,)))
    for copy in small:
        copy.wait()
    partners = partners_ref[...]
    logq = -(buckets_ref[...].astype(jnp.float32) + 0.5) / 4.0
    high = (partners >> DIGIT_BITS).astype(jnp.float32)
    low = (partners & (DIGIT - 1)).astype(jnp.float32)
    kinds = lax.broadcasted_iota(jnp.int32, (META, rows), 0)
    meta = jnp.where(kinds == 0, logq, jnp.where(kinds == 1, high, jnp.where(kinds == 2, low, 0.0)))
    msg_ref[pl.ds(rows, META), :] = meta.astype(jnp.bfloat16)
    inv_norm = lax.rsqrt(jnp.sum(projected * projected, axis=1, keepdims=True) + epsilon)
    normed = projected * inv_norm
    normed_ref[...] = normed
    inv_ref[...] = jnp.broadcast_to(inv_norm, inv_ref.shape)
    msg_ref[pl.ds(0, rows), :] = normed.astype(jnp.bfloat16)


def project(feats, tower_w, partners, buckets, parts):
    rows, din = feats.shape
    width = tower_w.shape[1]
    return pl.pallas_call(
        functools.partial(project_kernel, parts),
        out_shape=(
            jax.ShapeDtypeStruct((rows + META, width), jnp.bfloat16),
            jax.ShapeDtypeStruct((rows, width), jnp.float32),
            jax.ShapeDtypeStruct((rows, 128), jnp.float32),
        )
        + (jax.ShapeDtypeStruct((parts // 2, rows, din // parts), feats.dtype),) * 2,
        in_specs=[HBM, HBM, HBM, HBM],
        out_specs=(VMEM,) * 5,
        scratch_shapes=[
            pltpu.VMEM((din, width), jnp.bfloat16),
            pltpu.VMEM((1, rows), jnp.int32),
            pltpu.VMEM((1, rows), jnp.int32),
            pltpu.SemaphoreType.DMA((2, parts)),
            pltpu.SemaphoreType.DMA((2,)),
        ],
        compiler_params=pltpu.CompilerParams(vmem_limit_bytes=VMEM_LIMIT),
        cost_estimate=pl.CostEstimate(
            flops=2 * rows * din * width, bytes_accessed=2 * din * (rows + width), transcendentals=rows
        ),
        name="project",
    )(*(pltpu.with_memory_space_constraint(each, pltpu.HBM) for each in (feats, tower_w, partners, buckets)))


def folded(terms):
    total = terms[:, 0:128]
    for at in range(128, terms.shape[1], 128):
        total = total + terms[:, at:at + 128]
    return total


def rows_to_lanes(sums):
    return jnp.sum(jnp.transpose(sums), axis=0, keepdims=True)


def weight_of(msg_ref, counts_ref, flip):
    rows = msg_ref.shape[0] - META
    meta = msg_ref[pl.ds(rows, META), :].astype(jnp.float32)
    lanes = lax.broadcasted_iota(jnp.int32, (1, rows), 1)
    valid = lanes < counts_ref[lax.axis_index("dp"), lax.axis_index("pool") ^ flip]
    return jnp.where(valid, jnp.exp2(meta[0:1] * -LOG2E), 0.0)


def pair_sums(seen, fresh, counts_ref, msgs, sums_ref, own_ref, sums_out, kept_at):
    rows = own_ref.shape[0] if own_ref is not None else msgs[0].shape[0] - META
    emb = {k: msgs[k][pl.ds(0, rows), :] for k in seen + fresh}
    weight = {k: weight_of(msgs[k], counts_ref, k) for k in seen + fresh}
    sums = {k: sums_ref[k] for k in seen if k}
    own_sums = own_ref[...] if own_ref is not None else jnp.zeros((rows, 128), jnp.float32)
    off_diagonal = lax.broadcasted_iota(jnp.int32, (rows, rows), 0) != lax.broadcasted_iota(
        jnp.int32, (rows, rows), 1
    )

    def powers_of(left, right):
        return jnp.exp2(f32_dot(emb[left], emb[right], ((1,), (1,))) * EXP2_SCALE)

    def down(powers, column):
        return jnp.sum(powers * column, axis=0, keepdims=True)

    own_column = column_of(weight[0])[:, 0:1]
    for k in fresh:
        powers = powers_of(0, k)
        if k == 0:
            powers = jnp.where(off_diagonal, powers, 0.0)
        else:
            sums[k] = down(powers, own_column)
        kept_at(k)[...] = powers
        own_sums = own_sums + folded(powers * weight[k])
    others = [k for k in seen if k]
    for k in fresh:
        if k == 0:
            continue
        column = column_of(weight[k])[:, 0:1]
        mine = folded(jnp.where(off_diagonal, powers_of(k, k), 0.0) * weight[k])
        for other in others:
            powers = powers_of(k, other)
            mine = mine + folded(powers * weight[other])
            sums[other] = sums[other] + down(powers, column)
        sums[k] = sums[k] + rows_to_lanes(mine)
        others.append(k)
    return sums, own_sums, weight, own_column


def pairs_kernel(seen, fresh, *refs):
    known = seen + fresh
    counts_ref, refs = refs[0], refs[1:]
    msgs, refs = dict(zip(known, refs)), refs[len(known):]
    before = {}
    own_ref = None
    if seen:
        sums_ref, own_ref, refs = refs[0], refs[1], refs[2:]
        before = {k: sums_ref[at:at + 1, :] for at, k in enumerate(seen)}
    sums_out, own_out, kept_out = refs
    sums, own_sums, _, _ = pair_sums(
        seen, fresh, counts_ref, msgs, before, own_ref, sums_out, lambda k: kept_out.at[fresh.index(k)]
    )
    own_out[...] = own_sums
    for at, k in enumerate(known):
        sums_out[at:at + 1, :] = sums[k] if k else jnp.zeros_like(sums_out[0:1, :])


def pairs_cost(seen, fresh, rows, width):
    pairs = len(fresh) * len(seen) + len(fresh) * (len(fresh) + 1) // 2
    return pl.CostEstimate(
        flops=2 * pairs * rows * rows * width,
        bytes_accessed=2 * (len(seen) + len(fresh)) * rows * width + 4 * len(fresh) * rows * rows,
        transcendentals=pairs * rows * rows,
    )


def add_pairs(seen, fresh, counts, msgs, state):
    known = seen + fresh
    rows, width = msgs[0].shape[0] - META, msgs[0].shape[1]
    return pl.pallas_call(
        functools.partial(pairs_kernel, seen, fresh),
        out_shape=(
            jax.ShapeDtypeStruct((len(known), rows), jnp.float32),
            jax.ShapeDtypeStruct((rows, 128), jnp.float32),
            jax.ShapeDtypeStruct((len(fresh), rows, rows), jnp.float32),
        ),
        in_specs=[SMEM] + [VMEM] * (len(known) + len(state)),
        out_specs=(VMEM,) * 3,
        compiler_params=pltpu.CompilerParams(vmem_limit_bytes=VMEM_LIMIT),
        cost_estimate=pairs_cost(seen, fresh, rows, width),
        name="add_pairs",
    )(counts, *(msgs[k] for k in known), *state)


def grad_kernel(stages, fresh, *refs):
    seen = [k for stage in stages for k in stage]
    known = seen + fresh
    counts_ref, refs = refs[0], refs[1:]
    msgs, refs = dict(zip(known, refs)), refs[len(known):]
    sums_ref, own_ref, refs = refs[0], refs[1], refs[2:]
    stage_refs, refs = refs[:len(stages)], refs[len(stages):]
    normed_ref, inv_ref, out_ref, kept = refs[-4:]
    rows, width = normed_ref.shape
    before = {k: sums_ref[at:at + 1, :] for at, k in enumerate(seen)}
    sums, own_sums, weight, own_weight = pair_sums(
        seen, fresh, counts_ref, msgs, before, own_ref, None, lambda k: kept.at[fresh.index(k)]
    )
    sums[0] = rows_to_lanes(own_sums)
    places = {k: kept.at[at] for at, k in enumerate(fresh)}
    for stage, ref in zip(stages, stage_refs):
        for at, k in enumerate(stage):
            places[k] = ref.at[at]

    me = lax.axis_index("pool")
    lanes = lax.broadcasted_iota(jnp.int32, (1, rows), 1)
    own_rows = me * rows + lax.broadcasted_iota(jnp.int32, (rows, 1), 0)

    def partner_of(k):
        meta = msgs[k][pl.ds(rows, META), :].astype(jnp.float32)
        return jnp.where(weight[k] > 0.0, meta[1:2] * DIGIT + meta[2:3], -1.0)

    recip = {k: jnp.where(weight[k] > 0.0, 1.0 / sums[k], 0.0) for k in known}
    own_recip = column_of(recip[0])[:, 0:1]
    own_partner = column_of(partner_of(0))[:, 0:1].astype(jnp.int32)
    both = jnp.zeros((2 * rows, width), jnp.float32)
    for k in known:
        columns = (me ^ k) * rows + lanes
        powers = places[k][...]
        along = powers * weight[k] * own_recip - jnp.where(own_partner == columns, 1.0, 0.0)
        across = powers * own_weight * recip[k] - jnp.where(
            partner_of(k).astype(jnp.int32) == own_rows, 1.0, 0.0
        )
        coefficients = jnp.concatenate([along.astype(jnp.bfloat16), across.astype(jnp.bfloat16)], axis=0)
        both = both + f32_dot(coefficients, msgs[k][pl.ds(0, rows), :], ((1,), (0,)))
    grad = both[:rows] + both[rows:]
    normed = normed_ref[...]
    inward = jnp.sum(normed * grad, axis=1, keepdims=True)
    out_ref[0] = ((grad - normed * inward) * inv_ref[:, 0:1]).astype(jnp.bfloat16)


def group_grad(stages, fresh, counts, msgs, state, kept, earlier, normed, inv):
    seen = [k for stage in stages for k in stage]
    known = seen + fresh
    rows, width = normed.shape
    return pl.pallas_call(
        functools.partial(grad_kernel, stages, fresh),
        out_shape=jax.ShapeDtypeStruct((1, rows, width), jnp.bfloat16),
        in_specs=[SMEM] + [VMEM] * (len(known) + len(state) + len(kept) + len(earlier) + 2),
        out_specs=VMEM,
        scratch_shapes=[pltpu.VMEM((len(fresh), rows, rows), jnp.float32)],
        compiler_params=pltpu.CompilerParams(vmem_limit_bytes=VMEM_LIMIT),
        cost_estimate=pairs_cost(seen, fresh, rows, width),
        name="group_grad",
    )(counts, *(msgs[k] for k in known), *state, *kept, *earlier, normed, inv)


def distinct(arrays):
    found = []
    for array in arrays:
        if all(array is not other for other in found):
            found.append(array)
    return found, [next(at for at, other in enumerate(found) if array is other) for array in arrays]


def pack_kernel(places, *refs):
    for at, (array, row) in enumerate(places):
        refs[-1][at] = refs[array][row]


def pack(pieces, earlier=()):
    arrays, which = distinct([array for array, _ in pieces])
    shape = (len(pieces),) + arrays[0].shape[1:]
    return pl.pallas_call(
        functools.partial(pack_kernel, [(at, piece[1]) for at, piece in zip(which, pieces)]),
        out_shape=jax.ShapeDtypeStruct(shape, arrays[0].dtype),
        in_specs=[VMEM] * (len(arrays) + len(earlier)),
        out_specs=VMEM,
        compiler_params=pltpu.CompilerParams(vmem_limit_bytes=VMEM_LIMIT),
        cost_estimate=pl.CostEstimate(flops=0, bytes_accessed=4 * math.prod(shape), transcendentals=0),
        name="pack",
    )(*arrays, *earlier)


def weight_kernel(places, minor, inputs, *refs):
    arrays, outs, total = refs[:inputs], refs[inputs:-1], refs[-1]
    majors, piece, _ = outs[0].shape
    me = lax.axis_index("pool")
    result = None
    for array, row, grad_array, grad_row in places:
        term = f32_dot(arrays[array][row], arrays[grad_array][grad_row], ((0,), (0,)))
        result = term if result is None else result + term
    total[...] = result
    for near, out in enumerate(outs):
        for far in range(majors):
            first = pl.multiple_of((me ^ (far * minor + near)) * piece, piece)
            out[far] = total[pl.ds(first, piece), :].astype(out.dtype)


def weight_grad(blocks, grads, members, minor):
    blocks, grads = sorted(blocks, key=lambda each: each[0]), sorted(grads, key=lambda each: each[0])
    arrays, which = distinct([array for _, array, _ in blocks + grads])
    parts = len(blocks)
    places = [(which[at], blocks[at][2], which[parts + at], grads[at][2]) for at in range(parts)]
    _, rows, cols = blocks[0][1].shape
    width = grads[0][1].shape[2]
    pieces = (members // minor, cols // members, width)
    return pl.pallas_call(
        functools.partial(weight_kernel, places, minor, len(arrays)),
        out_shape=(jax.ShapeDtypeStruct(pieces, jnp.float32),)
        + (jax.ShapeDtypeStruct(pieces, jnp.bfloat16),) * (minor - 1),
        in_specs=[VMEM] * len(arrays),
        out_specs=(VMEM,) * minor,
        scratch_shapes=[pltpu.VMEM((cols, width), jnp.float32)],
        compiler_params=pltpu.CompilerParams(vmem_limit_bytes=VMEM_LIMIT),
        cost_estimate=pl.CostEstimate(
            flops=2 * parts * rows * cols * width, bytes_accessed=2 * parts * rows * cols, transcendentals=0
        ),
        name="weight_grad",
    )(*arrays)


def add_pieces_kernel(came, own_ref, *refs):
    for far, out in enumerate(refs[came:]):
        total = own_ref[far]
        for ref in refs[:came]:
            total = total + ref[far].astype(jnp.float32)
        out[...] = total.astype(out.dtype)


def add_pieces(own, came):
    majors, *piece = own.shape
    return pl.pallas_call(
        functools.partial(add_pieces_kernel, len(came)),
        out_shape=(jax.ShapeDtypeStruct(piece, jnp.float32),)
        + (jax.ShapeDtypeStruct(piece, jnp.bfloat16),) * (majors - 1),
        in_specs=[VMEM] * (1 + len(came)),
        out_specs=(VMEM,) * majors,
        compiler_params=pltpu.CompilerParams(vmem_limit_bytes=SMALL_VMEM_LIMIT),
        cost_estimate=pl.CostEstimate(flops=own.size, bytes_accessed=8 * own.size, transcendentals=0),
        name="add_pieces",
    )(own, *came)


def swap(value, axis, flip):
    size = lax.axis_size(axis)
    return lax.ppermute(value, axis, [(at, at ^ flip) for at in range(size)])


def order_kernel(value_ref, *refs):
    refs[-1][...] = value_ref[...]


def after(value, *earlier):
    return pl.pallas_call(
        order_kernel,
        out_shape=jax.ShapeDtypeStruct(value.shape, value.dtype),
        in_specs=[VMEM] * (1 + len(earlier)),
        out_specs=VMEM,
        compiler_params=pltpu.CompilerParams(vmem_limit_bytes=SMALL_VMEM_LIMIT),
        name="after",
    )(value, *earlier)


def per_device(feats, tower_w, partners, popularity_buckets, row_counts):
    members = lax.axis_size("pool")
    parts = lax.axis_size("dp")
    minor = 1 << ((members.bit_length() - 1) // 2)
    msg, normed, inv, near_cuts, far_cuts = project(feats, tower_w, partners[None, :], popularity_buckets[None, :], parts)

    came = swap(far_cuts, "dp", parts // 2)

    msgs = {0: msg}
    for near in range(1, minor):
        msgs[near] = swap(msg, "pool", near)
    bits = []
    bit = minor
    while bit < members:
        bits.append(bit)
        msgs[bit] = swap(msg, "pool", bit)
        bit *= 2
    first = bits[0]
    for near in range(1, minor):
        msgs[first + near] = swap(msgs[first], "pool", near)
    majors = list(range(0, members, minor))
    early = [far + near for far in majors[:-2] for near in range(minor)]
    held = early[1 - minor:]
    early = early[:1 - minor]
    state, kept, stages = (), [], []

    def add(fresh):
        nonlocal state
        *state, powers = add_pairs(sum(stages, []), fresh, row_counts, msgs, state)
        kept.append(powers)
        stages.append(fresh)

    add(early)
    last = bits[-1]
    for k in range(first + minor, last, minor):
        msgs[k] = swap(msgs[first], "pool", k ^ first)
    relayed = after(msgs[last], state[1])
    for k in range(last + minor, members, minor):
        msgs[k] = swap(relayed, "pool", k ^ last)
    for far in majors[2:-1]:
        for near in range(1, minor):
            msgs[far + near] = swap(msgs[far], "pool", near)
    add(held + majors[2:-1])
    relayed = after(msgs[majors[-1]], state[1])
    for near in range(1, minor):
        msgs[majors[-1] + near] = swap(relayed, "pool", near)
    add([majors[-1]])
    add([far + near for far in majors[2:-1] for near in range(1, minor)])
    bit = parts // 2
    blocks = {k: [(0, near_cuts, k), (bit, came, k)] for k in range(bit)}
    bit //= 2
    while bit:
        moving = [(k ^ bit, source ^ bit, array, at) for k in blocks if k & bit for source, array, at in blocks[k]]
        blocks = {k: blocks[k] for k in blocks if not k & bit}
        passed = swap(pack([each[2:] for each in moving], [state[1]]), "dp", bit)
        for at, (k, source, _, _) in enumerate(moving):
            blocks[k].append((source, passed, at))
        bit //= 2
    grad_proj = group_grad(
        stages, [majors[-1] + near for near in range(1, minor)], row_counts, msgs, state, kept, [], normed, inv
    )

    bit = parts // 2
    grads = [(0, grad_proj, 0)]
    while bit:
        sent = swap(grad_proj if len(grads) == 1 else pack([each[1:] for each in grads]), "dp", bit)
        grads += [(each[0] ^ bit, sent, at) for at, each in enumerate(grads)]
        bit //= 2

    own, *pieces = weight_grad(blocks[0], grads, members, minor)
    pieces = [swap(each, "pool", near + 1) for near, each in enumerate(pieces)]
    total, *pieces = add_pieces(own, pieces)
    for far in reversed(range(1, members // minor)):
        total = total + swap(pieces[far - 1], "pool", far * minor).astype(jnp.float32)
    return total


def solution(mesh):
    return jax.shard_map(
        per_device,
        mesh=mesh,
        in_specs=(P(("dp", "pool"), None), P(), P(("dp", "pool")), P(("dp", "pool")), P()),
        out_specs=P(("dp", "pool"), None),
        check_vma=False,
    )
```

```python
import functools
import math

import jax
import jax.numpy as jnp
from jax import lax
from jax.experimental import pallas as pl
from jax.experimental.pallas import tpu as pltpu
from jax.sharding import PartitionSpec as P

sharpness_scaler = 0.05
epsilon = 1e-06
META = 16
DIGIT_BITS = 8
DIGIT = 1 << DIGIT_BITS
EXP2_SCALE = math.log2(math.e) / sharpness_scaler
LOG2E = math.log2(math.e)
VMEM_LIMIT = 40 * 1024 * 1024
SMALL_VMEM_LIMIT = 8 * 1024 * 1024

VMEM = pl.BlockSpec(memory_space=pltpu.VMEM)
SMEM = pl.BlockSpec(memory_space=pltpu.SMEM)
HBM = pl.BlockSpec(memory_space=pltpu.HBM)


def f32_dot(left, right, dims):
    return lax.dot_general(left, right, (dims, ((), ())), preferred_element_type=jnp.float32)


def column_of(row):
    return jnp.transpose(jnp.broadcast_to(row, (128, row.shape[1])))


def project_kernel(parts, feats_hbm, w_hbm, partners_hbm, buckets_hbm, msg_ref, normed_ref, inv_ref,
                   near_ref, far_ref, w_v, partners_ref, buckets_ref, sems, small_sems):
    half, rows, step = near_ref.shape
    cuts = [near_ref.at[k] for k in range(half)] + [far_ref.at[k] for k in range(half)]
    width = w_v.shape[1]
    me = lax.axis_index("dp")
    small = (
        pltpu.make_async_copy(partners_hbm, partners_ref, small_sems.at[0]),
        pltpu.make_async_copy(buckets_hbm, buckets_ref, small_sems.at[1]),
    )
    for copy in small:
        copy.start()
    copies = []
    for k in range(parts):
        first = pl.multiple_of((me ^ k) * step, step)
        cut = pl.ds(first, step)
        pair = (
            pltpu.make_async_copy(feats_hbm.at[:, cut], cuts[k], sems.at[0, k]),
            pltpu.make_async_copy(w_hbm.at[cut, :], w_v.at[pl.ds(k * step, step), :], sems.at[1, k]),
        )
        pair[0].start()
        pair[1].start()
        copies.append(pair)
    projected = jnp.zeros((rows, width), jnp.float32)
    for k in range(parts):
        copies[k][0].wait()
        copies[k][1].wait()
        projected = projected + f32_dot(cuts[k][...], w_v[pl.ds(k * step, step), :], ((1,), (0,)))
    for copy in small:
        copy.wait()
    partners = partners_ref[...]
    logq = -(buckets_ref[...].astype(jnp.float32) + 0.5) / 4.0
    high = (partners >> DIGIT_BITS).astype(jnp.float32)
    low = (partners & (DIGIT - 1)).astype(jnp.float32)
    kinds = lax.broadcasted_iota(jnp.int32, (META, rows), 0)
    meta = jnp.where(kinds == 0, logq, jnp.where(kinds == 1, high, jnp.where(kinds == 2, low, 0.0)))
    msg_ref[pl.ds(rows, META), :] = meta.astype(jnp.bfloat16)
    inv_norm = lax.rsqrt(jnp.sum(projected * projected, axis=1, keepdims=True) + epsilon)
    normed = projected * inv_norm
    normed_ref[...] = normed
    inv_ref[...] = jnp.broadcast_to(inv_norm, inv_ref.shape)
    msg_ref[pl.ds(0, rows), :] = normed.astype(jnp.bfloat16)


def project(feats, tower_w, partners, buckets, parts):
    rows, din = feats.shape
    width = tower_w.shape[1]
    return pl.pallas_call(
        functools.partial(project_kernel, parts),
        out_shape=(
            jax.ShapeDtypeStruct((rows + META, width), jnp.bfloat16),
            jax.ShapeDtypeStruct((rows, width), jnp.float32),
            jax.ShapeDtypeStruct((rows, 128), jnp.float32),
        )
        + (jax.ShapeDtypeStruct((parts // 2, rows, din // parts), feats.dtype),) * 2,
        in_specs=[HBM, HBM, HBM, HBM],
        out_specs=(VMEM,) * 5,
        scratch_shapes=[
            pltpu.VMEM((din, width), jnp.bfloat16),
            pltpu.VMEM((1, rows), jnp.int32),
            pltpu.VMEM((1, rows), jnp.int32),
            pltpu.SemaphoreType.DMA((2, parts)),
            pltpu.SemaphoreType.DMA((2,)),
        ],
        compiler_params=pltpu.CompilerParams(vmem_limit_bytes=VMEM_LIMIT),
        cost_estimate=pl.CostEstimate(
            flops=2 * rows * din * width, bytes_accessed=2 * din * (rows + width), transcendentals=rows
        ),
        name="project",
    )(*(pltpu.with_memory_space_constraint(each, pltpu.HBM) for each in (feats, tower_w, partners, buckets)))


def folded(terms):
    total = terms[:, 0:128]
    for at in range(128, terms.shape[1], 128):
        total = total + terms[:, at:at + 128]
    return total


def rows_to_lanes(sums):
    return jnp.sum(jnp.transpose(sums), axis=0, keepdims=True)


def weight_of(msg_ref, counts_ref, flip):
    rows = msg_ref.shape[0] - META
    meta = msg_ref[pl.ds(rows, META), :].astype(jnp.float32)
    lanes = lax.broadcasted_iota(jnp.int32, (1, rows), 1)
    valid = lanes < counts_ref[lax.axis_index("dp"), lax.axis_index("pool") ^ flip]
    return jnp.where(valid, jnp.exp2(meta[0:1] * -LOG2E), 0.0)


def pair_sums(seen, fresh, counts_ref, msgs, sums_ref, own_ref, sums_out, kept_at):
    rows = own_ref.shape[0] if own_ref is not None else msgs[0].shape[0] - META
    emb = {k: msgs[k][pl.ds(0, rows), :] for k in seen + fresh}
    weight = {k: weight_of(msgs[k], counts_ref, k) for k in seen + fresh}
    sums = {k: sums_ref[k] for k in seen if k}
    own_sums = own_ref[...] if own_ref is not None else jnp.zeros((rows, 128), jnp.float32)
    off_diagonal = lax.broadcasted_iota(jnp.int32, (rows, rows), 0) != lax.broadcasted_iota(
        jnp.int32, (rows, rows), 1
    )

    def powers_of(left, right):
        return jnp.exp2(f32_dot(emb[left], emb[right], ((1,), (1,))) * EXP2_SCALE)

    def down(powers, column):
        return jnp.sum(powers * column, axis=0, keepdims=True)

    own_column = column_of(weight[0])[:, 0:1]
    for k in fresh:
        powers = powers_of(0, k)
        if k == 0:
            powers = jnp.where(off_diagonal, powers, 0.0)
        else:
            sums[k] = down(powers, own_column)
        kept_at(k)[...] = powers
        own_sums = own_sums + folded(powers * weight[k])
    others = [k for k in seen if k]
    for k in fresh:
        if k == 0:
            continue
        column = column_of(weight[k])[:, 0:1]
        mine = folded(jnp.where(off_diagonal, powers_of(k, k), 0.0) * weight[k])
        for other in others:
            powers = powers_of(k, other)
            mine = mine + folded(powers * weight[other])
            sums[other] = sums[other] + down(powers, column)
        sums[k] = sums[k] + rows_to_lanes(mine)
        others.append(k)
    return sums, own_sums, weight, own_column


def pairs_kernel(seen, fresh, *refs):
    known = seen + fresh
    counts_ref, refs = refs[0], refs[1:]
    msgs, refs = dict(zip(known, refs)), refs[len(known):]
    before = {}
    own_ref = None
    if seen:
        sums_ref, own_ref, refs = refs[0], refs[1], refs[2:]
        before = {k: sums_ref[at:at + 1, :] for at, k in enumerate(seen)}
    sums_out, own_out, kept_out = refs
    sums, own_sums, _, _ = pair_sums(
        seen, fresh, counts_ref, msgs, before, own_ref, sums_out, lambda k: kept_out.at[fresh.index(k)]
    )
    own_out[...] = own_sums
    for at, k in enumerate(known):
        sums_out[at:at + 1, :] = sums[k] if k else jnp.zeros_like(sums_out[0:1, :])


def pairs_cost(seen, fresh, rows, width):
    pairs = len(fresh) * len(seen) + len(fresh) * (len(fresh) + 1) // 2
    return pl.CostEstimate(
        flops=2 * pairs * rows * rows * width,
        bytes_accessed=2 * (len(seen) + len(fresh)) * rows * width + 4 * len(fresh) * rows * rows,
        transcendentals=pairs * rows * rows,
    )


def add_pairs(seen, fresh, counts, msgs, state):
    known = seen + fresh
    rows, width = msgs[0].shape[0] - META, msgs[0].shape[1]
    return pl.pallas_call(
        functools.partial(pairs_kernel, seen, fresh),
        out_shape=(
            jax.ShapeDtypeStruct((len(known), rows), jnp.float32),
            jax.ShapeDtypeStruct((rows, 128), jnp.float32),
            jax.ShapeDtypeStruct((len(fresh), rows, rows), jnp.float32),
        ),
        in_specs=[SMEM] + [VMEM] * (len(known) + len(state)),
        out_specs=(VMEM,) * 3,
        compiler_params=pltpu.CompilerParams(vmem_limit_bytes=VMEM_LIMIT),
        cost_estimate=pairs_cost(seen, fresh, rows, width),
        name="add_pairs",
    )(counts, *(msgs[k] for k in known), *state)


def grad_kernel(stages, fresh, *refs):
    seen = [k for stage in stages for k in stage]
    known = seen + fresh
    counts_ref, refs = refs[0], refs[1:]
    msgs, refs = dict(zip(known, refs)), refs[len(known):]
    sums_ref, own_ref, refs = refs[0], refs[1], refs[2:]
    stage_refs, refs = refs[:len(stages)], refs[len(stages):]
    normed_ref, inv_ref, out_ref, kept = refs[-4:]
    rows, width = normed_ref.shape
    before = {k: sums_ref[at:at + 1, :] for at, k in enumerate(seen)}
    sums, own_sums, weight, own_weight = pair_sums(
        seen, fresh, counts_ref, msgs, before, own_ref, None, lambda k: kept.at[fresh.index(k)]
    )
    sums[0] = rows_to_lanes(own_sums)
    places = {k: kept.at[at] for at, k in enumerate(fresh)}
    for stage, ref in zip(stages, stage_refs):
        for at, k in enumerate(stage):
            places[k] = ref.at[at]

    me = lax.axis_index("pool")
    lanes = lax.broadcasted_iota(jnp.int32, (1, rows), 1)
    own_rows = me * rows + lax.broadcasted_iota(jnp.int32, (rows, 1), 0)

    def partner_of(k):
        meta = msgs[k][pl.ds(rows, META), :].astype(jnp.float32)
        return jnp.where(weight[k] > 0.0, meta[1:2] * DIGIT + meta[2:3], -1.0)

    recip = {k: jnp.where(weight[k] > 0.0, 1.0 / sums[k], 0.0) for k in known}
    own_recip = column_of(recip[0])[:, 0:1]
    own_partner = column_of(partner_of(0))[:, 0:1].astype(jnp.int32)
    both = jnp.zeros((2 * rows, width), jnp.float32)
    for k in known:
        columns = (me ^ k) * rows + lanes
        powers = places[k][...]
        along = powers * weight[k] * own_recip - jnp.where(own_partner == columns, 1.0, 0.0)
        across = powers * own_weight * recip[k] - jnp.where(
            partner_of(k).astype(jnp.int32) == own_rows, 1.0, 0.0
        )
        coefficients = jnp.concatenate([along.astype(jnp.bfloat16), across.astype(jnp.bfloat16)], axis=0)
        both = both + f32_dot(coefficients, msgs[k][pl.ds(0, rows), :], ((1,), (0,)))
    grad = both[:rows] + both[rows:]
    normed = normed_ref[...]
    inward = jnp.sum(normed * grad, axis=1, keepdims=True)
    out_ref[0] = ((grad - normed * inward) * inv_ref[:, 0:1]).astype(jnp.bfloat16)


def group_grad(stages, fresh, counts, msgs, state, kept, earlier, normed, inv):
    seen = [k for stage in stages for k in stage]
    known = seen + fresh
    rows, width = normed.shape
    return pl.pallas_call(
        functools.partial(grad_kernel, stages, fresh),
        out_shape=jax.ShapeDtypeStruct((1, rows, width), jnp.bfloat16),
        in_specs=[SMEM] + [VMEM] * (len(known) + len(state) + len(kept) + len(earlier) + 2),
        out_specs=VMEM,
        scratch_shapes=[pltpu.VMEM((len(fresh), rows, rows), jnp.float32)],
        compiler_params=pltpu.CompilerParams(vmem_limit_bytes=VMEM_LIMIT),
        cost_estimate=pairs_cost(seen, fresh, rows, width),
        name="group_grad",
    )(counts, *(msgs[k] for k in known), *state, *kept, *earlier, normed, inv)


def distinct(arrays):
    found = []
    for array in arrays:
        if all(array is not other for other in found):
            found.append(array)
    return found, [next(at for at, other in enumerate(found) if array is other) for array in arrays]


def pack_kernel(places, *refs):
    for at, (array, row) in enumerate(places):
        refs[-1][at] = refs[array][row]


def pack(pieces, earlier=()):
    arrays, which = distinct([array for array, _ in pieces])
    shape = (len(pieces),) + arrays[0].shape[1:]
    return pl.pallas_call(
        functools.partial(pack_kernel, [(at, piece[1]) for at, piece in zip(which, pieces)]),
        out_shape=jax.ShapeDtypeStruct(shape, arrays[0].dtype),
        in_specs=[VMEM] * (len(arrays) + len(earlier)),
        out_specs=VMEM,
        compiler_params=pltpu.CompilerParams(vmem_limit_bytes=VMEM_LIMIT),
        cost_estimate=pl.CostEstimate(flops=0, bytes_accessed=4 * math.prod(shape), transcendentals=0),
        name="pack",
    )(*arrays, *earlier)


def weight_kernel(places, minor, inputs, *refs):
    arrays, outs, total = refs[:inputs], refs[inputs:-1], refs[-1]
    majors, piece, _ = outs[0].shape
    me = lax.axis_index("pool")
    result = None
    for array, row, grad_array, grad_row in places:
        term = f32_dot(arrays[array][row], arrays[grad_array][grad_row], ((0,), (0,)))
        result = term if result is None else result + term
    total[...] = result
    for near, out in enumerate(outs):
        for far in range(majors):
            first = pl.multiple_of((me ^ (far * minor + near)) * piece, piece)
            out[far] = total[pl.ds(first, piece), :].astype(out.dtype)


def weight_grad(blocks, grads, members, minor):
    blocks, grads = sorted(blocks, key=lambda each: each[0]), sorted(grads, key=lambda each: each[0])
    arrays, which = distinct([array for _, array, _ in blocks + grads])
    parts = len(blocks)
    places = [(which[at], blocks[at][2], which[parts + at], grads[at][2]) for at in range(parts)]
    _, rows, cols = blocks[0][1].shape
    width = grads[0][1].shape[2]
    pieces = (members // minor, cols // members, width)
    return pl.pallas_call(
        functools.partial(weight_kernel, places, minor, len(arrays)),
        out_shape=(jax.ShapeDtypeStruct(pieces, jnp.float32),)
        + (jax.ShapeDtypeStruct(pieces, jnp.bfloat16),) * (minor - 1),
        in_specs=[VMEM] * len(arrays),
        out_specs=(VMEM,) * minor,
        scratch_shapes=[pltpu.VMEM((cols, width), jnp.float32)],
        compiler_params=pltpu.CompilerParams(vmem_limit_bytes=VMEM_LIMIT),
        cost_estimate=pl.CostEstimate(
            flops=2 * parts * rows * cols * width, bytes_accessed=2 * parts * rows * cols, transcendentals=0
        ),
        name="weight_grad",
    )(*arrays)


def add_pieces_kernel(came, own_ref, *refs):
    for far, out in enumerate(refs[came:]):
        total = own_ref[far]
        for ref in refs[:came]:
            total = total + ref[far].astype(jnp.float32)
        out[...] = total.astype(out.dtype)


def add_pieces(own, came):
    majors, *piece = own.shape
    return pl.pallas_call(
        functools.partial(add_pieces_kernel, len(came)),
        out_shape=(jax.ShapeDtypeStruct(piece, jnp.float32),)
        + (jax.ShapeDtypeStruct(piece, jnp.bfloat16),) * (majors - 1),
        in_specs=[VMEM] * (1 + len(came)),
        out_specs=(VMEM,) * majors,
        compiler_params=pltpu.CompilerParams(vmem_limit_bytes=SMALL_VMEM_LIMIT),
        cost_estimate=pl.CostEstimate(flops=own.size, bytes_accessed=8 * own.size, transcendentals=0),
        name="add_pieces",
    )(own, *came)


def swap(value, axis, flip):
    size = lax.axis_size(axis)
    return lax.ppermute(value, axis, [(at, at ^ flip) for at in range(size)])


def order_kernel(value_ref, *refs):
    refs[-1][...] = value_ref[...]


def after(value, *earlier):
    return pl.pallas_call(
        order_kernel,
        out_shape=jax.ShapeDtypeStruct(value.shape, value.dtype),
        in_specs=[VMEM] * (1 + len(earlier)),
        out_specs=VMEM,
        compiler_params=pltpu.CompilerParams(vmem_limit_bytes=SMALL_VMEM_LIMIT),
        name="after",
    )(value, *earlier)


def per_device(feats, tower_w, partners, popularity_buckets, row_counts):
    members = lax.axis_size("pool")
    parts = lax.axis_size("dp")
    minor = 1 << ((members.bit_length() - 1) // 2)
    msg, normed, inv, near_cuts, far_cuts = project(feats, tower_w, partners[None, :], popularity_buckets[None, :], parts)

    majors = list(range(0, members, minor))
    last = members // 2
    msgs = {0: msg}
    msgs[last] = swap(msg, "pool", last)
    for k in majors[1:]:
        if k < last:
            msgs[k] = swap(msg, "pool", k)
    for near in range(1, minor):
        msgs[near] = swap(msg, "pool", near)
    for far in majors[1:-2]:
        for near in range(1, minor):
            msgs[far + near] = swap(msgs[far], "pool", near)
    relayed = msgs[last]
    for k in majors:
        if k > last:
            msgs[k] = swap(relayed, "pool", k ^ last)
    for near in range(1, minor):
        msgs[last + near] = swap(msgs[last], "pool", near)

    came = swap(far_cuts, "dp", parts // 2)

    state, kept, stages = (), [], []

    def add(fresh):
        nonlocal state
        *state, powers = add_pairs(sum(stages, []), fresh, row_counts, msgs, state)
        kept.append(powers)
        stages.append(fresh)

    add(majors[:-1] + list(range(1, minor)))
    add([far + near for far in majors[1:-2] for near in range(1, minor)])
    msgs3 = after(msgs[majors[-1]], state[1])
    for near in range(1, minor):
        msgs[majors[-1] + near] = swap(msgs3, "pool", near)
    add([majors[-1]])
    add([majors[-2] + near for near in range(1, minor)])
    bit = parts // 2
    blocks = {k: [(0, near_cuts, k), (bit, came, k)] for k in range(bit)}
    bit //= 2
    while bit:
        moving = [(k ^ bit, source ^ bit, array, at) for k in blocks if k & bit for source, array, at in blocks[k]]
        blocks = {k: blocks[k] for k in blocks if not k & bit}
        passed = swap(pack([each[2:] for each in moving], [state[1]]), "dp", bit)
        for at, (k, source, _, _) in enumerate(moving):
            blocks[k].append((source, passed, at))
        bit //= 2

    final = [majors[-1] + near for near in range(1, minor)]
    grad_proj = group_grad(stages, final, row_counts, msgs, state, kept, [], normed, inv)

    bit = parts // 2
    grads = [(0, grad_proj, 0)]
    while bit:
        sent = swap(grad_proj if len(grads) == 1 else pack([each[1:] for each in grads]), "dp", bit)
        grads += [(each[0] ^ bit, sent, at) for at, each in enumerate(grads)]
        bit //= 2

    own, *pieces = weight_grad(blocks[0], grads, members, minor)
    pieces = [swap(each, "pool", near + 1) for near, each in enumerate(pieces)]
    total, *pieces = add_pieces(own, pieces)
    for far in reversed(range(1, members // minor)):
        total = total + swap(pieces[far - 1], "pool", far * minor).astype(jnp.float32)
    return total


def solution(mesh):
    return jax.shard_map(
        per_device,
        mesh=mesh,
        in_specs=(P(("dp", "pool"), None), P(), P(("dp", "pool")), P(("dp", "pool")), P()),
        out_specs=P(("dp", "pool"), None),
        check_vma=False,
    )
```

```python
import functools
import math

import jax
import jax.numpy as jnp
from jax import lax
from jax.experimental import pallas as pl
from jax.experimental.pallas import tpu as pltpu
from jax.sharding import PartitionSpec as P

sharpness_scaler = 0.05
epsilon = 1e-06
META = 16
DIGIT_BITS = 8
DIGIT = 1 << DIGIT_BITS
EXP2_SCALE = math.log2(math.e) / sharpness_scaler
LOG2E = math.log2(math.e)
VMEM_LIMIT = 40 * 1024 * 1024
SMALL_VMEM_LIMIT = 8 * 1024 * 1024

VMEM = pl.BlockSpec(memory_space=pltpu.VMEM)
SMEM = pl.BlockSpec(memory_space=pltpu.SMEM)
HBM = pl.BlockSpec(memory_space=pltpu.HBM)


def f32_dot(left, right, dims):
    return lax.dot_general(left, right, (dims, ((), ())), preferred_element_type=jnp.float32)


def column_of(row):
    return jnp.transpose(jnp.broadcast_to(row, (128, row.shape[1])))


def project_kernel(parts, feats_hbm, w_hbm, partners_hbm, buckets_hbm, msg_ref, normed_ref, inv_ref,
                   near_ref, far_ref, w_v, partners_ref, buckets_ref, sems, small_sems):
    half, rows, step = near_ref.shape
    cuts = [near_ref.at[k] for k in range(half)] + [far_ref.at[k] for k in range(half)]
    width = w_v.shape[1]
    me = lax.axis_index("dp")
    small = (
        pltpu.make_async_copy(partners_hbm, partners_ref, small_sems.at[0]),
        pltpu.make_async_copy(buckets_hbm, buckets_ref, small_sems.at[1]),
    )
    for copy in small:
        copy.start()
    copies = []
    for k in range(parts):
        first = pl.multiple_of((me ^ k) * step, step)
        cut = pl.ds(first, step)
        pair = (
            pltpu.make_async_copy(feats_hbm.at[:, cut], cuts[k], sems.at[0, k]),
            pltpu.make_async_copy(w_hbm.at[cut, :], w_v.at[pl.ds(k * step, step), :], sems.at[1, k]),
        )
        pair[0].start()
        pair[1].start()
        copies.append(pair)
    projected = jnp.zeros((rows, width), jnp.float32)
    for k in range(parts):
        copies[k][0].wait()
        copies[k][1].wait()
        projected = projected + f32_dot(cuts[k][...], w_v[pl.ds(k * step, step), :], ((1,), (0,)))
    for copy in small:
        copy.wait()
    partners = partners_ref[...]
    logq = -(buckets_ref[...].astype(jnp.float32) + 0.5) / 4.0
    high = (partners >> DIGIT_BITS).astype(jnp.float32)
    low = (partners & (DIGIT - 1)).astype(jnp.float32)
    kinds = lax.broadcasted_iota(jnp.int32, (META, rows), 0)
    meta = jnp.where(kinds == 0, logq, jnp.where(kinds == 1, high, jnp.where(kinds == 2, low, 0.0)))
    msg_ref[pl.ds(rows, META), :] = meta.astype(jnp.bfloat16)
    inv_norm = lax.rsqrt(jnp.sum(projected * projected, axis=1, keepdims=True) + epsilon)
    normed = projected * inv_norm
    normed_ref[...] = normed
    inv_ref[...] = jnp.broadcast_to(inv_norm, inv_ref.shape)
    msg_ref[pl.ds(0, rows), :] = normed.astype(jnp.bfloat16)


def project(feats, tower_w, partners, buckets, parts):
    rows, din = feats.shape
    width = tower_w.shape[1]
    return pl.pallas_call(
        functools.partial(project_kernel, parts),
        out_shape=(
            jax.ShapeDtypeStruct((rows + META, width), jnp.bfloat16),
            jax.ShapeDtypeStruct((rows, width), jnp.float32),
            jax.ShapeDtypeStruct((rows, 128), jnp.float32),
        )
        + (jax.ShapeDtypeStruct((parts // 2, rows, din // parts), feats.dtype),) * 2,
        in_specs=[HBM, HBM, HBM, HBM],
        out_specs=(VMEM,) * 5,
        scratch_shapes=[
            pltpu.VMEM((din, width), jnp.bfloat16),
            pltpu.VMEM((1, rows), jnp.int32),
            pltpu.VMEM((1, rows), jnp.int32),
            pltpu.SemaphoreType.DMA((2, parts)),
            pltpu.SemaphoreType.DMA((2,)),
        ],
        compiler_params=pltpu.CompilerParams(vmem_limit_bytes=VMEM_LIMIT),
        cost_estimate=pl.CostEstimate(
            flops=2 * rows * din * width, bytes_accessed=2 * din * (rows + width), transcendentals=rows
        ),
        name="project",
    )(*(pltpu.with_memory_space_constraint(each, pltpu.HBM) for each in (feats, tower_w, partners, buckets)))


def folded(terms):
    total = terms[:, 0:128]
    for at in range(128, terms.shape[1], 128):
        total = total + terms[:, at:at + 128]
    return total


def rows_to_lanes(sums):
    return jnp.sum(jnp.transpose(sums), axis=0, keepdims=True)


def weight_of(msg_ref, counts_ref, flip):
    rows = msg_ref.shape[0] - META
    meta = msg_ref[pl.ds(rows, META), :].astype(jnp.float32)
    lanes = lax.broadcasted_iota(jnp.int32, (1, rows), 1)
    valid = lanes < counts_ref[lax.axis_index("dp"), lax.axis_index("pool") ^ flip]
    return jnp.where(valid, jnp.exp2(meta[0:1] * -LOG2E), 0.0)


def pair_sums(seen, fresh, counts_ref, msgs, sums_ref, own_ref, sums_out, kept_at):
    rows = own_ref.shape[0] if own_ref is not None else msgs[0].shape[0] - META
    emb = {k: msgs[k][pl.ds(0, rows), :] for k in seen + fresh}
    weight = {k: weight_of(msgs[k], counts_ref, k) for k in seen + fresh}
    sums = {k: sums_ref[k] for k in seen if k}
    own_sums = own_ref[...] if own_ref is not None else jnp.zeros((rows, 128), jnp.float32)
    off_diagonal = lax.broadcasted_iota(jnp.int32, (rows, rows), 0) != lax.broadcasted_iota(
        jnp.int32, (rows, rows), 1
    )

    def powers_of(left, right):
        return jnp.exp2(f32_dot(emb[left], emb[right], ((1,), (1,))) * EXP2_SCALE)

    def down(powers, column):
        return jnp.sum(powers * column, axis=0, keepdims=True)

    own_column = column_of(weight[0])[:, 0:1]
    for k in fresh:
        powers = powers_of(0, k)
        if k == 0:
            powers = jnp.where(off_diagonal, powers, 0.0)
        else:
            sums[k] = down(powers, own_column)
        kept_at(k)[...] = powers
        own_sums = own_sums + folded(powers * weight[k])
    others = [k for k in seen if k]
    for k in fresh:
        if k == 0:
            continue
        column = column_of(weight[k])[:, 0:1]
        mine = folded(jnp.where(off_diagonal, powers_of(k, k), 0.0) * weight[k])
        for other in others:
            powers = powers_of(k, other)
            mine = mine + folded(powers * weight[other])
            sums[other] = sums[other] + down(powers, column)
        sums[k] = sums[k] + rows_to_lanes(mine)
        others.append(k)
    return sums, own_sums, weight, own_column


def pairs_kernel(seen, fresh, *refs):
    known = seen + fresh
    counts_ref, refs = refs[0], refs[1:]
    msgs, refs = dict(zip(known, refs)), refs[len(known):]
    before = {}
    own_ref = None
    if seen:
        sums_ref, own_ref, refs = refs[0], refs[1], refs[2:]
        before = {k: sums_ref[at:at + 1, :] for at, k in enumerate(seen)}
    sums_out, own_out, kept_out = refs
    sums, own_sums, _, _ = pair_sums(
        seen, fresh, counts_ref, msgs, before, own_ref, sums_out, lambda k: kept_out.at[fresh.index(k)]
    )
    own_out[...] = own_sums
    for at, k in enumerate(known):
        sums_out[at:at + 1, :] = sums[k] if k else jnp.zeros_like(sums_out[0:1, :])


def pairs_cost(seen, fresh, rows, width):
    pairs = len(fresh) * len(seen) + len(fresh) * (len(fresh) + 1) // 2
    return pl.CostEstimate(
        flops=2 * pairs * rows * rows * width,
        bytes_accessed=2 * (len(seen) + len(fresh)) * rows * width + 4 * len(fresh) * rows * rows,
        transcendentals=pairs * rows * rows,
    )


def add_pairs(seen, fresh, counts, msgs, state):
    known = seen + fresh
    rows, width = msgs[0].shape[0] - META, msgs[0].shape[1]
    return pl.pallas_call(
        functools.partial(pairs_kernel, seen, fresh),
        out_shape=(
            jax.ShapeDtypeStruct((len(known), rows), jnp.float32),
            jax.ShapeDtypeStruct((rows, 128), jnp.float32),
            jax.ShapeDtypeStruct((len(fresh), rows, rows), jnp.float32),
        ),
        in_specs=[SMEM] + [VMEM] * (len(known) + len(state)),
        out_specs=(VMEM,) * 3,
        compiler_params=pltpu.CompilerParams(vmem_limit_bytes=VMEM_LIMIT),
        cost_estimate=pairs_cost(seen, fresh, rows, width),
        name="add_pairs",
    )(counts, *(msgs[k] for k in known), *state)


def grad_kernel(stages, fresh, *refs):
    seen = [k for stage in stages for k in stage]
    known = seen + fresh
    counts_ref, refs = refs[0], refs[1:]
    msgs, refs = dict(zip(known, refs)), refs[len(known):]
    sums_ref, own_ref, refs = refs[0], refs[1], refs[2:]
    stage_refs, refs = refs[:len(stages)], refs[len(stages):]
    normed_ref, inv_ref, out_ref, kept = refs[-4:]
    rows, width = normed_ref.shape
    before = {k: sums_ref[at:at + 1, :] for at, k in enumerate(seen)}
    sums, own_sums, weight, own_weight = pair_sums(
        seen, fresh, counts_ref, msgs, before, own_ref, None, lambda k: kept.at[fresh.index(k)]
    )
    sums[0] = rows_to_lanes(own_sums)
    places = {k: kept.at[at] for at, k in enumerate(fresh)}
    for stage, ref in zip(stages, stage_refs):
        for at, k in enumerate(stage):
            places[k] = ref.at[at]

    me = lax.axis_index("pool")
    lanes = lax.broadcasted_iota(jnp.int32, (1, rows), 1)
    own_rows = me * rows + lax.broadcasted_iota(jnp.int32, (rows, 1), 0)

    def partner_of(k):
        meta = msgs[k][pl.ds(rows, META), :].astype(jnp.float32)
        return jnp.where(weight[k] > 0.0, meta[1:2] * DIGIT + meta[2:3], -1.0)

    recip = {k: jnp.where(weight[k] > 0.0, 1.0 / sums[k], 0.0) for k in known}
    own_recip = column_of(recip[0])[:, 0:1]
    own_partner = column_of(partner_of(0))[:, 0:1].astype(jnp.int32)
    both = jnp.zeros((2 * rows, width), jnp.float32)
    for k in known:
        columns = (me ^ k) * rows + lanes
        powers = places[k][...]
        along = powers * weight[k] * own_recip - jnp.where(own_partner == columns, 1.0, 0.0)
        across = powers * own_weight * recip[k] - jnp.where(
            partner_of(k).astype(jnp.int32) == own_rows, 1.0, 0.0
        )
        coefficients = jnp.concatenate([along.astype(jnp.bfloat16), across.astype(jnp.bfloat16)], axis=0)
        both = both + f32_dot(coefficients, msgs[k][pl.ds(0, rows), :], ((1,), (0,)))
    grad = both[:rows] + both[rows:]
    normed = normed_ref[...]
    inward = jnp.sum(normed * grad, axis=1, keepdims=True)
    out_ref[0] = ((grad - normed * inward) * inv_ref[:, 0:1]).astype(jnp.bfloat16)


def group_grad(stages, fresh, counts, msgs, state, kept, earlier, normed, inv):
    seen = [k for stage in stages for k in stage]
    known = seen + fresh
    rows, width = normed.shape
    return pl.pallas_call(
        functools.partial(grad_kernel, stages, fresh),
        out_shape=jax.ShapeDtypeStruct((1, rows, width), jnp.bfloat16),
        in_specs=[SMEM] + [VMEM] * (len(known) + len(state) + len(kept) + len(earlier) + 2),
        out_specs=VMEM,
        scratch_shapes=[pltpu.VMEM((len(fresh), rows, rows), jnp.float32)],
        compiler_params=pltpu.CompilerParams(vmem_limit_bytes=VMEM_LIMIT),
        cost_estimate=pairs_cost(seen, fresh, rows, width),
        name="group_grad",
    )(counts, *(msgs[k] for k in known), *state, *kept, *earlier, normed, inv)


def distinct(arrays):
    found = []
    for array in arrays:
        if all(array is not other for other in found):
            found.append(array)
    return found, [next(at for at, other in enumerate(found) if array is other) for array in arrays]


def pack_kernel(places, *refs):
    for at, (array, row) in enumerate(places):
        refs[-1][at] = refs[array][row]


def pack(pieces, earlier=()):
    arrays, which = distinct([array for array, _ in pieces])
    shape = (len(pieces),) + arrays[0].shape[1:]
    return pl.pallas_call(
        functools.partial(pack_kernel, [(at, piece[1]) for at, piece in zip(which, pieces)]),
        out_shape=jax.ShapeDtypeStruct(shape, arrays[0].dtype),
        in_specs=[VMEM] * (len(arrays) + len(earlier)),
        out_specs=VMEM,
        compiler_params=pltpu.CompilerParams(vmem_limit_bytes=VMEM_LIMIT),
        cost_estimate=pl.CostEstimate(flops=0, bytes_accessed=4 * math.prod(shape), transcendentals=0),
        name="pack",
    )(*arrays, *earlier)


def weight_kernel(places, minor, inputs, *refs):
    arrays, outs, total = refs[:inputs], refs[inputs:-1], refs[-1]
    half, piece, _ = outs[0].shape
    me = lax.axis_index("pool")
    result = None
    for array, row, grad_array, grad_row in places:
        term = f32_dot(arrays[array][row], arrays[grad_array][grad_row], ((0,), (0,)))
        result = term if result is None else result + term
    total[...] = result
    for at, out in enumerate(outs):
        near, start = at // 2, half * (1 - at % 2)
        for far in range(half):
            first = pl.multiple_of((me ^ ((start + far) * minor + near)) * piece, piece)
            out[far] = total[pl.ds(first, piece), :].astype(out.dtype)


def weight_grad(blocks, grads, members, minor):
    blocks, grads = sorted(blocks, key=lambda each: each[0]), sorted(grads, key=lambda each: each[0])
    arrays, which = distinct([array for _, array, _ in blocks + grads])
    parts = len(blocks)
    places = [(which[at], blocks[at][2], which[parts + at], grads[at][2]) for at in range(parts)]
    _, rows, cols = blocks[0][1].shape
    width = grads[0][1].shape[2]
    pieces = (members // minor // 2, cols // members, width)
    return pl.pallas_call(
        functools.partial(weight_kernel, places, minor, len(arrays)),
        out_shape=(jax.ShapeDtypeStruct(pieces, jnp.float32),) * 2
        + (jax.ShapeDtypeStruct(pieces, jnp.bfloat16),) * (2 * minor - 2),
        in_specs=[VMEM] * len(arrays),
        out_specs=(VMEM,) * (2 * minor),
        scratch_shapes=[pltpu.VMEM((cols, width), jnp.float32)],
        compiler_params=pltpu.CompilerParams(vmem_limit_bytes=VMEM_LIMIT),
        cost_estimate=pl.CostEstimate(
            flops=2 * parts * rows * cols * width, bytes_accessed=2 * parts * rows * cols, transcendentals=0
        ),
        name="weight_grad",
    )(*arrays)


def add_pieces_kernel(came, own_ref, *refs):
    for far, out in enumerate(refs[came:]):
        total = own_ref[far]
        for ref in refs[:came]:
            total = total + ref[far].astype(jnp.float32)
        out[...] = total.astype(out.dtype)


def add_pieces(own, came, first_type):
    majors, *piece = own.shape
    return pl.pallas_call(
        functools.partial(add_pieces_kernel, len(came)),
        out_shape=(jax.ShapeDtypeStruct(piece, first_type),)
        + (jax.ShapeDtypeStruct(piece, jnp.bfloat16),) * (majors - 1),
        in_specs=[VMEM] * (1 + len(came)),
        out_specs=(VMEM,) * majors,
        compiler_params=pltpu.CompilerParams(vmem_limit_bytes=SMALL_VMEM_LIMIT),
        cost_estimate=pl.CostEstimate(flops=own.size, bytes_accessed=8 * own.size, transcendentals=0),
        name="add_pieces",
    )(own, *came)


def add_all_kernel(*refs):
    total = refs[0][...].astype(jnp.float32)
    for ref in refs[1:-1]:
        total = total + ref[...].astype(jnp.float32)
    refs[-1][...] = total


def add_all(pieces):
    return pl.pallas_call(
        add_all_kernel,
        out_shape=jax.ShapeDtypeStruct(pieces[0].shape, jnp.float32),
        in_specs=[VMEM] * len(pieces),
        out_specs=VMEM,
        compiler_params=pltpu.CompilerParams(vmem_limit_bytes=SMALL_VMEM_LIMIT),
        name="add_all",
    )(*pieces)


def swap(value, axis, flip):
    size = lax.axis_size(axis)
    return lax.ppermute(value, axis, [(at, at ^ flip) for at in range(size)])


def order_kernel(value_ref, *refs):
    refs[-1][...] = value_ref[...]


def after(value, *earlier):
    return pl.pallas_call(
        order_kernel,
        out_shape=jax.ShapeDtypeStruct(value.shape, value.dtype),
        in_specs=[VMEM] * (1 + len(earlier)),
        out_specs=VMEM,
        compiler_params=pltpu.CompilerParams(vmem_limit_bytes=SMALL_VMEM_LIMIT),
        name="after",
    )(value, *earlier)


def per_device(feats, tower_w, partners, popularity_buckets, row_counts):
    members = lax.axis_size("pool")
    parts = lax.axis_size("dp")
    minor = 1 << ((members.bit_length() - 1) // 2)
    msg, normed, inv, near_cuts, far_cuts = project(feats, tower_w, partners[None, :], popularity_buckets[None, :], parts)

    majors = list(range(0, members, minor))
    last = members // 2
    msgs = {0: msg}
    msgs[last] = swap(msg, "pool", last)
    for k in majors[1:]:
        if k < last:
            msgs[k] = swap(msg, "pool", k)
    for near in range(1, minor):
        msgs[near] = swap(msg, "pool", near)
    for far in majors[1:-2]:
        for near in range(1, minor):
            msgs[far + near] = swap(msgs[far], "pool", near)
    relayed = msgs[last]
    for k in majors:
        if k > last:
            msgs[k] = swap(relayed, "pool", k ^ last)
    for near in range(1, minor):
        msgs[last + near] = swap(msgs[last], "pool", near)

    came = swap(far_cuts, "dp", parts // 2)

    state, kept, stages = (), [], []

    def add(fresh):
        nonlocal state
        *state, powers = add_pairs(sum(stages, []), fresh, row_counts, msgs, state)
        kept.append(powers)
        stages.append(fresh)

    add(majors[:-1] + list(range(1, minor)))
    add([far + near for far in majors[1:-2] for near in range(1, minor)])
    msgs3 = after(msgs[majors[-1]], state[1])
    for near in range(1, minor):
        msgs[majors[-1] + near] = swap(msgs3, "pool", near)
    add([majors[-1]])
    add([majors[-2] + near for near in range(1, minor)])
    bit = parts // 2
    blocks = {k: [(0, near_cuts, k), (bit, came, k)] for k in range(bit)}
    bit //= 2
    while bit:
        moving = [(k ^ bit, source ^ bit, array, at) for k in blocks if k & bit for source, array, at in blocks[k]]
        blocks = {k: blocks[k] for k in blocks if not k & bit}
        passed = swap(pack([each[2:] for each in moving], [state[1]]), "dp", bit)
        for at, (k, source, _, _) in enumerate(moving):
            blocks[k].append((source, passed, at))
        bit //= 2

    final = [majors[-1] + near for near in range(1, minor)]
    grad_proj = group_grad(stages, final, row_counts, msgs, state, kept, [], normed, inv)

    bit = parts // 2
    grads = [(0, grad_proj, 0)]
    while bit:
        sent = swap(grad_proj if len(grads) == 1 else pack([each[1:] for each in grads]), "dp", bit)
        grads += [(each[0] ^ bit, sent, at) for at, each in enumerate(grads)]
        bit //= 2

    own_far, own_near, *pieces = weight_grad(blocks[0], grads, members, minor)
    far_came = [swap(each, "pool", at + 1) for at, each in enumerate(pieces[0::2])]
    near_came = [swap(each, "pool", at + 1) for at, each in enumerate(pieces[1::2])]
    far_sums = add_pieces(own_far, far_came, jnp.bfloat16)
    total, *near_sums = add_pieces(own_near, near_came, jnp.float32)
    half = members // minor // 2
    far_came = [swap(each, "pool", (half + at) * minor) for at, each in enumerate(far_sums)]
    near_came = [swap(each, "pool", (1 + at) * minor) for at, each in enumerate(near_sums)]
    far_total = add_all(far_came)
    total = total + far_total
    for each in near_came:
        total = total + after(each, far_total).astype(jnp.float32)
    return total


def solution(mesh):
    return jax.shard_map(
        per_device,
        mesh=mesh,
        in_specs=(P(("dp", "pool"), None), P(), P(("dp", "pool")), P(("dp", "pool")), P()),
        out_specs=P(("dp", "pool"), None),
        check_vma=False,
    )
```

```python
import functools
import math

import jax
import jax.numpy as jnp
from jax import lax
from jax.experimental import pallas as pl
from jax.experimental.pallas import tpu as pltpu
from jax.sharding import PartitionSpec as P

sharpness_scaler = 0.05
epsilon = 1e-06
META = 16
DIGIT_BITS = 8
DIGIT = 1 << DIGIT_BITS
EXP2_SCALE = math.log2(math.e) / sharpness_scaler
LOG2E = math.log2(math.e)
VMEM_LIMIT = 40 * 1024 * 1024
SMALL_VMEM_LIMIT = 8 * 1024 * 1024

VMEM = pl.BlockSpec(memory_space=pltpu.VMEM)
SMEM = pl.BlockSpec(memory_space=pltpu.SMEM)
HBM = pl.BlockSpec(memory_space=pltpu.HBM)


def f32_dot(left, right, dims):
    return lax.dot_general(left, right, (dims, ((), ())), preferred_element_type=jnp.float32)


def column_of(row):
    return jnp.transpose(jnp.broadcast_to(row, (128, row.shape[1])))


def project_kernel(parts, feats_hbm, w_hbm, partners_hbm, buckets_hbm, msg_ref, normed_ref, inv_ref,
                   near_ref, far_ref, w_v, partners_ref, buckets_ref, sems, small_sems):
    half, rows, step = near_ref.shape
    cuts = [near_ref.at[k] for k in range(half)] + [far_ref.at[k] for k in range(half)]
    width = w_v.shape[1]
    me = lax.axis_index("dp")
    small = (
        pltpu.make_async_copy(partners_hbm, partners_ref, small_sems.at[0]),
        pltpu.make_async_copy(buckets_hbm, buckets_ref, small_sems.at[1]),
    )
    for copy in small:
        copy.start()
    copies = []
    for k in range(parts):
        first = pl.multiple_of((me ^ k) * step, step)
        cut = pl.ds(first, step)
        pair = (
            pltpu.make_async_copy(feats_hbm.at[:, cut], cuts[k], sems.at[0, k]),
            pltpu.make_async_copy(w_hbm.at[cut, :], w_v.at[pl.ds(k * step, step), :], sems.at[1, k]),
        )
        pair[0].start()
        pair[1].start()
        copies.append(pair)
    projected = jnp.zeros((rows, width), jnp.float32)
    for k in range(parts):
        copies[k][0].wait()
        copies[k][1].wait()
        projected = projected + f32_dot(cuts[k][...], w_v[pl.ds(k * step, step), :], ((1,), (0,)))
    for copy in small:
        copy.wait()
    partners = partners_ref[...]
    logq = -(buckets_ref[...].astype(jnp.float32) + 0.5) / 4.0
    high = (partners >> DIGIT_BITS).astype(jnp.float32)
    low = (partners & (DIGIT - 1)).astype(jnp.float32)
    kinds = lax.broadcasted_iota(jnp.int32, (META, rows), 0)
    meta = jnp.where(kinds == 0, logq, jnp.where(kinds == 1, high, jnp.where(kinds == 2, low, 0.0)))
    msg_ref[pl.ds(rows, META), :] = meta.astype(jnp.bfloat16)
    inv_norm = lax.rsqrt(jnp.sum(projected * projected, axis=1, keepdims=True) + epsilon)
    normed = projected * inv_norm
    normed_ref[...] = normed
    inv_ref[...] = jnp.broadcast_to(inv_norm, inv_ref.shape)
    msg_ref[pl.ds(0, rows), :] = normed.astype(jnp.bfloat16)


def project(feats, tower_w, partners, buckets, parts):
    rows, din = feats.shape
    width = tower_w.shape[1]
    return pl.pallas_call(
        functools.partial(project_kernel, parts),
        out_shape=(
            jax.ShapeDtypeStruct((rows + META, width), jnp.bfloat16),
            jax.ShapeDtypeStruct((rows, width), jnp.float32),
            jax.ShapeDtypeStruct((rows, 128), jnp.float32),
        )
        + (jax.ShapeDtypeStruct((parts // 2, rows, din // parts), feats.dtype),) * 2,
        in_specs=[HBM, HBM, HBM, HBM],
        out_specs=(VMEM,) * 5,
        scratch_shapes=[
            pltpu.VMEM((din, width), jnp.bfloat16),
            pltpu.VMEM((1, rows), jnp.int32),
            pltpu.VMEM((1, rows), jnp.int32),
            pltpu.SemaphoreType.DMA((2, parts)),
            pltpu.SemaphoreType.DMA((2,)),
        ],
        compiler_params=pltpu.CompilerParams(vmem_limit_bytes=VMEM_LIMIT),
        cost_estimate=pl.CostEstimate(
            flops=2 * rows * din * width, bytes_accessed=2 * din * (rows + width), transcendentals=rows
        ),
        name="project",
    )(*(pltpu.with_memory_space_constraint(each, pltpu.HBM) for each in (feats, tower_w, partners, buckets)))


def folded(terms):
    total = terms[:, 0:128]
    for at in range(128, terms.shape[1], 128):
        total = total + terms[:, at:at + 128]
    return total


def rows_to_lanes(sums):
    return jnp.sum(jnp.transpose(sums), axis=0, keepdims=True)


def weight_of(msg_ref, counts_ref, flip):
    rows = msg_ref.shape[0] - META
    meta = msg_ref[pl.ds(rows, META), :].astype(jnp.float32)
    lanes = lax.broadcasted_iota(jnp.int32, (1, rows), 1)
    valid = lanes < counts_ref[lax.axis_index("dp"), lax.axis_index("pool") ^ flip]
    return jnp.where(valid, jnp.exp2(meta[0:1] * -LOG2E), 0.0)


def pair_sums(seen, fresh, counts_ref, msgs, sums_ref, own_ref, sums_out, kept_at):
    rows = own_ref.shape[0] if own_ref is not None else msgs[0].shape[0] - META
    emb = {k: msgs[k][pl.ds(0, rows), :] for k in seen + fresh}
    weight = {k: weight_of(msgs[k], counts_ref, k) for k in seen + fresh}
    sums = {k: sums_ref[k] for k in seen if k}
    own_sums = own_ref[...] if own_ref is not None else jnp.zeros((rows, 128), jnp.float32)
    off_diagonal = lax.broadcasted_iota(jnp.int32, (rows, rows), 0) != lax.broadcasted_iota(
        jnp.int32, (rows, rows), 1
    )

    def powers_of(left, right):
        return jnp.exp2(f32_dot(emb[left], emb[right], ((1,), (1,))) * EXP2_SCALE)

    def down(powers, column):
        return jnp.sum(powers * column, axis=0, keepdims=True)

    own_column = column_of(weight[0])[:, 0:1]
    for k in fresh:
        powers = powers_of(0, k)
        if k == 0:
            powers = jnp.where(off_diagonal, powers, 0.0)
        else:
            sums[k] = down(powers, own_column)
        kept_at(k)[...] = powers
        own_sums = own_sums + folded(powers * weight[k])
    others = [k for k in seen if k]
    for k in fresh:
        if k == 0:
            continue
        column = column_of(weight[k])[:, 0:1]
        mine = folded(jnp.where(off_diagonal, powers_of(k, k), 0.0) * weight[k])
        for other in others:
            powers = powers_of(k, other)
            mine = mine + folded(powers * weight[other])
            sums[other] = sums[other] + down(powers, column)
        sums[k] = sums[k] + rows_to_lanes(mine)
        others.append(k)
    return sums, own_sums, weight, own_column


def pairs_kernel(seen, fresh, *refs):
    known = seen + fresh
    counts_ref, refs = refs[0], refs[1:]
    msgs, refs = dict(zip(known, refs)), refs[len(known):]
    before = {}
    own_ref = None
    if seen:
        sums_ref, own_ref, refs = refs[0], refs[1], refs[2:]
        before = {k: sums_ref[at:at + 1, :] for at, k in enumerate(seen)}
    sums_out, own_out, kept_out = refs
    sums, own_sums, _, _ = pair_sums(
        seen, fresh, counts_ref, msgs, before, own_ref, sums_out, lambda k: kept_out.at[fresh.index(k)]
    )
    own_out[...] = own_sums
    for at, k in enumerate(known):
        sums_out[at:at + 1, :] = sums[k] if k else jnp.zeros_like(sums_out[0:1, :])


def pairs_cost(seen, fresh, rows, width):
    pairs = len(fresh) * len(seen) + len(fresh) * (len(fresh) + 1) // 2
    return pl.CostEstimate(
        flops=2 * pairs * rows * rows * width,
        bytes_accessed=2 * (len(seen) + len(fresh)) * rows * width + 4 * len(fresh) * rows * rows,
        transcendentals=pairs * rows * rows,
    )


def add_pairs(seen, fresh, counts, msgs, state):
    known = seen + fresh
    rows, width = msgs[0].shape[0] - META, msgs[0].shape[1]
    return pl.pallas_call(
        functools.partial(pairs_kernel, seen, fresh),
        out_shape=(
            jax.ShapeDtypeStruct((len(known), rows), jnp.float32),
            jax.ShapeDtypeStruct((rows, 128), jnp.float32),
            jax.ShapeDtypeStruct((len(fresh), rows, rows), jnp.float32),
        ),
        in_specs=[SMEM] + [VMEM] * (len(known) + len(state)),
        out_specs=(VMEM,) * 3,
        compiler_params=pltpu.CompilerParams(vmem_limit_bytes=VMEM_LIMIT),
        cost_estimate=pairs_cost(seen, fresh, rows, width),
        name="add_pairs",
    )(counts, *(msgs[k] for k in known), *state)


def grad_kernel(stages, fresh, *refs):
    seen = [k for stage in stages for k in stage]
    known = seen + fresh
    counts_ref, refs = refs[0], refs[1:]
    msgs, refs = dict(zip(known, refs)), refs[len(known):]
    sums_ref, own_ref, refs = refs[0], refs[1], refs[2:]
    stage_refs, refs = refs[:len(stages)], refs[len(stages):]
    normed_ref, inv_ref, out_ref, kept = refs[-4:]
    rows, width = normed_ref.shape
    before = {k: sums_ref[at:at + 1, :] for at, k in enumerate(seen)}
    sums, own_sums, weight, own_weight = pair_sums(
        seen, fresh, counts_ref, msgs, before, own_ref, None, lambda k: kept.at[fresh.index(k)]
    )
    sums[0] = rows_to_lanes(own_sums)
    places = {k: kept.at[at] for at, k in enumerate(fresh)}
    for stage, ref in zip(stages, stage_refs):
        for at, k in enumerate(stage):
            places[k] = ref.at[at]

    me = lax.axis_index("pool")
    lanes = lax.broadcasted_iota(jnp.int32, (1, rows), 1)
    own_rows = me * rows + lax.broadcasted_iota(jnp.int32, (rows, 1), 0)

    def partner_of(k):
        meta = msgs[k][pl.ds(rows, META), :].astype(jnp.float32)
        return jnp.where(weight[k] > 0.0, meta[1:2] * DIGIT + meta[2:3], -1.0)

    recip = {k: jnp.where(weight[k] > 0.0, 1.0 / sums[k], 0.0) for k in known}
    own_recip = column_of(recip[0])[:, 0:1]
    own_partner = column_of(partner_of(0))[:, 0:1].astype(jnp.int32)
    both = jnp.zeros((2 * rows, width), jnp.float32)
    for k in known:
        columns = (me ^ k) * rows + lanes
        powers = places[k][...]
        along = powers * weight[k] * own_recip - jnp.where(own_partner == columns, 1.0, 0.0)
        across = powers * own_weight * recip[k] - jnp.where(
            partner_of(k).astype(jnp.int32) == own_rows, 1.0, 0.0
        )
        coefficients = jnp.concatenate([along.astype(jnp.bfloat16), across.astype(jnp.bfloat16)], axis=0)
        both = both + f32_dot(coefficients, msgs[k][pl.ds(0, rows), :], ((1,), (0,)))
    grad = both[:rows] + both[rows:]
    normed = normed_ref[...]
    inward = jnp.sum(normed * grad, axis=1, keepdims=True)
    out_ref[0] = ((grad - normed * inward) * inv_ref[:, 0:1]).astype(jnp.bfloat16)


def group_grad(stages, fresh, counts, msgs, state, kept, earlier, normed, inv):
    seen = [k for stage in stages for k in stage]
    known = seen + fresh
    rows, width = normed.shape
    return pl.pallas_call(
        functools.partial(grad_kernel, stages, fresh),
        out_shape=jax.ShapeDtypeStruct((1, rows, width), jnp.bfloat16),
        in_specs=[SMEM] + [VMEM] * (len(known) + len(state) + len(kept) + len(earlier) + 2),
        out_specs=VMEM,
        scratch_shapes=[pltpu.VMEM((len(fresh), rows, rows), jnp.float32)],
        compiler_params=pltpu.CompilerParams(vmem_limit_bytes=VMEM_LIMIT),
        cost_estimate=pairs_cost(seen, fresh, rows, width),
        name="group_grad",
    )(counts, *(msgs[k] for k in known), *state, *kept, *earlier, normed, inv)


def distinct(arrays):
    found = []
    for array in arrays:
        if all(array is not other for other in found):
            found.append(array)
    return found, [next(at for at, other in enumerate(found) if array is other) for array in arrays]


def pack_kernel(places, *refs):
    for at, (array, row) in enumerate(places):
        refs[-1][at] = refs[array][row]


def pack(pieces, earlier=()):
    arrays, which = distinct([array for array, _ in pieces])
    shape = (len(pieces),) + arrays[0].shape[1:]
    return pl.pallas_call(
        functools.partial(pack_kernel, [(at, piece[1]) for at, piece in zip(which, pieces)]),
        out_shape=jax.ShapeDtypeStruct(shape, arrays[0].dtype),
        in_specs=[VMEM] * (len(arrays) + len(earlier)),
        out_specs=VMEM,
        compiler_params=pltpu.CompilerParams(vmem_limit_bytes=VMEM_LIMIT),
        cost_estimate=pl.CostEstimate(flops=0, bytes_accessed=4 * math.prod(shape), transcendentals=0),
        name="pack",
    )(*arrays, *earlier)


def weight_kernel(places, minor, inputs, *refs):
    arrays, outs, total = refs[:inputs], refs[inputs:-1], refs[-1]
    half, piece, _ = outs[0].shape
    me = lax.axis_index("pool")
    result = None
    for array, row, grad_array, grad_row in places:
        term = f32_dot(arrays[array][row], arrays[grad_array][grad_row], ((0,), (0,)))
        result = term if result is None else result + term
    total[...] = result
    for at, out in enumerate(outs):
        near, start = at // 2, half * (1 - at % 2)
        for far in range(half):
            first = pl.multiple_of((me ^ ((start + far) * minor + near)) * piece, piece)
            out[far] = total[pl.ds(first, piece), :].astype(out.dtype)


def weight_grad(blocks, grads, members, minor):
    blocks, grads = sorted(blocks, key=lambda each: each[0]), sorted(grads, key=lambda each: each[0])
    arrays, which = distinct([array for _, array, _ in blocks + grads])
    parts = len(blocks)
    places = [(which[at], blocks[at][2], which[parts + at], grads[at][2]) for at in range(parts)]
    _, rows, cols = blocks[0][1].shape
    width = grads[0][1].shape[2]
    pieces = (members // minor // 2, cols // members, width)
    return pl.pallas_call(
        functools.partial(weight_kernel, places, minor, len(arrays)),
        out_shape=(jax.ShapeDtypeStruct(pieces, jnp.float32),) * 2
        + (jax.ShapeDtypeStruct(pieces, jnp.bfloat16),) * (2 * minor - 2),
        in_specs=[VMEM] * len(arrays),
        out_specs=(VMEM,) * (2 * minor),
        scratch_shapes=[pltpu.VMEM((cols, width), jnp.float32)],
        compiler_params=pltpu.CompilerParams(vmem_limit_bytes=VMEM_LIMIT),
        cost_estimate=pl.CostEstimate(
            flops=2 * parts * rows * cols * width, bytes_accessed=2 * parts * rows * cols, transcendentals=0
        ),
        name="weight_grad",
    )(*arrays)


def add_pieces_kernel(came, own_ref, *refs):
    for far, out in enumerate(refs[came:]):
        total = own_ref[far]
        for ref in refs[:came]:
            total = total + ref[far].astype(jnp.float32)
        out[...] = total.astype(out.dtype)


def add_pieces(own, came, first_type):
    majors, *piece = own.shape
    return pl.pallas_call(
        functools.partial(add_pieces_kernel, len(came)),
        out_shape=(jax.ShapeDtypeStruct(piece, first_type),)
        + (jax.ShapeDtypeStruct(piece, jnp.bfloat16),) * (majors - 1),
        in_specs=[VMEM] * (1 + len(came)),
        out_specs=(VMEM,) * majors,
        compiler_params=pltpu.CompilerParams(vmem_limit_bytes=SMALL_VMEM_LIMIT),
        cost_estimate=pl.CostEstimate(flops=own.size, bytes_accessed=8 * own.size, transcendentals=0),
        name="add_pieces",
    )(own, *came)


def add_all_kernel(*refs):
    total = refs[0][...].astype(jnp.float32)
    for ref in refs[1:-1]:
        total = total + ref[...].astype(jnp.float32)
    refs[-1][...] = total


def add_all(pieces):
    return pl.pallas_call(
        add_all_kernel,
        out_shape=jax.ShapeDtypeStruct(pieces[0].shape, jnp.float32),
        in_specs=[VMEM] * len(pieces),
        out_specs=VMEM,
        compiler_params=pltpu.CompilerParams(vmem_limit_bytes=SMALL_VMEM_LIMIT),
        name="add_all",
    )(*pieces)


def swap(value, axis, flip):
    size = lax.axis_size(axis)
    return lax.ppermute(value, axis, [(at, at ^ flip) for at in range(size)])


def order_kernel(value_ref, *refs):
    refs[-1][...] = value_ref[...]


def after(value, *earlier):
    return pl.pallas_call(
        order_kernel,
        out_shape=jax.ShapeDtypeStruct(value.shape, value.dtype),
        in_specs=[VMEM] * (1 + len(earlier)),
        out_specs=VMEM,
        compiler_params=pltpu.CompilerParams(vmem_limit_bytes=SMALL_VMEM_LIMIT),
        name="after",
    )(value, *earlier)


def per_device(feats, tower_w, partners, popularity_buckets, row_counts):
    members = lax.axis_size("pool")
    parts = lax.axis_size("dp")
    minor = 1 << ((members.bit_length() - 1) // 2)
    msg, normed, inv, near_cuts, far_cuts = project(feats, tower_w, partners[None, :], popularity_buckets[None, :], parts)

    majors = list(range(0, members, minor))
    last = members // 2
    msgs = {0: msg}
    msgs[last] = swap(msg, "pool", last)
    for k in majors[1:]:
        if k < last:
            msgs[k] = swap(msg, "pool", k)
    for near in range(1, minor):
        msgs[near] = swap(msg, "pool", near)
    for far in majors[1:-2]:
        for near in range(1, minor):
            msgs[far + near] = swap(msgs[far], "pool", near)
    relayed = msgs[last]
    for k in majors:
        if k > last:
            msgs[k] = swap(relayed, "pool", k ^ last)
    for near in range(1, minor):
        msgs[last + near] = swap(msgs[last], "pool", near)

    came = swap(far_cuts, "dp", parts // 2)

    state, kept, stages = (), [], []

    def add(fresh):
        nonlocal state
        *state, powers = add_pairs(sum(stages, []), fresh, row_counts, msgs, state)
        kept.append(powers)
        stages.append(fresh)

    add(majors[:-1] + list(range(1, minor)))
    add([far + near for far in majors[1:-2] for near in range(1, minor)])
    msgs3 = after(msgs[majors[-1]], state[1])
    for near in range(1, minor):
        msgs[majors[-1] + near] = swap(msgs3, "pool", near)
    add([majors[-1]])
    add([majors[-2] + near for near in range(1, minor)])
    bit = parts // 2
    blocks = {k: [(0, near_cuts, k), (bit, came, k)] for k in range(bit)}
    bit //= 2
    while bit:
        moving = [(k ^ bit, source ^ bit, array, at) for k in blocks if k & bit for source, array, at in blocks[k]]
        blocks = {k: blocks[k] for k in blocks if not k & bit}
        passed = swap(pack([each[2:] for each in moving], [state[1]]), "dp", bit)
        for at, (k, source, _, _) in enumerate(moving):
            blocks[k].append((source, passed, at))
        bit //= 2

    final = [majors[-1] + near for near in range(1, minor)]
    grad_proj = group_grad(stages, final, row_counts, msgs, state, kept, [], normed, inv)

    bit = parts // 2
    grads = [(0, grad_proj, 0)]
    while bit:
        sent = swap(grad_proj if len(grads) == 1 else pack([each[1:] for each in grads]), "dp", bit)
        grads += [(each[0] ^ bit, sent, at) for at, each in enumerate(grads)]
        bit //= 2

    own_far, own_near, *pieces = weight_grad(blocks[0], grads, members, minor)
    far_came = [swap(each, "pool", at + 1) for at, each in enumerate(pieces[0::2])]
    near_came = [swap(after(each, *far_came), "pool", at + 1) for at, each in enumerate(pieces[1::2])]
    far_sums = add_pieces(own_far, far_came, jnp.bfloat16)
    total, *near_sums = add_pieces(own_near, near_came, jnp.float32)
    half = members // minor // 2
    far_came = [swap(each, "pool", (half + at) * minor) for at, each in enumerate(far_sums)]
    near_came = [swap(each, "pool", (1 + at) * minor) for at, each in enumerate(near_sums)]
    far_total = add_all(far_came)
    total = total + far_total
    for each in near_came:
        total = total + after(each, far_total).astype(jnp.float32)
    return total


def solution(mesh):
    return jax.shard_map(
        per_device,
        mesh=mesh,
        in_specs=(P(("dp", "pool"), None), P(), P(("dp", "pool")), P(("dp", "pool")), P()),
        out_specs=P(("dp", "pool"), None),
        check_vma=False,
    )
```

```python
import functools
import math

import jax
import jax.numpy as jnp
from jax import lax
from jax.experimental import pallas as pl
from jax.experimental.pallas import tpu as pltpu
from jax.sharding import PartitionSpec as P

sharpness_scaler = 0.05
epsilon = 1e-06
META = 16
DIGIT_BITS = 8
DIGIT = 1 << DIGIT_BITS
EXP2_SCALE = math.log2(math.e) / sharpness_scaler
LOG2E = math.log2(math.e)
VMEM_LIMIT = 40 * 1024 * 1024
SMALL_VMEM_LIMIT = 8 * 1024 * 1024

VMEM = pl.BlockSpec(memory_space=pltpu.VMEM)
SMEM = pl.BlockSpec(memory_space=pltpu.SMEM)
HBM = pl.BlockSpec(memory_space=pltpu.HBM)


def f32_dot(left, right, dims):
    return lax.dot_general(left, right, (dims, ((), ())), preferred_element_type=jnp.float32)


def column_of(row):
    return jnp.transpose(jnp.broadcast_to(row, (128, row.shape[1])))


def project_kernel(parts, feats_hbm, w_hbm, partners_hbm, buckets_hbm, msg_ref, normed_ref, inv_ref,
                   near_ref, far_ref, w_v, partners_ref, buckets_ref, sems, small_sems):
    half, rows, step = near_ref.shape
    cuts = [near_ref.at[k] for k in range(half)] + [far_ref.at[k] for k in range(half)]
    width = w_v.shape[1]
    me = lax.axis_index("dp")
    small = (
        pltpu.make_async_copy(partners_hbm, partners_ref, small_sems.at[0]),
        pltpu.make_async_copy(buckets_hbm, buckets_ref, small_sems.at[1]),
    )
    for copy in small:
        copy.start()
    copies = []
    for k in range(parts):
        first = pl.multiple_of((me ^ k) * step, step)
        cut = pl.ds(first, step)
        pair = (
            pltpu.make_async_copy(feats_hbm.at[:, cut], cuts[k], sems.at[0, k]),
            pltpu.make_async_copy(w_hbm.at[cut, :], w_v.at[pl.ds(k * step, step), :], sems.at[1, k]),
        )
        pair[0].start()
        pair[1].start()
        copies.append(pair)
    projected = jnp.zeros((rows, width), jnp.float32)
    for k in range(parts):
        copies[k][0].wait()
        copies[k][1].wait()
        projected = projected + f32_dot(cuts[k][...], w_v[pl.ds(k * step, step), :], ((1,), (0,)))
    for copy in small:
        copy.wait()
    partners = partners_ref[...]
    logq = -(buckets_ref[...].astype(jnp.float32) + 0.5) / 4.0
    high = (partners >> DIGIT_BITS).astype(jnp.float32)
    low = (partners & (DIGIT - 1)).astype(jnp.float32)
    kinds = lax.broadcasted_iota(jnp.int32, (META, rows), 0)
    meta = jnp.where(kinds == 0, logq, jnp.where(kinds == 1, high, jnp.where(kinds == 2, low, 0.0)))
    msg_ref[pl.ds(rows, META), :] = meta.astype(jnp.bfloat16)
    inv_norm = lax.rsqrt(jnp.sum(projected * projected, axis=1, keepdims=True) + epsilon)
    normed = projected * inv_norm
    normed_ref[...] = normed
    inv_ref[...] = jnp.broadcast_to(inv_norm, inv_ref.shape)
    msg_ref[pl.ds(0, rows), :] = normed.astype(jnp.bfloat16)


def project(feats, tower_w, partners, buckets, parts):
    rows, din = feats.shape
    width = tower_w.shape[1]
    return pl.pallas_call(
        functools.partial(project_kernel, parts),
        out_shape=(
            jax.ShapeDtypeStruct((rows + META, width), jnp.bfloat16),
            jax.ShapeDtypeStruct((rows, width), jnp.float32),
            jax.ShapeDtypeStruct((rows, 128), jnp.float32),
        )
        + (jax.ShapeDtypeStruct((parts // 2, rows, din // parts), feats.dtype),) * 2,
        in_specs=[HBM, HBM, HBM, HBM],
        out_specs=(VMEM,) * 5,
        scratch_shapes=[
            pltpu.VMEM((din, width), jnp.bfloat16),
            pltpu.VMEM((1, rows), jnp.int32),
            pltpu.VMEM((1, rows), jnp.int32),
            pltpu.SemaphoreType.DMA((2, parts)),
            pltpu.SemaphoreType.DMA((2,)),
        ],
        compiler_params=pltpu.CompilerParams(vmem_limit_bytes=VMEM_LIMIT),
        cost_estimate=pl.CostEstimate(
            flops=2 * rows * din * width, bytes_accessed=2 * din * (rows + width), transcendentals=rows
        ),
        name="project",
    )(*(pltpu.with_memory_space_constraint(each, pltpu.HBM) for each in (feats, tower_w, partners, buckets)))


def folded(terms):
    total = terms[:, 0:128]
    for at in range(128, terms.shape[1], 128):
        total = total + terms[:, at:at + 128]
    return total


def rows_to_lanes(sums):
    return jnp.sum(jnp.transpose(sums), axis=0, keepdims=True)


def weight_of(msg_ref, counts_ref, flip):
    rows = msg_ref.shape[0] - META
    meta = msg_ref[pl.ds(rows, META), :].astype(jnp.float32)
    lanes = lax.broadcasted_iota(jnp.int32, (1, rows), 1)
    valid = lanes < counts_ref[lax.axis_index("dp"), lax.axis_index("pool") ^ flip]
    return jnp.where(valid, jnp.exp2(meta[0:1] * -LOG2E), 0.0)


def pair_sums(seen, fresh, counts_ref, msgs, sums_ref, own_ref, sums_out, kept_at):
    rows = own_ref.shape[0] if own_ref is not None else msgs[0].shape[0] - META
    emb = {k: msgs[k][pl.ds(0, rows), :] for k in seen + fresh}
    weight = {k: weight_of(msgs[k], counts_ref, k) for k in seen + fresh}
    sums = {k: sums_ref[k] for k in seen if k}
    own_sums = own_ref[...] if own_ref is not None else jnp.zeros((rows, 128), jnp.float32)
    off_diagonal = lax.broadcasted_iota(jnp.int32, (rows, rows), 0) != lax.broadcasted_iota(
        jnp.int32, (rows, rows), 1
    )

    def powers_of(left, right):
        return jnp.exp2(f32_dot(emb[left], emb[right], ((1,), (1,))) * EXP2_SCALE)

    def down(powers, column):
        return jnp.sum(powers * column, axis=0, keepdims=True)

    own_column = column_of(weight[0])[:, 0:1]
    for k in fresh:
        powers = powers_of(0, k)
        if k == 0:
            powers = jnp.where(off_diagonal, powers, 0.0)
        else:
            sums[k] = down(powers, own_column)
        kept_at(k)[...] = powers
        own_sums = own_sums + folded(powers * weight[k])
    others = [k for k in seen if k]
    for k in fresh:
        if k == 0:
            continue
        column = column_of(weight[k])[:, 0:1]
        mine = folded(jnp.where(off_diagonal, powers_of(k, k), 0.0) * weight[k])
        for other in others:
            powers = powers_of(k, other)
            mine = mine + folded(powers * weight[other])
            sums[other] = sums[other] + down(powers, column)
        sums[k] = sums[k] + rows_to_lanes(mine)
        others.append(k)
    return sums, own_sums, weight, own_column


def pairs_kernel(seen, fresh, *refs):
    known = seen + fresh
    counts_ref, refs = refs[0], refs[1:]
    msgs, refs = dict(zip(known, refs)), refs[len(known):]
    before = {}
    own_ref = None
    if seen:
        sums_ref, own_ref, refs = refs[0], refs[1], refs[2:]
        before = {k: sums_ref[at:at + 1, :] for at, k in enumerate(seen)}
    sums_out, own_out, kept_out = refs
    sums, own_sums, _, _ = pair_sums(
        seen, fresh, counts_ref, msgs, before, own_ref, sums_out, lambda k: kept_out.at[fresh.index(k)]
    )
    own_out[...] = own_sums
    for at, k in enumerate(known):
        sums_out[at:at + 1, :] = sums[k] if k else jnp.zeros_like(sums_out[0:1, :])


def pairs_cost(seen, fresh, rows, width):
    pairs = len(fresh) * len(seen) + len(fresh) * (len(fresh) + 1) // 2
    return pl.CostEstimate(
        flops=2 * pairs * rows * rows * width,
        bytes_accessed=2 * (len(seen) + len(fresh)) * rows * width + 4 * len(fresh) * rows * rows,
        transcendentals=pairs * rows * rows,
    )


def add_pairs(seen, fresh, counts, msgs, state):
    known = seen + fresh
    rows, width = msgs[0].shape[0] - META, msgs[0].shape[1]
    return pl.pallas_call(
        functools.partial(pairs_kernel, seen, fresh),
        out_shape=(
            jax.ShapeDtypeStruct((len(known), rows), jnp.float32),
            jax.ShapeDtypeStruct((rows, 128), jnp.float32),
            jax.ShapeDtypeStruct((len(fresh), rows, rows), jnp.float32),
        ),
        in_specs=[SMEM] + [VMEM] * (len(known) + len(state)),
        out_specs=(VMEM,) * 3,
        compiler_params=pltpu.CompilerParams(vmem_limit_bytes=VMEM_LIMIT),
        cost_estimate=pairs_cost(seen, fresh, rows, width),
        name="add_pairs",
    )(counts, *(msgs[k] for k in known), *state)


def grad_kernel(stages, fresh, *refs):
    seen = [k for stage in stages for k in stage]
    known = seen + fresh
    counts_ref, refs = refs[0], refs[1:]
    msgs, refs = dict(zip(known, refs)), refs[len(known):]
    sums_ref, own_ref, refs = refs[0], refs[1], refs[2:]
    stage_refs, refs = refs[:len(stages)], refs[len(stages):]
    normed_ref, inv_ref, out_ref, kept = refs[-4:]
    rows, width = normed_ref.shape
    before = {k: sums_ref[at:at + 1, :] for at, k in enumerate(seen)}
    sums, own_sums, weight, own_weight = pair_sums(
        seen, fresh, counts_ref, msgs, before, own_ref, None, lambda k: kept.at[fresh.index(k)]
    )
    sums[0] = rows_to_lanes(own_sums)
    places = {k: kept.at[at] for at, k in enumerate(fresh)}
    for stage, ref in zip(stages, stage_refs):
        for at, k in enumerate(stage):
            places[k] = ref.at[at]

    me = lax.axis_index("pool")
    lanes = lax.broadcasted_iota(jnp.int32, (1, rows), 1)
    own_rows = me * rows + lax.broadcasted_iota(jnp.int32, (rows, 1), 0)

    def partner_of(k):
        meta = msgs[k][pl.ds(rows, META), :].astype(jnp.float32)
        return jnp.where(weight[k] > 0.0, meta[1:2] * DIGIT + meta[2:3], -1.0)

    recip = {k: jnp.where(weight[k] > 0.0, 1.0 / sums[k], 0.0) for k in known}
    own_recip = column_of(recip[0])[:, 0:1]
    own_partner = column_of(partner_of(0))[:, 0:1].astype(jnp.int32)
    both = jnp.zeros((2 * rows, width), jnp.float32)
    for k in known:
        columns = (me ^ k) * rows + lanes
        powers = places[k][...]
        along = powers * weight[k] * own_recip - jnp.where(own_partner == columns, 1.0, 0.0)
        across = powers * own_weight * recip[k] - jnp.where(
            partner_of(k).astype(jnp.int32) == own_rows, 1.0, 0.0
        )
        coefficients = jnp.concatenate([along.astype(jnp.bfloat16), across.astype(jnp.bfloat16)], axis=0)
        both = both + f32_dot(coefficients, msgs[k][pl.ds(0, rows), :], ((1,), (0,)))
    grad = both[:rows] + both[rows:]
    normed = normed_ref[...]
    inward = jnp.sum(normed * grad, axis=1, keepdims=True)
    out_ref[0] = ((grad - normed * inward) * inv_ref[:, 0:1]).astype(jnp.bfloat16)


def group_grad(stages, fresh, counts, msgs, state, kept, earlier, normed, inv):
    seen = [k for stage in stages for k in stage]
    known = seen + fresh
    rows, width = normed.shape
    return pl.pallas_call(
        functools.partial(grad_kernel, stages, fresh),
        out_shape=jax.ShapeDtypeStruct((1, rows, width), jnp.bfloat16),
        in_specs=[SMEM] + [VMEM] * (len(known) + len(state) + len(kept) + len(earlier) + 2),
        out_specs=VMEM,
        scratch_shapes=[pltpu.VMEM((len(fresh), rows, rows), jnp.float32)],
        compiler_params=pltpu.CompilerParams(vmem_limit_bytes=VMEM_LIMIT),
        cost_estimate=pairs_cost(seen, fresh, rows, width),
        name="group_grad",
    )(counts, *(msgs[k] for k in known), *state, *kept, *earlier, normed, inv)


def distinct(arrays):
    found = []
    for array in arrays:
        if all(array is not other for other in found):
            found.append(array)
    return found, [next(at for at, other in enumerate(found) if array is other) for array in arrays]


def pack_kernel(places, *refs):
    for at, (array, row) in enumerate(places):
        refs[-1][at] = refs[array][row]


def pack(pieces, earlier=()):
    arrays, which = distinct([array for array, _ in pieces])
    shape = (len(pieces),) + arrays[0].shape[1:]
    return pl.pallas_call(
        functools.partial(pack_kernel, [(at, piece[1]) for at, piece in zip(which, pieces)]),
        out_shape=jax.ShapeDtypeStruct(shape, arrays[0].dtype),
        in_specs=[VMEM] * (len(arrays) + len(earlier)),
        out_specs=VMEM,
        compiler_params=pltpu.CompilerParams(vmem_limit_bytes=VMEM_LIMIT),
        cost_estimate=pl.CostEstimate(flops=0, bytes_accessed=4 * math.prod(shape), transcendentals=0),
        name="pack",
    )(*arrays, *earlier)


def weight_kernel(places, minor, inputs, *refs):
    arrays, outs, total = refs[:inputs], refs[inputs:-1], refs[-1]
    half, piece, _ = outs[0].shape
    me = lax.axis_index("pool")
    result = None
    for array, row, grad_array, grad_row in places:
        term = f32_dot(arrays[array][row], arrays[grad_array][grad_row], ((0,), (0,)))
        result = term if result is None else result + term
    total[...] = result
    for at, out in enumerate(outs):
        near, start = at // 2, half * (1 - at % 2)
        for far in range(half):
            first = pl.multiple_of((me ^ ((start + far) * minor + near)) * piece, piece)
            out[far] = total[pl.ds(first, piece), :].astype(out.dtype)


def weight_grad(blocks, grads, members, minor):
    blocks, grads = sorted(blocks, key=lambda each: each[0]), sorted(grads, key=lambda each: each[0])
    arrays, which = distinct([array for _, array, _ in blocks + grads])
    parts = len(blocks)
    places = [(which[at], blocks[at][2], which[parts + at], grads[at][2]) for at in range(parts)]
    _, rows, cols = blocks[0][1].shape
    width = grads[0][1].shape[2]
    pieces = (members // minor // 2, cols // members, width)
    return pl.pallas_call(
        functools.partial(weight_kernel, places, minor, len(arrays)),
        out_shape=(jax.ShapeDtypeStruct(pieces, jnp.float32),) * 2
        + (jax.ShapeDtypeStruct(pieces, jnp.bfloat16),) * (2 * minor - 2),
        in_specs=[VMEM] * len(arrays),
        out_specs=(VMEM,) * (2 * minor),
        scratch_shapes=[pltpu.VMEM((cols, width), jnp.float32)],
        compiler_params=pltpu.CompilerParams(vmem_limit_bytes=VMEM_LIMIT),
        cost_estimate=pl.CostEstimate(
            flops=2 * parts * rows * cols * width, bytes_accessed=2 * parts * rows * cols, transcendentals=0
        ),
        name="weight_grad",
    )(*arrays)


def add_pieces_kernel(came, own_ref, *refs):
    for far, out in enumerate(refs[came:]):
        total = own_ref[far]
        for ref in refs[:came]:
            total = total + ref[far].astype(jnp.float32)
        out[...] = total.astype(out.dtype)


def add_pieces(own, came, first_type):
    majors, *piece = own.shape
    return pl.pallas_call(
        functools.partial(add_pieces_kernel, len(came)),
        out_shape=(jax.ShapeDtypeStruct(piece, first_type),)
        + (jax.ShapeDtypeStruct(piece, jnp.bfloat16),) * (majors - 1),
        in_specs=[VMEM] * (1 + len(came)),
        out_specs=(VMEM,) * majors,
        compiler_params=pltpu.CompilerParams(vmem_limit_bytes=SMALL_VMEM_LIMIT),
        cost_estimate=pl.CostEstimate(flops=own.size, bytes_accessed=8 * own.size, transcendentals=0),
        name="add_pieces",
    )(own, *came)


def add_all_kernel(*refs):
    total = refs[0][...].astype(jnp.float32)
    for ref in refs[1:-1]:
        total = total + ref[...].astype(jnp.float32)
    refs[-1][...] = total


def add_all(pieces):
    return pl.pallas_call(
        add_all_kernel,
        out_shape=jax.ShapeDtypeStruct(pieces[0].shape, jnp.float32),
        in_specs=[VMEM] * len(pieces),
        out_specs=VMEM,
        compiler_params=pltpu.CompilerParams(vmem_limit_bytes=SMALL_VMEM_LIMIT),
        name="add_all",
    )(*pieces)


def swap(value, axis, flip):
    size = lax.axis_size(axis)
    return lax.ppermute(value, axis, [(at, at ^ flip) for at in range(size)])


def order_kernel(value_ref, *refs):
    refs[-1][...] = value_ref[...]


def after(value, *earlier):
    return pl.pallas_call(
        order_kernel,
        out_shape=jax.ShapeDtypeStruct(value.shape, value.dtype),
        in_specs=[VMEM] * (1 + len(earlier)),
        out_specs=VMEM,
        compiler_params=pltpu.CompilerParams(vmem_limit_bytes=SMALL_VMEM_LIMIT),
        name="after",
    )(value, *earlier)


def per_device(feats, tower_w, partners, popularity_buckets, row_counts):
    members = lax.axis_size("pool")
    parts = lax.axis_size("dp")
    minor = 1 << ((members.bit_length() - 1) // 2)
    msg, normed, inv, near_cuts, far_cuts = project(feats, tower_w, partners[None, :], popularity_buckets[None, :], parts)

    majors = list(range(0, members, minor))
    last = members // 2
    msgs = {0: msg}
    msgs[last] = swap(msg, "pool", last)
    for k in majors[1:]:
        if k < last:
            msgs[k] = swap(msg, "pool", k)
    for near in range(1, minor):
        msgs[near] = swap(msg, "pool", near)
    for far in majors[1:-2]:
        for near in range(1, minor):
            msgs[far + near] = swap(msgs[far], "pool", near)
    relayed = msgs[last]
    for k in majors:
        if k > last:
            msgs[k] = swap(relayed, "pool", k ^ last)
    for near in range(1, minor):
        msgs[last + near] = swap(msgs[last], "pool", near)

    came = swap(far_cuts, "dp", parts // 2)

    state, kept, stages = (), [], []

    def add(fresh):
        nonlocal state
        *state, powers = add_pairs(sum(stages, []), fresh, row_counts, msgs, state)
        kept.append(powers)
        stages.append(fresh)

    add(majors[:-1] + list(range(1, minor)))
    for near in range(1, minor):
        msgs[majors[-1] + near] = swap(msgs[majors[-1]], "pool", near)
    add([far + near for far in majors[1:-2] for near in range(1, minor)] + [majors[-1]])
    add([majors[-2] + near for near in range(1, minor)])
    bit = parts // 2
    blocks = {k: [(0, near_cuts, k), (bit, came, k)] for k in range(bit)}
    bit //= 2
    while bit:
        moving = [(k ^ bit, source ^ bit, array, at) for k in blocks if k & bit for source, array, at in blocks[k]]
        blocks = {k: blocks[k] for k in blocks if not k & bit}
        passed = swap(pack([each[2:] for each in moving], [state[1]]), "dp", bit)
        for at, (k, source, _, _) in enumerate(moving):
            blocks[k].append((source, passed, at))
        bit //= 2

    final = [majors[-1] + near for near in range(1, minor)]
    grad_proj = group_grad(stages, final, row_counts, msgs, state, kept, [], normed, inv)

    bit = parts // 2
    grads = [(0, grad_proj, 0)]
    while bit:
        sent = swap(grad_proj if len(grads) == 1 else pack([each[1:] for each in grads]), "dp", bit)
        grads += [(each[0] ^ bit, sent, at) for at, each in enumerate(grads)]
        bit //= 2

    own_far, own_near, *pieces = weight_grad(blocks[0], grads, members, minor)
    far_came = [swap(each, "pool", at + 1) for at, each in enumerate(pieces[0::2])]
    near_came = [swap(each, "pool", at + 1) for at, each in enumerate(pieces[1::2])]
    far_sums = add_pieces(own_far, far_came, jnp.bfloat16)
    total, *near_sums = add_pieces(own_near, near_came, jnp.float32)
    half = members // minor // 2
    far_came = [swap(each, "pool", (half + at) * minor) for at, each in enumerate(far_sums)]
    near_came = [swap(each, "pool", (1 + at) * minor) for at, each in enumerate(near_sums)]
    far_total = add_all(far_came)
    total = total + far_total
    for each in near_came:
        total = total + after(each, far_total).astype(jnp.float32)
    return total


def solution(mesh):
    return jax.shard_map(
        per_device,
        mesh=mesh,
        in_specs=(P(("dp", "pool"), None), P(), P(("dp", "pool")), P(("dp", "pool")), P()),
        out_specs=P(("dp", "pool"), None),
        check_vma=False,
    )
```

```python
import functools
import math

import jax
import jax.numpy as jnp
from jax import lax
from jax.experimental import pallas as pl
from jax.experimental.pallas import tpu as pltpu
from jax.sharding import PartitionSpec as P

sharpness_scaler = 0.05
epsilon = 1e-06
META = 16
DIGIT_BITS = 8
DIGIT = 1 << DIGIT_BITS
EXP2_SCALE = math.log2(math.e) / sharpness_scaler
LOG2E = math.log2(math.e)
VMEM_LIMIT = 40 * 1024 * 1024
SMALL_VMEM_LIMIT = 8 * 1024 * 1024

VMEM = pl.BlockSpec(memory_space=pltpu.VMEM)
SMEM = pl.BlockSpec(memory_space=pltpu.SMEM)
HBM = pl.BlockSpec(memory_space=pltpu.HBM)


def f32_dot(left, right, dims):
    return lax.dot_general(left, right, (dims, ((), ())), preferred_element_type=jnp.float32)


def column_of(row):
    return jnp.transpose(jnp.broadcast_to(row, (128, row.shape[1])))


def project_kernel(parts, feats_hbm, w_hbm, partners_hbm, buckets_hbm, msg_ref, normed_ref, inv_ref,
                   near_ref, far_ref, w_v, partners_ref, buckets_ref, sems, small_sems):
    half, rows, step = near_ref.shape
    cuts = [near_ref.at[k] for k in range(half)] + [far_ref.at[k] for k in range(half)]
    width = w_v.shape[1]
    me = lax.axis_index("dp")
    small = (
        pltpu.make_async_copy(partners_hbm, partners_ref, small_sems.at[0]),
        pltpu.make_async_copy(buckets_hbm, buckets_ref, small_sems.at[1]),
    )
    for copy in small:
        copy.start()
    copies = []
    for k in range(parts):
        first = pl.multiple_of((me ^ k) * step, step)
        cut = pl.ds(first, step)
        pair = (
            pltpu.make_async_copy(feats_hbm.at[:, cut], cuts[k], sems.at[0, k]),
            pltpu.make_async_copy(w_hbm.at[cut, :], w_v.at[pl.ds(k * step, step), :], sems.at[1, k]),
        )
        pair[0].start()
        pair[1].start()
        copies.append(pair)
    projected = jnp.zeros((rows, width), jnp.float32)
    for k in range(parts):
        copies[k][0].wait()
        copies[k][1].wait()
        projected = projected + f32_dot(cuts[k][...], w_v[pl.ds(k * step, step), :], ((1,), (0,)))
    for copy in small:
        copy.wait()
    partners = partners_ref[...]
    logq = -(buckets_ref[...].astype(jnp.float32) + 0.5) / 4.0
    high = (partners >> DIGIT_BITS).astype(jnp.float32)
    low = (partners & (DIGIT - 1)).astype(jnp.float32)
    kinds = lax.broadcasted_iota(jnp.int32, (META, rows), 0)
    meta = jnp.where(kinds == 0, logq, jnp.where(kinds == 1, high, jnp.where(kinds == 2, low, 0.0)))
    msg_ref[pl.ds(rows, META), :] = meta.astype(jnp.bfloat16)
    inv_norm = lax.rsqrt(jnp.sum(projected * projected, axis=1, keepdims=True) + epsilon)
    normed = projected * inv_norm
    normed_ref[...] = normed
    inv_ref[...] = jnp.broadcast_to(inv_norm, inv_ref.shape)
    msg_ref[pl.ds(0, rows), :] = normed.astype(jnp.bfloat16)


def project(feats, tower_w, partners, buckets, parts):
    rows, din = feats.shape
    width = tower_w.shape[1]
    return pl.pallas_call(
        functools.partial(project_kernel, parts),
        out_shape=(
            jax.ShapeDtypeStruct((rows + META, width), jnp.bfloat16),
            jax.ShapeDtypeStruct((rows, width), jnp.float32),
            jax.ShapeDtypeStruct((rows, 128), jnp.float32),
        )
        + (jax.ShapeDtypeStruct((parts // 2, rows, din // parts), feats.dtype),) * 2,
        in_specs=[HBM, HBM, HBM, HBM],
        out_specs=(VMEM,) * 5,
        scratch_shapes=[
            pltpu.VMEM((din, width), jnp.bfloat16),
            pltpu.VMEM((1, rows), jnp.int32),
            pltpu.VMEM((1, rows), jnp.int32),
            pltpu.SemaphoreType.DMA((2, parts)),
            pltpu.SemaphoreType.DMA((2,)),
        ],
        compiler_params=pltpu.CompilerParams(vmem_limit_bytes=VMEM_LIMIT),
        cost_estimate=pl.CostEstimate(
            flops=2 * rows * din * width, bytes_accessed=2 * din * (rows + width), transcendentals=rows
        ),
        name="project",
    )(*(pltpu.with_memory_space_constraint(each, pltpu.HBM) for each in (feats, tower_w, partners, buckets)))


def folded(terms):
    total = terms[:, 0:128]
    for at in range(128, terms.shape[1], 128):
        total = total + terms[:, at:at + 128]
    return total


def rows_to_lanes(sums):
    return jnp.sum(jnp.transpose(sums), axis=0, keepdims=True)


def weight_of(msg_ref, counts_ref, flip):
    rows = msg_ref.shape[0] - META
    meta = msg_ref[pl.ds(rows, META), :].astype(jnp.float32)
    lanes = lax.broadcasted_iota(jnp.int32, (1, rows), 1)
    valid = lanes < counts_ref[lax.axis_index("dp"), lax.axis_index("pool") ^ flip]
    return jnp.where(valid, jnp.exp2(meta[0:1] * -LOG2E), 0.0)


def pair_sums(seen, fresh, counts_ref, msgs, sums_ref, own_ref, sums_out, kept_at):
    rows = own_ref.shape[0] if own_ref is not None else msgs[0].shape[0] - META
    emb = {k: msgs[k][pl.ds(0, rows), :] for k in seen + fresh}
    weight = {k: weight_of(msgs[k], counts_ref, k) for k in seen + fresh}
    sums = {k: sums_ref[k] for k in seen if k}
    own_sums = own_ref[...] if own_ref is not None else jnp.zeros((rows, 128), jnp.float32)
    off_diagonal = lax.broadcasted_iota(jnp.int32, (rows, rows), 0) != lax.broadcasted_iota(
        jnp.int32, (rows, rows), 1
    )

    def powers_of(left, right):
        return jnp.exp2(f32_dot(emb[left], emb[right], ((1,), (1,))) * EXP2_SCALE)

    def down(powers, column):
        return jnp.sum(powers * column, axis=0, keepdims=True)

    own_column = column_of(weight[0])[:, 0:1]
    for k in fresh:
        powers = powers_of(0, k)
        if k == 0:
            powers = jnp.where(off_diagonal, powers, 0.0)
        else:
            sums[k] = down(powers, own_column)
        kept_at(k)[...] = powers
        own_sums = own_sums + folded(powers * weight[k])
    others = [k for k in seen if k]
    for k in fresh:
        if k == 0:
            continue
        column = column_of(weight[k])[:, 0:1]
        mine = folded(jnp.where(off_diagonal, powers_of(k, k), 0.0) * weight[k])
        for other in others:
            powers = powers_of(k, other)
            mine = mine + folded(powers * weight[other])
            sums[other] = sums[other] + down(powers, column)
        sums[k] = sums[k] + rows_to_lanes(mine)
        others.append(k)
    return sums, own_sums, weight, own_column


def pairs_kernel(seen, fresh, *refs):
    known = seen + fresh
    counts_ref, refs = refs[0], refs[1:]
    msgs, refs = dict(zip(known, refs)), refs[len(known):]
    before = {}
    own_ref = None
    if seen:
        sums_ref, own_ref, refs = refs[0], refs[1], refs[2:]
        before = {k: sums_ref[at:at + 1, :] for at, k in enumerate(seen)}
    sums_out, own_out, kept_out = refs
    sums, own_sums, _, _ = pair_sums(
        seen, fresh, counts_ref, msgs, before, own_ref, sums_out, lambda k: kept_out.at[fresh.index(k)]
    )
    own_out[...] = own_sums
    for at, k in enumerate(known):
        sums_out[at:at + 1, :] = sums[k] if k else jnp.zeros_like(sums_out[0:1, :])


def pairs_cost(seen, fresh, rows, width):
    pairs = len(fresh) * len(seen) + len(fresh) * (len(fresh) + 1) // 2
    return pl.CostEstimate(
        flops=2 * pairs * rows * rows * width,
        bytes_accessed=2 * (len(seen) + len(fresh)) * rows * width + 4 * len(fresh) * rows * rows,
        transcendentals=pairs * rows * rows,
    )


def add_pairs(seen, fresh, counts, msgs, state):
    known = seen + fresh
    rows, width = msgs[0].shape[0] - META, msgs[0].shape[1]
    return pl.pallas_call(
        functools.partial(pairs_kernel, seen, fresh),
        out_shape=(
            jax.ShapeDtypeStruct((len(known), rows), jnp.float32),
            jax.ShapeDtypeStruct((rows, 128), jnp.float32),
            jax.ShapeDtypeStruct((len(fresh), rows, rows), jnp.float32),
        ),
        in_specs=[SMEM] + [VMEM] * (len(known) + len(state)),
        out_specs=(VMEM,) * 3,
        compiler_params=pltpu.CompilerParams(vmem_limit_bytes=VMEM_LIMIT),
        cost_estimate=pairs_cost(seen, fresh, rows, width),
        name="add_pairs",
    )(counts, *(msgs[k] for k in known), *state)


def grad_kernel(stages, fresh, *refs):
    seen = [k for stage in stages for k in stage]
    known = seen + fresh
    counts_ref, refs = refs[0], refs[1:]
    msgs, refs = dict(zip(known, refs)), refs[len(known):]
    sums_ref, own_ref, refs = refs[0], refs[1], refs[2:]
    stage_refs, refs = refs[:len(stages)], refs[len(stages):]
    normed_ref, inv_ref, out_ref, kept = refs[-4:]
    rows, width = normed_ref.shape
    before = {k: sums_ref[at:at + 1, :] for at, k in enumerate(seen)}
    sums, own_sums, weight, own_weight = pair_sums(
        seen, fresh, counts_ref, msgs, before, own_ref, None, lambda k: kept.at[fresh.index(k)]
    )
    sums[0] = rows_to_lanes(own_sums)
    places = {k: kept.at[at] for at, k in enumerate(fresh)}
    for stage, ref in zip(stages, stage_refs):
        for at, k in enumerate(stage):
            places[k] = ref.at[at]

    me = lax.axis_index("pool")
    lanes = lax.broadcasted_iota(jnp.int32, (1, rows), 1)
    own_rows = me * rows + lax.broadcasted_iota(jnp.int32, (rows, 1), 0)

    def partner_of(k):
        meta = msgs[k][pl.ds(rows, META), :].astype(jnp.float32)
        return jnp.where(weight[k] > 0.0, meta[1:2] * DIGIT + meta[2:3], -1.0)

    recip = {k: jnp.where(weight[k] > 0.0, 1.0 / sums[k], 0.0) for k in known}
    own_recip = column_of(recip[0])[:, 0:1]
    own_partner = column_of(partner_of(0))[:, 0:1].astype(jnp.int32)
    both = jnp.zeros((2 * rows, width), jnp.float32)
    for k in known:
        columns = (me ^ k) * rows + lanes
        powers = places[k][...]
        along = powers * weight[k] * own_recip - jnp.where(own_partner == columns, 1.0, 0.0)
        across = powers * own_weight * recip[k] - jnp.where(
            partner_of(k).astype(jnp.int32) == own_rows, 1.0, 0.0
        )
        coefficients = jnp.concatenate([along.astype(jnp.bfloat16), across.astype(jnp.bfloat16)], axis=0)
        both = both + f32_dot(coefficients, msgs[k][pl.ds(0, rows), :], ((1,), (0,)))
    grad = both[:rows] + both[rows:]
    normed = normed_ref[...]
    inward = jnp.sum(normed * grad, axis=1, keepdims=True)
    out_ref[0] = ((grad - normed * inward) * inv_ref[:, 0:1]).astype(jnp.bfloat16)


def group_grad(stages, fresh, counts, msgs, state, kept, earlier, normed, inv):
    seen = [k for stage in stages for k in stage]
    known = seen + fresh
    rows, width = normed.shape
    return pl.pallas_call(
        functools.partial(grad_kernel, stages, fresh),
        out_shape=jax.ShapeDtypeStruct((1, rows, width), jnp.bfloat16),
        in_specs=[SMEM] + [VMEM] * (len(known) + len(state) + len(kept) + len(earlier) + 2),
        out_specs=VMEM,
        scratch_shapes=[pltpu.VMEM((len(fresh), rows, rows), jnp.float32)],
        compiler_params=pltpu.CompilerParams(vmem_limit_bytes=VMEM_LIMIT),
        cost_estimate=pairs_cost(seen, fresh, rows, width),
        name="group_grad",
    )(counts, *(msgs[k] for k in known), *state, *kept, *earlier, normed, inv)


def distinct(arrays):
    found = []
    for array in arrays:
        if all(array is not other for other in found):
            found.append(array)
    return found, [next(at for at, other in enumerate(found) if array is other) for array in arrays]


def pack_kernel(places, *refs):
    for at, (array, row) in enumerate(places):
        refs[-1][at] = refs[array][row]


def pack(pieces, earlier=()):
    arrays, which = distinct([array for array, _ in pieces])
    shape = (len(pieces),) + arrays[0].shape[1:]
    return pl.pallas_call(
        functools.partial(pack_kernel, [(at, piece[1]) for at, piece in zip(which, pieces)]),
        out_shape=jax.ShapeDtypeStruct(shape, arrays[0].dtype),
        in_specs=[VMEM] * (len(arrays) + len(earlier)),
        out_specs=VMEM,
        compiler_params=pltpu.CompilerParams(vmem_limit_bytes=VMEM_LIMIT),
        cost_estimate=pl.CostEstimate(flops=0, bytes_accessed=4 * math.prod(shape), transcendentals=0),
        name="pack",
    )(*arrays, *earlier)


def weight_kernel(places, minor, inputs, *refs):
    arrays, outs, total = refs[:inputs], refs[inputs:-1], refs[-1]
    half, piece, _ = outs[0].shape
    me = lax.axis_index("pool")
    result = None
    for array, row, grad_array, grad_row in places:
        term = f32_dot(arrays[array][row], arrays[grad_array][grad_row], ((0,), (0,)))
        result = term if result is None else result + term
    total[...] = result
    for at, out in enumerate(outs):
        near, start = at // 2, half * (1 - at % 2)
        for far in range(half):
            first = pl.multiple_of((me ^ ((start + far) * minor + near)) * piece, piece)
            out[far] = total[pl.ds(first, piece), :].astype(out.dtype)


def weight_grad(blocks, grads, members, minor):
    blocks, grads = sorted(blocks, key=lambda each: each[0]), sorted(grads, key=lambda each: each[0])
    arrays, which = distinct([array for _, array, _ in blocks + grads])
    parts = len(blocks)
    places = [(which[at], blocks[at][2], which[parts + at], grads[at][2]) for at in range(parts)]
    _, rows, cols = blocks[0][1].shape
    width = grads[0][1].shape[2]
    pieces = (members // minor // 2, cols // members, width)
    return pl.pallas_call(
        functools.partial(weight_kernel, places, minor, len(arrays)),
        out_shape=(jax.ShapeDtypeStruct(pieces, jnp.float32),) * 2
        + (jax.ShapeDtypeStruct(pieces, jnp.bfloat16),) * (2 * minor - 2),
        in_specs=[VMEM] * len(arrays),
        out_specs=(VMEM,) * (2 * minor),
        scratch_shapes=[pltpu.VMEM((cols, width), jnp.float32)],
        compiler_params=pltpu.CompilerParams(vmem_limit_bytes=VMEM_LIMIT),
        cost_estimate=pl.CostEstimate(
            flops=2 * parts * rows * cols * width, bytes_accessed=2 * parts * rows * cols, transcendentals=0
        ),
        name="weight_grad",
    )(*arrays)


def add_pieces_kernel(came, own_ref, *refs):
    for far, out in enumerate(refs[came:]):
        total = own_ref[far]
        for ref in refs[:came]:
            total = total + ref[far].astype(jnp.float32)
        out[...] = total.astype(out.dtype)


def add_pieces(own, came, first_type):
    majors, *piece = own.shape
    return pl.pallas_call(
        functools.partial(add_pieces_kernel, len(came)),
        out_shape=(jax.ShapeDtypeStruct(piece, first_type),)
        + (jax.ShapeDtypeStruct(piece, jnp.bfloat16),) * (majors - 1),
        in_specs=[VMEM] * (1 + len(came)),
        out_specs=(VMEM,) * majors,
        compiler_params=pltpu.CompilerParams(vmem_limit_bytes=SMALL_VMEM_LIMIT),
        cost_estimate=pl.CostEstimate(flops=own.size, bytes_accessed=8 * own.size, transcendentals=0),
        name="add_pieces",
    )(own, *came)


def add_all_kernel(*refs):
    total = refs[0][...].astype(jnp.float32)
    for ref in refs[1:-1]:
        total = total + ref[...].astype(jnp.float32)
    refs[-1][...] = total


def add_all(pieces):
    return pl.pallas_call(
        add_all_kernel,
        out_shape=jax.ShapeDtypeStruct(pieces[0].shape, jnp.float32),
        in_specs=[VMEM] * len(pieces),
        out_specs=VMEM,
        compiler_params=pltpu.CompilerParams(vmem_limit_bytes=SMALL_VMEM_LIMIT),
        name="add_all",
    )(*pieces)


def swap(value, axis, flip):
    size = lax.axis_size(axis)
    return lax.ppermute(value, axis, [(at, at ^ flip) for at in range(size)])


def order_kernel(value_ref, *refs):
    refs[-1][...] = value_ref[...]


def after(value, *earlier):
    return pl.pallas_call(
        order_kernel,
        out_shape=jax.ShapeDtypeStruct(value.shape, value.dtype),
        in_specs=[VMEM] * (1 + len(earlier)),
        out_specs=VMEM,
        compiler_params=pltpu.CompilerParams(vmem_limit_bytes=SMALL_VMEM_LIMIT),
        name="after",
    )(value, *earlier)


def per_device(feats, tower_w, partners, popularity_buckets, row_counts):
    members = lax.axis_size("pool")
    parts = lax.axis_size("dp")
    minor = 1 << ((members.bit_length() - 1) // 2)
    msg, normed, inv, near_cuts, far_cuts = project(feats, tower_w, partners[None, :], popularity_buckets[None, :], parts)

    majors = list(range(0, members, minor))
    last = members // 2
    msgs = {0: msg}
    msgs[last] = swap(msg, "pool", last)
    for k in majors[1:]:
        if k < last:
            msgs[k] = swap(msg, "pool", k)
    for near in range(1, minor):
        msgs[near] = swap(msg, "pool", near)
    for far in majors[1:-2]:
        for near in range(1, minor):
            msgs[far + near] = swap(msgs[far], "pool", near)
    relayed = msgs[last]
    for k in majors:
        if k > last:
            msgs[k] = swap(relayed, "pool", k ^ last)
    for near in range(1, minor):
        msgs[last + near] = swap(msgs[last], "pool", near)

    came = swap(far_cuts, "dp", parts // 2)

    state, kept, stages = (), [], []

    def add(fresh):
        nonlocal state
        *state, powers = add_pairs(sum(stages, []), fresh, row_counts, msgs, state)
        kept.append(powers)
        stages.append(fresh)

    add(majors[:-1] + list(range(1, minor)))
    add([far + near for far in majors[1:-2] for near in range(1, minor)])
    msgs3 = after(msgs[majors[-1]], state[1])
    for near in range(1, minor):
        msgs[majors[-1] + near] = swap(msgs3, "pool", near)
    add([majors[-1]])
    add([majors[-2] + near for near in range(1, minor)])
    final = [majors[-1] + near for near in range(1, minor)]
    grad_proj = group_grad(stages, final, row_counts, msgs, state, kept, [], normed, inv)

    bit = parts // 2
    grads = [(0, grad_proj, 0), (bit, swap(grad_proj, "dp", bit), 0)]
    blocks = {k: [(0, near_cuts, k), (bit, came, k)] for k in range(bit)}
    bit //= 2
    while bit:
        moving = [(k ^ bit, source ^ bit, array, at) for k in blocks if k & bit for source, array, at in blocks[k]]
        blocks = {k: blocks[k] for k in blocks if not k & bit}
        passed = swap(pack([each[2:] for each in moving], [grads[-1][1]]), "dp", bit)
        for at, (k, source, _, _) in enumerate(moving):
            blocks[k].append((source, passed, at))
        bit //= 2
    bit = parts // 4
    while bit:
        sent = swap(pack([each[1:] for each in grads]), "dp", bit)
        grads += [(each[0] ^ bit, sent, at) for at, each in enumerate(grads)]
        bit //= 2

    own_far, own_near, *pieces = weight_grad(blocks[0], grads, members, minor)
    far_came = [swap(each, "pool", at + 1) for at, each in enumerate(pieces[0::2])]
    near_came = [swap(each, "pool", at + 1) for at, each in enumerate(pieces[1::2])]
    far_sums = add_pieces(own_far, far_came, jnp.bfloat16)
    total, *near_sums = add_pieces(own_near, near_came, jnp.float32)
    half = members // minor // 2
    far_came = [swap(each, "pool", (half + at) * minor) for at, each in enumerate(far_sums)]
    near_came = [swap(each, "pool", (1 + at) * minor) for at, each in enumerate(near_sums)]
    far_total = add_all(far_came)
    total = total + far_total
    for each in near_came:
        total = total + after(each, far_total).astype(jnp.float32)
    return total


def solution(mesh):
    return jax.shard_map(
        per_device,
        mesh=mesh,
        in_specs=(P(("dp", "pool"), None), P(), P(("dp", "pool")), P(("dp", "pool")), P()),
        out_specs=P(("dp", "pool"), None),
        check_vma=False,
    )
```

```python
import functools
import math

import jax
import jax.numpy as jnp
from jax import lax
from jax.experimental import pallas as pl
from jax.experimental.pallas import tpu as pltpu
from jax.sharding import PartitionSpec as P

sharpness_scaler = 0.05
epsilon = 1e-06
META = 16
DIGIT_BITS = 8
DIGIT = 1 << DIGIT_BITS
EXP2_SCALE = math.log2(math.e) / sharpness_scaler
LOG2E = math.log2(math.e)
VMEM_LIMIT = 40 * 1024 * 1024
SMALL_VMEM_LIMIT = 8 * 1024 * 1024

VMEM = pl.BlockSpec(memory_space=pltpu.VMEM)
SMEM = pl.BlockSpec(memory_space=pltpu.SMEM)
HBM = pl.BlockSpec(memory_space=pltpu.HBM)


def f32_dot(left, right, dims):
    return lax.dot_general(left, right, (dims, ((), ())), preferred_element_type=jnp.float32)


def column_of(row):
    return jnp.transpose(jnp.broadcast_to(row, (128, row.shape[1])))


def project_kernel(parts, feats_hbm, w_hbm, partners_hbm, buckets_hbm, msg_ref, normed_ref, inv_ref,
                   near_ref, far_ref, w_v, partners_ref, buckets_ref, sems, small_sems):
    half, rows, step = near_ref.shape
    cuts = [near_ref.at[k] for k in range(half)] + [far_ref.at[k] for k in range(half)]
    width = w_v.shape[1]
    me = lax.axis_index("dp")
    small = (
        pltpu.make_async_copy(partners_hbm, partners_ref, small_sems.at[0]),
        pltpu.make_async_copy(buckets_hbm, buckets_ref, small_sems.at[1]),
    )
    for copy in small:
        copy.start()
    copies = []
    for k in range(parts):
        first = pl.multiple_of((me ^ k) * step, step)
        cut = pl.ds(first, step)
        pair = (
            pltpu.make_async_copy(feats_hbm.at[:, cut], cuts[k], sems.at[0, k]),
            pltpu.make_async_copy(w_hbm.at[cut, :], w_v.at[pl.ds(k * step, step), :], sems.at[1, k]),
        )
        pair[0].start()
        pair[1].start()
        copies.append(pair)
    projected = jnp.zeros((rows, width), jnp.float32)
    for k in range(parts):
        copies[k][0].wait()
        copies[k][1].wait()
        projected = projected + f32_dot(cuts[k][...], w_v[pl.ds(k * step, step), :], ((1,), (0,)))
    for copy in small:
        copy.wait()
    partners = partners_ref[...]
    logq = -(buckets_ref[...].astype(jnp.float32) + 0.5) / 4.0
    high = (partners >> DIGIT_BITS).astype(jnp.float32)
    low = (partners & (DIGIT - 1)).astype(jnp.float32)
    kinds = lax.broadcasted_iota(jnp.int32, (META, rows), 0)
    meta = jnp.where(kinds == 0, logq, jnp.where(kinds == 1, high, jnp.where(kinds == 2, low, 0.0)))
    msg_ref[pl.ds(rows, META), :] = meta.astype(jnp.bfloat16)
    inv_norm = lax.rsqrt(jnp.sum(projected * projected, axis=1, keepdims=True) + epsilon)
    normed = projected * inv_norm
    normed_ref[...] = normed
    inv_ref[...] = jnp.broadcast_to(inv_norm, inv_ref.shape)
    msg_ref[pl.ds(0, rows), :] = normed.astype(jnp.bfloat16)


def project(feats, tower_w, partners, buckets, parts):
    rows, din = feats.shape
    width = tower_w.shape[1]
    return pl.pallas_call(
        functools.partial(project_kernel, parts),
        out_shape=(
            jax.ShapeDtypeStruct((rows + META, width), jnp.bfloat16),
            jax.ShapeDtypeStruct((rows, width), jnp.float32),
            jax.ShapeDtypeStruct((rows, 128), jnp.float32),
        )
        + (jax.ShapeDtypeStruct((parts // 2, rows, din // parts), feats.dtype),) * 2,
        in_specs=[HBM, HBM, HBM, HBM],
        out_specs=(VMEM,) * 5,
        scratch_shapes=[
            pltpu.VMEM((din, width), jnp.bfloat16),
            pltpu.VMEM((1, rows), jnp.int32),
            pltpu.VMEM((1, rows), jnp.int32),
            pltpu.SemaphoreType.DMA((2, parts)),
            pltpu.SemaphoreType.DMA((2,)),
        ],
        compiler_params=pltpu.CompilerParams(vmem_limit_bytes=VMEM_LIMIT),
        cost_estimate=pl.CostEstimate(
            flops=2 * rows * din * width, bytes_accessed=2 * din * (rows + width), transcendentals=rows
        ),
        name="project",
    )(*(pltpu.with_memory_space_constraint(each, pltpu.HBM) for each in (feats, tower_w, partners, buckets)))


def folded(terms):
    total = terms[:, 0:128]
    for at in range(128, terms.shape[1], 128):
        total = total + terms[:, at:at + 128]
    return total


def rows_to_lanes(sums):
    return jnp.sum(jnp.transpose(sums), axis=0, keepdims=True)


def weight_of(msg_ref, counts_ref, flip):
    rows = msg_ref.shape[0] - META
    meta = msg_ref[pl.ds(rows, META), :].astype(jnp.float32)
    lanes = lax.broadcasted_iota(jnp.int32, (1, rows), 1)
    valid = lanes < counts_ref[lax.axis_index("dp"), lax.axis_index("pool") ^ flip]
    return jnp.where(valid, jnp.exp2(meta[0:1] * -LOG2E), 0.0)


def pair_sums(seen, fresh, counts_ref, msgs, sums_ref, own_ref, sums_out, kept_at):
    rows = own_ref.shape[0] if own_ref is not None else msgs[0].shape[0] - META
    emb = {k: msgs[k][pl.ds(0, rows), :] for k in seen + fresh}
    weight = {k: weight_of(msgs[k], counts_ref, k) for k in seen + fresh}
    sums = {k: sums_ref[k] for k in seen if k}
    own_sums = own_ref[...] if own_ref is not None else jnp.zeros((rows, 128), jnp.float32)
    off_diagonal = lax.broadcasted_iota(jnp.int32, (rows, rows), 0) != lax.broadcasted_iota(
        jnp.int32, (rows, rows), 1
    )

    def powers_of(left, right):
        return jnp.exp2(f32_dot(emb[left], emb[right], ((1,), (1,))) * EXP2_SCALE)

    def down(powers, column):
        return jnp.sum(powers * column, axis=0, keepdims=True)

    own_column = column_of(weight[0])[:, 0:1]
    for k in fresh:
        powers = powers_of(0, k)
        if k == 0:
            powers = jnp.where(off_diagonal, powers, 0.0)
        else:
            sums[k] = down(powers, own_column)
        kept_at(k)[...] = powers
        own_sums = own_sums + folded(powers * weight[k])
    others = [k for k in seen if k]
    for k in fresh:
        if k == 0:
            continue
        column = column_of(weight[k])[:, 0:1]
        mine = folded(jnp.where(off_diagonal, powers_of(k, k), 0.0) * weight[k])
        for other in others:
            powers = powers_of(k, other)
            mine = mine + folded(powers * weight[other])
            sums[other] = sums[other] + down(powers, column)
        sums[k] = sums[k] + rows_to_lanes(mine)
        others.append(k)
    return sums, own_sums, weight, own_column


def pairs_kernel(seen, fresh, *refs):
    known = seen + fresh
    counts_ref, refs = refs[0], refs[1:]
    msgs, refs = dict(zip(known, refs)), refs[len(known):]
    before = {}
    own_ref = None
    if seen:
        sums_ref, own_ref, refs = refs[0], refs[1], refs[2:]
        before = {k: sums_ref[at:at + 1, :] for at, k in enumerate(seen)}
    sums_out, own_out, kept_out = refs
    sums, own_sums, _, _ = pair_sums(
        seen, fresh, counts_ref, msgs, before, own_ref, sums_out, lambda k: kept_out.at[fresh.index(k)]
    )
    own_out[...] = own_sums
    for at, k in enumerate(known):
        sums_out[at:at + 1, :] = sums[k] if k else jnp.zeros_like(sums_out[0:1, :])


def pairs_cost(seen, fresh, rows, width):
    pairs = len(fresh) * len(seen) + len(fresh) * (len(fresh) + 1) // 2
    return pl.CostEstimate(
        flops=2 * pairs * rows * rows * width,
        bytes_accessed=2 * (len(seen) + len(fresh)) * rows * width + 4 * len(fresh) * rows * rows,
        transcendentals=pairs * rows * rows,
    )


def add_pairs(seen, fresh, counts, msgs, state):
    known = seen + fresh
    rows, width = msgs[0].shape[0] - META, msgs[0].shape[1]
    return pl.pallas_call(
        functools.partial(pairs_kernel, seen, fresh),
        out_shape=(
            jax.ShapeDtypeStruct((len(known), rows), jnp.float32),
            jax.ShapeDtypeStruct((rows, 128), jnp.float32),
            jax.ShapeDtypeStruct((len(fresh), rows, rows), jnp.float32),
        ),
        in_specs=[SMEM] + [VMEM] * (len(known) + len(state)),
        out_specs=(VMEM,) * 3,
        compiler_params=pltpu.CompilerParams(vmem_limit_bytes=VMEM_LIMIT),
        cost_estimate=pairs_cost(seen, fresh, rows, width),
        name="add_pairs",
    )(counts, *(msgs[k] for k in known), *state)


def grad_kernel(stages, fresh, *refs):
    seen = [k for stage in stages for k in stage]
    known = seen + fresh
    counts_ref, refs = refs[0], refs[1:]
    msgs, refs = dict(zip(known, refs)), refs[len(known):]
    sums_ref, own_ref, refs = refs[0], refs[1], refs[2:]
    stage_refs, refs = refs[:len(stages)], refs[len(stages):]
    normed_ref, inv_ref, first_ref, second_ref, kept = refs[-5:]
    rows, width = normed_ref.shape
    before = {k: sums_ref[at:at + 1, :] for at, k in enumerate(seen)}
    sums, own_sums, weight, own_weight = pair_sums(
        seen, fresh, counts_ref, msgs, before, own_ref, None, lambda k: kept.at[fresh.index(k)]
    )
    sums[0] = rows_to_lanes(own_sums)
    places = {k: kept.at[at] for at, k in enumerate(fresh)}
    for stage, ref in zip(stages, stage_refs):
        for at, k in enumerate(stage):
            places[k] = ref.at[at]

    me = lax.axis_index("pool")
    lanes = lax.broadcasted_iota(jnp.int32, (1, rows), 1)
    own_rows = me * rows + lax.broadcasted_iota(jnp.int32, (rows, 1), 0)

    def partner_of(k):
        meta = msgs[k][pl.ds(rows, META), :].astype(jnp.float32)
        return jnp.where(weight[k] > 0.0, meta[1:2] * DIGIT + meta[2:3], -1.0)

    recip = {k: jnp.where(weight[k] > 0.0, 1.0 / sums[k], 0.0) for k in known}
    own_recip = column_of(recip[0])[:, 0:1]
    own_partner = column_of(partner_of(0))[:, 0:1].astype(jnp.int32)
    both = jnp.zeros((2 * rows, width), jnp.float32)
    for k in known:
        columns = (me ^ k) * rows + lanes
        powers = places[k][...]
        along = powers * weight[k] * own_recip - jnp.where(own_partner == columns, 1.0, 0.0)
        across = powers * own_weight * recip[k] - jnp.where(
            partner_of(k).astype(jnp.int32) == own_rows, 1.0, 0.0
        )
        coefficients = jnp.concatenate([along.astype(jnp.bfloat16), across.astype(jnp.bfloat16)], axis=0)
        both = both + f32_dot(coefficients, msgs[k][pl.ds(0, rows), :], ((1,), (0,)))
    grad = both[:rows] + both[rows:]
    normed = normed_ref[...]
    inward = jnp.sum(normed * grad, axis=1, keepdims=True)
    result = ((grad - normed * inward) * inv_ref[:, 0:1]).astype(jnp.bfloat16)
    first_ref[...] = result[:rows // 2]
    second_ref[...] = result[rows // 2:]


def group_grad(stages, fresh, counts, msgs, state, kept, earlier, normed, inv):
    seen = [k for stage in stages for k in stage]
    known = seen + fresh
    rows, width = normed.shape
    return pl.pallas_call(
        functools.partial(grad_kernel, stages, fresh),
        out_shape=(jax.ShapeDtypeStruct((rows // 2, width), jnp.bfloat16),) * 2,
        in_specs=[SMEM] + [VMEM] * (len(known) + len(state) + len(kept) + len(earlier) + 2),
        out_specs=(VMEM, VMEM),
        scratch_shapes=[pltpu.VMEM((len(fresh), rows, rows), jnp.float32)],
        compiler_params=pltpu.CompilerParams(vmem_limit_bytes=VMEM_LIMIT),
        cost_estimate=pairs_cost(seen, fresh, rows, width),
        name="group_grad",
    )(counts, *(msgs[k] for k in known), *state, *kept, *earlier, normed, inv)


def distinct(arrays):
    found = []
    for array in arrays:
        if all(array is not other for other in found):
            found.append(array)
    return found, [next(at for at, other in enumerate(found) if array is other) for array in arrays]


def join_kernel(*refs):
    half = refs[0].shape[0]
    for at, ref in enumerate(refs[:-1]):
        refs[-1][at // 2, pl.ds(at % 2 * half, half), :] = ref[...]


def join(halves):
    half, width = halves[0].shape
    return pl.pallas_call(
        join_kernel,
        out_shape=jax.ShapeDtypeStruct((len(halves) // 2, 2 * half, width), halves[0].dtype),
        in_specs=[VMEM] * len(halves),
        out_specs=VMEM,
        compiler_params=pltpu.CompilerParams(vmem_limit_bytes=SMALL_VMEM_LIMIT),
        name="join",
    )(*halves)


def pack_kernel(places, *refs):
    for at, (array, row) in enumerate(places):
        refs[-1][at] = refs[array][row]


def pack(pieces, earlier=()):
    arrays, which = distinct([array for array, _ in pieces])
    shape = (len(pieces),) + arrays[0].shape[1:]
    return pl.pallas_call(
        functools.partial(pack_kernel, [(at, piece[1]) for at, piece in zip(which, pieces)]),
        out_shape=jax.ShapeDtypeStruct(shape, arrays[0].dtype),
        in_specs=[VMEM] * (len(arrays) + len(earlier)),
        out_specs=VMEM,
        compiler_params=pltpu.CompilerParams(vmem_limit_bytes=VMEM_LIMIT),
        cost_estimate=pl.CostEstimate(flops=0, bytes_accessed=4 * math.prod(shape), transcendentals=0),
        name="pack",
    )(*arrays, *earlier)


def weight_kernel(places, minor, inputs, *refs):
    arrays, outs, total = refs[:inputs], refs[inputs:-1], refs[-1]
    half, piece, _ = outs[0].shape
    me = lax.axis_index("pool")
    result = None
    for array, row, grad_array, grad_row in places:
        term = f32_dot(arrays[array][row], arrays[grad_array][grad_row], ((0,), (0,)))
        result = term if result is None else result + term
    total[...] = result
    for at, out in enumerate(outs):
        near, start = at // 2, half * (1 - at % 2)
        for far in range(half):
            first = pl.multiple_of((me ^ ((start + far) * minor + near)) * piece, piece)
            out[far] = total[pl.ds(first, piece), :].astype(out.dtype)


def weight_grad(blocks, grads, members, minor):
    blocks, grads = sorted(blocks, key=lambda each: each[0]), sorted(grads, key=lambda each: each[0])
    arrays, which = distinct([array for _, array, _ in blocks + grads])
    parts = len(blocks)
    places = [(which[at], blocks[at][2], which[parts + at], grads[at][2]) for at in range(parts)]
    _, rows, cols = blocks[0][1].shape
    width = grads[0][1].shape[2]
    pieces = (members // minor // 2, cols // members, width)
    return pl.pallas_call(
        functools.partial(weight_kernel, places, minor, len(arrays)),
        out_shape=(jax.ShapeDtypeStruct(pieces, jnp.float32),) * 2
        + (jax.ShapeDtypeStruct(pieces, jnp.bfloat16),) * (2 * minor - 2),
        in_specs=[VMEM] * len(arrays),
        out_specs=(VMEM,) * (2 * minor),
        scratch_shapes=[pltpu.VMEM((cols, width), jnp.float32)],
        compiler_params=pltpu.CompilerParams(vmem_limit_bytes=VMEM_LIMIT),
        cost_estimate=pl.CostEstimate(
            flops=2 * parts * rows * cols * width, bytes_accessed=2 * parts * rows * cols, transcendentals=0
        ),
        name="weight_grad",
    )(*arrays)


def add_pieces_kernel(came, own_ref, *refs):
    for far, out in enumerate(refs[came:]):
        total = own_ref[far]
        for ref in refs[:came]:
            total = total + ref[far].astype(jnp.float32)
        out[...] = total.astype(out.dtype)


def add_pieces(own, came, first_type):
    majors, *piece = own.shape
    return pl.pallas_call(
        functools.partial(add_pieces_kernel, len(came)),
        out_shape=(jax.ShapeDtypeStruct(piece, first_type),)
        + (jax.ShapeDtypeStruct(piece, jnp.bfloat16),) * (majors - 1),
        in_specs=[VMEM] * (1 + len(came)),
        out_specs=(VMEM,) * majors,
        compiler_params=pltpu.CompilerParams(vmem_limit_bytes=SMALL_VMEM_LIMIT),
        cost_estimate=pl.CostEstimate(flops=own.size, bytes_accessed=8 * own.size, transcendentals=0),
        name="add_pieces",
    )(own, *came)


def add_all_kernel(*refs):
    total = refs[0][...].astype(jnp.float32)
    for ref in refs[1:-1]:
        total = total + ref[...].astype(jnp.float32)
    refs[-1][...] = total


def add_all(pieces):
    return pl.pallas_call(
        add_all_kernel,
        out_shape=jax.ShapeDtypeStruct(pieces[0].shape, jnp.float32),
        in_specs=[VMEM] * len(pieces),
        out_specs=VMEM,
        compiler_params=pltpu.CompilerParams(vmem_limit_bytes=SMALL_VMEM_LIMIT),
        name="add_all",
    )(*pieces)


def swap(value, axis, flip):
    size = lax.axis_size(axis)
    return lax.ppermute(value, axis, [(at, at ^ flip) for at in range(size)])


def order_kernel(value_ref, *refs):
    refs[-1][...] = value_ref[...]


def after(value, *earlier):
    return pl.pallas_call(
        order_kernel,
        out_shape=jax.ShapeDtypeStruct(value.shape, value.dtype),
        in_specs=[VMEM] * (1 + len(earlier)),
        out_specs=VMEM,
        compiler_params=pltpu.CompilerParams(vmem_limit_bytes=SMALL_VMEM_LIMIT),
        name="after",
    )(value, *earlier)


def per_device(feats, tower_w, partners, popularity_buckets, row_counts):
    members = lax.axis_size("pool")
    parts = lax.axis_size("dp")
    minor = 1 << ((members.bit_length() - 1) // 2)
    msg, normed, inv, near_cuts, far_cuts = project(feats, tower_w, partners[None, :], popularity_buckets[None, :], parts)

    majors = list(range(0, members, minor))
    last = members // 2
    msgs = {0: msg}
    msgs[last] = swap(msg, "pool", last)
    for k in majors[1:]:
        if k < last:
            msgs[k] = swap(msg, "pool", k)
    for near in range(1, minor):
        msgs[near] = swap(msg, "pool", near)
    for far in majors[1:-2]:
        for near in range(1, minor):
            msgs[far + near] = swap(msgs[far], "pool", near)
    relayed = msgs[last]
    for k in majors:
        if k > last:
            msgs[k] = swap(relayed, "pool", k ^ last)
    for near in range(1, minor):
        msgs[last + near] = swap(msgs[last], "pool", near)

    came = swap(far_cuts, "dp", parts // 2)

    state, kept, stages = (), [], []

    def add(fresh):
        nonlocal state
        *state, powers = add_pairs(sum(stages, []), fresh, row_counts, msgs, state)
        kept.append(powers)
        stages.append(fresh)

    add(majors[:-1] + list(range(1, minor)))
    add([far + near for far in majors[1:-2] for near in range(1, minor)])
    msgs3 = after(msgs[majors[-1]], state[1])
    for near in range(1, minor):
        msgs[majors[-1] + near] = swap(msgs3, "pool", near)
    add([majors[-1]])
    add([majors[-2] + near for near in range(1, minor)])
    final = [majors[-1] + near for near in range(1, minor)]
    halves = group_grad(stages, final, row_counts, msgs, state, kept, [], normed, inv)

    bit = parts // 2
    came_halves = [swap(each, "dp", bit) for each in halves]
    joined = join([*halves, *came_halves])
    grads = [(0, joined, 0), (bit, joined, 1)]
    blocks = {k: [(0, near_cuts, k), (bit, came, k)] for k in range(bit)}
    bit //= 2
    while bit:
        moving = [(k ^ bit, source ^ bit, array, at) for k in blocks if k & bit for source, array, at in blocks[k]]
        blocks = {k: blocks[k] for k in blocks if not k & bit}
        passed = swap(pack([each[2:] for each in moving], list(came_halves)), "dp", bit)
        for at, (k, source, _, _) in enumerate(moving):
            blocks[k].append((source, passed, at))
        bit //= 2
    bit = parts // 4
    while bit:
        sent = swap(pack([each[1:] for each in grads]), "dp", bit)
        grads += [(each[0] ^ bit, sent, at) for at, each in enumerate(grads)]
        bit //= 2

    own_far, own_near, *pieces = weight_grad(blocks[0], grads, members, minor)
    far_came = [swap(each, "pool", at + 1) for at, each in enumerate(pieces[0::2])]
    near_came = [swap(each, "pool", at + 1) for at, each in enumerate(pieces[1::2])]
    far_sums = add_pieces(own_far, far_came, jnp.bfloat16)
    total, *near_sums = add_pieces(own_near, near_came, jnp.float32)
    half = members // minor // 2
    far_came = [swap(each, "pool", (half + at) * minor) for at, each in enumerate(far_sums)]
    near_came = [swap(each, "pool", (1 + at) * minor) for at, each in enumerate(near_sums)]
    far_total = add_all(far_came)
    total = total + far_total
    for each in near_came:
        total = total + after(each, far_total).astype(jnp.float32)
    return total


def solution(mesh):
    return jax.shard_map(
        per_device,
        mesh=mesh,
        in_specs=(P(("dp", "pool"), None), P(), P(("dp", "pool")), P(("dp", "pool")), P()),
        out_specs=P(("dp", "pool"), None),
        check_vma=False,
    )
```

```python
import functools
import math

import jax
import jax.numpy as jnp
from jax import lax
from jax.experimental import pallas as pl
from jax.experimental.pallas import tpu as pltpu
from jax.sharding import PartitionSpec as P

sharpness_scaler = 0.05
epsilon = 1e-06
META = 16
DIGIT_BITS = 8
DIGIT = 1 << DIGIT_BITS
EXP2_SCALE = math.log2(math.e) / sharpness_scaler
LOG2E = math.log2(math.e)
VMEM_LIMIT = 40 * 1024 * 1024
SMALL_VMEM_LIMIT = 8 * 1024 * 1024

VMEM = pl.BlockSpec(memory_space=pltpu.VMEM)
SMEM = pl.BlockSpec(memory_space=pltpu.SMEM)
HBM = pl.BlockSpec(memory_space=pltpu.HBM)


def f32_dot(left, right, dims):
    return lax.dot_general(left, right, (dims, ((), ())), preferred_element_type=jnp.float32)


def column_of(row):
    return jnp.transpose(jnp.broadcast_to(row, (128, row.shape[1])))


def project_kernel(parts, feats_hbm, w_hbm, partners_hbm, buckets_hbm, msg_ref, normed_ref, inv_ref,
                   near_ref, far_ref, w_v, partners_ref, buckets_ref, sems, small_sems):
    half, rows, step = near_ref.shape
    cuts = [near_ref.at[k] for k in range(half)] + [far_ref.at[k] for k in range(half)]
    width = w_v.shape[1]
    me = lax.axis_index("dp")
    small = (
        pltpu.make_async_copy(partners_hbm, partners_ref, small_sems.at[0]),
        pltpu.make_async_copy(buckets_hbm, buckets_ref, small_sems.at[1]),
    )
    for copy in small:
        copy.start()
    halves = sems.shape[1] // parts
    part = step // halves
    copies = []
    for at in range(parts * halves):
        k, half = at // halves, at % halves
        first = pl.multiple_of((me ^ k) * step + half * part, part)
        feats_part = cuts[k].at[:, pl.ds(half * part, part)]
        w_part = w_v.at[pl.ds(at * part, part), :]
        pair = (
            pltpu.make_async_copy(feats_hbm.at[:, pl.ds(first, part)], feats_part, sems.at[0, at]),
            pltpu.make_async_copy(w_hbm.at[pl.ds(first, part), :], w_part, sems.at[1, at]),
        )
        pair[0].start()
        pair[1].start()
        copies.append((pair, feats_part, w_part))
    projected = jnp.zeros((rows, width), jnp.float32)
    for pair, feats_part, w_part in copies:
        pair[0].wait()
        pair[1].wait()
        projected = projected + f32_dot(feats_part[...], w_part[...], ((1,), (0,)))
    for copy in small:
        copy.wait()
    partners = partners_ref[...]
    logq = -(buckets_ref[...].astype(jnp.float32) + 0.5) / 4.0
    high = (partners >> DIGIT_BITS).astype(jnp.float32)
    low = (partners & (DIGIT - 1)).astype(jnp.float32)
    kinds = lax.broadcasted_iota(jnp.int32, (META, rows), 0)
    meta = jnp.where(kinds == 0, logq, jnp.where(kinds == 1, high, jnp.where(kinds == 2, low, 0.0)))
    msg_ref[pl.ds(rows, META), :] = meta.astype(jnp.bfloat16)
    inv_norm = lax.rsqrt(jnp.sum(projected * projected, axis=1, keepdims=True) + epsilon)
    normed = projected * inv_norm
    normed_ref[...] = normed
    inv_ref[...] = jnp.broadcast_to(inv_norm, inv_ref.shape)
    msg_ref[pl.ds(0, rows), :] = normed.astype(jnp.bfloat16)


def project(feats, tower_w, partners, buckets, parts):
    rows, din = feats.shape
    width = tower_w.shape[1]
    halves = 2 if din // parts % 256 == 0 else 1
    return pl.pallas_call(
        functools.partial(project_kernel, parts),
        out_shape=(
            jax.ShapeDtypeStruct((rows + META, width), jnp.bfloat16),
            jax.ShapeDtypeStruct((rows, width), jnp.float32),
            jax.ShapeDtypeStruct((rows, 128), jnp.float32),
        )
        + (jax.ShapeDtypeStruct((parts // 2, rows, din // parts), feats.dtype),) * 2,
        in_specs=[HBM, HBM, HBM, HBM],
        out_specs=(VMEM,) * 5,
        scratch_shapes=[
            pltpu.VMEM((din, width), jnp.bfloat16),
            pltpu.VMEM((1, rows), jnp.int32),
            pltpu.VMEM((1, rows), jnp.int32),
            pltpu.SemaphoreType.DMA((2, parts * halves)),
            pltpu.SemaphoreType.DMA((2,)),
        ],
        compiler_params=pltpu.CompilerParams(vmem_limit_bytes=VMEM_LIMIT),
        cost_estimate=pl.CostEstimate(
            flops=2 * rows * din * width, bytes_accessed=2 * din * (rows + width), transcendentals=rows
        ),
        name="project",
    )(*(pltpu.with_memory_space_constraint(each, pltpu.HBM) for each in (feats, tower_w, partners, buckets)))


def folded(terms):
    total = terms[:, 0:128]
    for at in range(128, terms.shape[1], 128):
        total = total + terms[:, at:at + 128]
    return total


def rows_to_lanes(sums):
    return jnp.sum(jnp.transpose(sums), axis=0, keepdims=True)


def weight_of(msg_ref, counts_ref, flip):
    rows = msg_ref.shape[0] - META
    meta = msg_ref[pl.ds(rows, META), :].astype(jnp.float32)
    lanes = lax.broadcasted_iota(jnp.int32, (1, rows), 1)
    valid = lanes < counts_ref[lax.axis_index("dp"), lax.axis_index("pool") ^ flip]
    return jnp.where(valid, jnp.exp2(meta[0:1] * -LOG2E), 0.0)


def pair_sums(seen, fresh, counts_ref, msgs, sums_ref, own_ref, sums_out, kept_at):
    rows = own_ref.shape[0] if own_ref is not None else msgs[0].shape[0] - META
    emb = {k: msgs[k][pl.ds(0, rows), :] for k in seen + fresh}
    weight = {k: weight_of(msgs[k], counts_ref, k) for k in seen + fresh}
    sums = {k: sums_ref[k] for k in seen if k}
    own_sums = own_ref[...] if own_ref is not None else jnp.zeros((rows, 128), jnp.float32)
    off_diagonal = lax.broadcasted_iota(jnp.int32, (rows, rows), 0) != lax.broadcasted_iota(
        jnp.int32, (rows, rows), 1
    )

    def powers_of(left, right):
        return jnp.exp2(f32_dot(emb[left], emb[right], ((1,), (1,))) * EXP2_SCALE)

    def down(powers, column):
        return jnp.sum(powers * column, axis=0, keepdims=True)

    own_column = column_of(weight[0])[:, 0:1]
    for k in fresh:
        powers = powers_of(0, k)
        if k == 0:
            powers = jnp.where(off_diagonal, powers, 0.0)
        else:
            sums[k] = down(powers, own_column)
        kept_at(k)[...] = powers
        own_sums = own_sums + folded(powers * weight[k])
    others = [k for k in seen if k]
    for k in fresh:
        if k == 0:
            continue
        column = column_of(weight[k])[:, 0:1]
        mine = folded(jnp.where(off_diagonal, powers_of(k, k), 0.0) * weight[k])
        for other in others:
            powers = powers_of(k, other)
            mine = mine + folded(powers * weight[other])
            sums[other] = sums[other] + down(powers, column)
        sums[k] = sums[k] + rows_to_lanes(mine)
        others.append(k)
    return sums, own_sums, weight, own_column


def pairs_kernel(seen, fresh, *refs):
    known = seen + fresh
    counts_ref, refs = refs[0], refs[1:]
    msgs, refs = dict(zip(known, refs)), refs[len(known):]
    before = {}
    own_ref = None
    if seen:
        sums_ref, own_ref, refs = refs[0], refs[1], refs[2:]
        before = {k: sums_ref[at:at + 1, :] for at, k in enumerate(seen)}
    sums_out, own_out, kept_out = refs
    sums, own_sums, _, _ = pair_sums(
        seen, fresh, counts_ref, msgs, before, own_ref, sums_out, lambda k: kept_out.at[fresh.index(k)]
    )
    own_out[...] = own_sums
    for at, k in enumerate(known):
        sums_out[at:at + 1, :] = sums[k] if k else jnp.zeros_like(sums_out[0:1, :])


def pairs_cost(seen, fresh, rows, width):
    pairs = len(fresh) * len(seen) + len(fresh) * (len(fresh) + 1) // 2
    return pl.CostEstimate(
        flops=2 * pairs * rows * rows * width,
        bytes_accessed=2 * (len(seen) + len(fresh)) * rows * width + 4 * len(fresh) * rows * rows,
        transcendentals=pairs * rows * rows,
    )


def add_pairs(seen, fresh, counts, msgs, state):
    known = seen + fresh
    rows, width = msgs[0].shape[0] - META, msgs[0].shape[1]
    return pl.pallas_call(
        functools.partial(pairs_kernel, seen, fresh),
        out_shape=(
            jax.ShapeDtypeStruct((len(known), rows), jnp.float32),
            jax.ShapeDtypeStruct((rows, 128), jnp.float32),
            jax.ShapeDtypeStruct((len(fresh), rows, rows), jnp.float32),
        ),
        in_specs=[SMEM] + [VMEM] * (len(known) + len(state)),
        out_specs=(VMEM,) * 3,
        compiler_params=pltpu.CompilerParams(vmem_limit_bytes=VMEM_LIMIT),
        cost_estimate=pairs_cost(seen, fresh, rows, width),
        name="add_pairs",
    )(counts, *(msgs[k] for k in known), *state)


def grad_kernel(stages, fresh, *refs):
    seen = [k for stage in stages for k in stage]
    known = seen + fresh
    counts_ref, refs = refs[0], refs[1:]
    msgs, refs = dict(zip(known, refs)), refs[len(known):]
    sums_ref, own_ref, refs = refs[0], refs[1], refs[2:]
    stage_refs, refs = refs[:len(stages)], refs[len(stages):]
    normed_ref, inv_ref, out_ref, kept = refs[-4:]
    rows, width = normed_ref.shape
    before = {k: sums_ref[at:at + 1, :] for at, k in enumerate(seen)}
    sums, own_sums, weight, own_weight = pair_sums(
        seen, fresh, counts_ref, msgs, before, own_ref, None, lambda k: kept.at[fresh.index(k)]
    )
    sums[0] = rows_to_lanes(own_sums)
    places = {k: kept.at[at] for at, k in enumerate(fresh)}
    for stage, ref in zip(stages, stage_refs):
        for at, k in enumerate(stage):
            places[k] = ref.at[at]

    me = lax.axis_index("pool")
    lanes = lax.broadcasted_iota(jnp.int32, (1, rows), 1)
    own_rows = me * rows + lax.broadcasted_iota(jnp.int32, (rows, 1), 0)

    def partner_of(k):
        meta = msgs[k][pl.ds(rows, META), :].astype(jnp.float32)
        return jnp.where(weight[k] > 0.0, meta[1:2] * DIGIT + meta[2:3], -1.0)

    recip = {k: jnp.where(weight[k] > 0.0, 1.0 / sums[k], 0.0) for k in known}
    own_recip = column_of(recip[0])[:, 0:1]
    own_partner = column_of(partner_of(0))[:, 0:1].astype(jnp.int32)
    both = jnp.zeros((2 * rows, width), jnp.float32)
    for k in known:
        columns = (me ^ k) * rows + lanes
        powers = places[k][...]
        along = powers * weight[k] * own_recip - jnp.where(own_partner == columns, 1.0, 0.0)
        across = powers * own_weight * recip[k] - jnp.where(
            partner_of(k).astype(jnp.int32) == own_rows, 1.0, 0.0
        )
        coefficients = jnp.concatenate([along.astype(jnp.bfloat16), across.astype(jnp.bfloat16)], axis=0)
        both = both + f32_dot(coefficients, msgs[k][pl.ds(0, rows), :], ((1,), (0,)))
    grad = both[:rows] + both[rows:]
    normed = normed_ref[...]
    inward = jnp.sum(normed * grad, axis=1, keepdims=True)
    out_ref[0] = ((grad - normed * inward) * inv_ref[:, 0:1]).astype(jnp.bfloat16)


def group_grad(stages, fresh, counts, msgs, state, kept, earlier, normed, inv):
    seen = [k for stage in stages for k in stage]
    known = seen + fresh
    rows, width = normed.shape
    return pl.pallas_call(
        functools.partial(grad_kernel, stages, fresh),
        out_shape=jax.ShapeDtypeStruct((1, rows, width), jnp.bfloat16),
        in_specs=[SMEM] + [VMEM] * (len(known) + len(state) + len(kept) + len(earlier) + 2),
        out_specs=VMEM,
        scratch_shapes=[pltpu.VMEM((len(fresh), rows, rows), jnp.float32)],
        compiler_params=pltpu.CompilerParams(vmem_limit_bytes=VMEM_LIMIT),
        cost_estimate=pairs_cost(seen, fresh, rows, width),
        name="group_grad",
    )(counts, *(msgs[k] for k in known), *state, *kept, *earlier, normed, inv)


def distinct(arrays):
    found = []
    for array in arrays:
        if all(array is not other for other in found):
            found.append(array)
    return found, [next(at for at, other in enumerate(found) if array is other) for array in arrays]


def pack_kernel(places, *refs):
    for at, (array, row) in enumerate(places):
        refs[-1][at] = refs[array][row]


def pack(pieces, earlier=()):
    arrays, which = distinct([array for array, _ in pieces])
    shape = (len(pieces),) + arrays[0].shape[1:]
    return pl.pallas_call(
        functools.partial(pack_kernel, [(at, piece[1]) for at, piece in zip(which, pieces)]),
        out_shape=jax.ShapeDtypeStruct(shape, arrays[0].dtype),
        in_specs=[VMEM] * (len(arrays) + len(earlier)),
        out_specs=VMEM,
        compiler_params=pltpu.CompilerParams(vmem_limit_bytes=VMEM_LIMIT),
        cost_estimate=pl.CostEstimate(flops=0, bytes_accessed=4 * math.prod(shape), transcendentals=0),
        name="pack",
    )(*arrays, *earlier)


def weight_kernel(places, minor, inputs, *refs):
    arrays, outs, total = refs[:inputs], refs[inputs:-1], refs[-1]
    half, piece, _ = outs[0].shape
    me = lax.axis_index("pool")
    result = None
    for array, row, grad_array, grad_row in places:
        term = f32_dot(arrays[array][row], arrays[grad_array][grad_row], ((0,), (0,)))
        result = term if result is None else result + term
    total[...] = result
    for at, out in enumerate(outs):
        near, start = at // 2, half * (1 - at % 2)
        for far in range(half):
            first = pl.multiple_of((me ^ ((start + far) * minor + near)) * piece, piece)
            out[far] = total[pl.ds(first, piece), :].astype(out.dtype)


def weight_grad(blocks, grads, members, minor):
    blocks, grads = sorted(blocks, key=lambda each: each[0]), sorted(grads, key=lambda each: each[0])
    arrays, which = distinct([array for _, array, _ in blocks + grads])
    parts = len(blocks)
    places = [(which[at], blocks[at][2], which[parts + at], grads[at][2]) for at in range(parts)]
    _, rows, cols = blocks[0][1].shape
    width = grads[0][1].shape[2]
    pieces = (members // minor // 2, cols // members, width)
    return pl.pallas_call(
        functools.partial(weight_kernel, places, minor, len(arrays)),
        out_shape=(jax.ShapeDtypeStruct(pieces, jnp.float32),) * 2
        + (jax.ShapeDtypeStruct(pieces, jnp.bfloat16),) * (2 * minor - 2),
        in_specs=[VMEM] * len(arrays),
        out_specs=(VMEM,) * (2 * minor),
        scratch_shapes=[pltpu.VMEM((cols, width), jnp.float32)],
        compiler_params=pltpu.CompilerParams(vmem_limit_bytes=VMEM_LIMIT),
        cost_estimate=pl.CostEstimate(
            flops=2 * parts * rows * cols * width, bytes_accessed=2 * parts * rows * cols, transcendentals=0
        ),
        name="weight_grad",
    )(*arrays)


def add_pieces_kernel(came, own_ref, *refs):
    for far, out in enumerate(refs[came:]):
        total = own_ref[far]
        for ref in refs[:came]:
            total = total + ref[far].astype(jnp.float32)
        out[...] = total.astype(out.dtype)


def add_pieces(own, came, first_type):
    majors, *piece = own.shape
    return pl.pallas_call(
        functools.partial(add_pieces_kernel, len(came)),
        out_shape=(jax.ShapeDtypeStruct(piece, first_type),)
        + (jax.ShapeDtypeStruct(piece, jnp.bfloat16),) * (majors - 1),
        in_specs=[VMEM] * (1 + len(came)),
        out_specs=(VMEM,) * majors,
        compiler_params=pltpu.CompilerParams(vmem_limit_bytes=SMALL_VMEM_LIMIT),
        cost_estimate=pl.CostEstimate(flops=own.size, bytes_accessed=8 * own.size, transcendentals=0),
        name="add_pieces",
    )(own, *came)


def add_all_kernel(*refs):
    total = refs[0][...].astype(jnp.float32)
    for ref in refs[1:-1]:
        total = total + ref[...].astype(jnp.float32)
    refs[-1][...] = total


def add_all(pieces):
    return pl.pallas_call(
        add_all_kernel,
        out_shape=jax.ShapeDtypeStruct(pieces[0].shape, jnp.float32),
        in_specs=[VMEM] * len(pieces),
        out_specs=VMEM,
        compiler_params=pltpu.CompilerParams(vmem_limit_bytes=SMALL_VMEM_LIMIT),
        name="add_all",
    )(*pieces)


def swap(value, axis, flip):
    size = lax.axis_size(axis)
    return lax.ppermute(value, axis, [(at, at ^ flip) for at in range(size)])


def order_kernel(value_ref, *refs):
    refs[-1][...] = value_ref[...]


def after(value, *earlier):
    return pl.pallas_call(
        order_kernel,
        out_shape=jax.ShapeDtypeStruct(value.shape, value.dtype),
        in_specs=[VMEM] * (1 + len(earlier)),
        out_specs=VMEM,
        compiler_params=pltpu.CompilerParams(vmem_limit_bytes=SMALL_VMEM_LIMIT),
        name="after",
    )(value, *earlier)


def per_device(feats, tower_w, partners, popularity_buckets, row_counts):
    members = lax.axis_size("pool")
    parts = lax.axis_size("dp")
    minor = 1 << ((members.bit_length() - 1) // 2)
    msg, normed, inv, near_cuts, far_cuts = project(feats, tower_w, partners[None, :], popularity_buckets[None, :], parts)

    majors = list(range(0, members, minor))
    last = members // 2
    msgs = {0: msg}
    msgs[last] = swap(msg, "pool", last)
    for k in majors[1:]:
        if k < last:
            msgs[k] = swap(msg, "pool", k)
    for near in range(1, minor):
        msgs[near] = swap(msg, "pool", near)
    for far in majors[1:-2]:
        for near in range(1, minor):
            msgs[far + near] = swap(msgs[far], "pool", near)
    relayed = msgs[last]
    for k in majors:
        if k > last:
            msgs[k] = swap(relayed, "pool", k ^ last)
    for near in range(1, minor):
        msgs[last + near] = swap(msgs[last], "pool", near)

    came = swap(far_cuts, "dp", parts // 2)

    state, kept, stages = (), [], []

    def add(fresh):
        nonlocal state
        *state, powers = add_pairs(sum(stages, []), fresh, row_counts, msgs, state)
        kept.append(powers)
        stages.append(fresh)

    add(majors[:-1] + list(range(1, minor)))
    add([far + near for far in majors[1:-2] for near in range(1, minor)])
    msgs3 = after(msgs[majors[-1]], state[1])
    for near in range(1, minor):
        msgs[majors[-1] + near] = swap(msgs3, "pool", near)
    add([majors[-1]])
    add([majors[-2] + near for near in range(1, minor)])
    final = [majors[-1] + near for near in range(1, minor)]
    grad_proj = group_grad(stages, final, row_counts, msgs, state, kept, [], normed, inv)

    bit = parts // 2
    grads = [(0, grad_proj, 0), (bit, swap(grad_proj, "dp", bit), 0)]
    blocks = {k: [(0, near_cuts, k), (bit, came, k)] for k in range(bit)}
    bit //= 2
    while bit:
        moving = [(k ^ bit, source ^ bit, array, at) for k in blocks if k & bit for source, array, at in blocks[k]]
        blocks = {k: blocks[k] for k in blocks if not k & bit}
        passed = swap(pack([each[2:] for each in moving], [grads[-1][1]]), "dp", bit)
        for at, (k, source, _, _) in enumerate(moving):
            blocks[k].append((source, passed, at))
        bit //= 2
    bit = parts // 4
    while bit:
        sent = swap(pack([each[1:] for each in grads]), "dp", bit)
        grads += [(each[0] ^ bit, sent, at) for at, each in enumerate(grads)]
        bit //= 2

    own_far, own_near, *pieces = weight_grad(blocks[0], grads, members, minor)
    far_came = [swap(each, "pool", at + 1) for at, each in enumerate(pieces[0::2])]
    near_came = [swap(each, "pool", at + 1) for at, each in enumerate(pieces[1::2])]
    far_sums = add_pieces(own_far, far_came, jnp.bfloat16)
    total, *near_sums = add_pieces(own_near, near_came, jnp.float32)
    half = members // minor // 2
    far_came = [swap(each, "pool", (half + at) * minor) for at, each in enumerate(far_sums)]
    near_came = [swap(each, "pool", (1 + at) * minor) for at, each in enumerate(near_sums)]
    far_total = add_all(far_came)
    total = total + far_total
    for each in near_came:
        total = total + after(each, far_total).astype(jnp.float32)
    return total


def solution(mesh):
    return jax.shard_map(
        per_device,
        mesh=mesh,
        in_specs=(P(("dp", "pool"), None), P(), P(("dp", "pool")), P(("dp", "pool")), P()),
        out_specs=P(("dp", "pool"), None),
        check_vma=False,
    )
```

```python
import functools
import math

import jax
import jax.numpy as jnp
from jax import lax
from jax.experimental import pallas as pl
from jax.experimental.pallas import tpu as pltpu
from jax.sharding import PartitionSpec as P

sharpness_scaler = 0.05
epsilon = 1e-06
META = 16
DIGIT_BITS = 8
DIGIT = 1 << DIGIT_BITS
EXP2_SCALE = math.log2(math.e) / sharpness_scaler
LOG2E = math.log2(math.e)
VMEM_LIMIT = 40 * 1024 * 1024
SMALL_VMEM_LIMIT = 8 * 1024 * 1024

VMEM = pl.BlockSpec(memory_space=pltpu.VMEM)
SMEM = pl.BlockSpec(memory_space=pltpu.SMEM)
HBM = pl.BlockSpec(memory_space=pltpu.HBM)


def f32_dot(left, right, dims):
    return lax.dot_general(left, right, (dims, ((), ())), preferred_element_type=jnp.float32)


def column_of(row):
    return jnp.transpose(jnp.broadcast_to(row, (128, row.shape[1])))


def project_kernel(parts, feats_hbm, w_hbm, partners_hbm, buckets_hbm, msg_ref, normed_ref, inv_ref,
                   near_ref, far_ref, w_v, partners_ref, buckets_ref, sems, small_sems):
    half, rows, step = near_ref.shape
    cuts = [near_ref.at[k] for k in range(half)] + [far_ref.at[k] for k in range(half)]
    width = w_v.shape[1]
    me = lax.axis_index("dp")
    small = (
        pltpu.make_async_copy(partners_hbm, partners_ref, small_sems.at[0]),
        pltpu.make_async_copy(buckets_hbm, buckets_ref, small_sems.at[1]),
    )
    for copy in small:
        copy.start()
    copies = []
    for k in range(parts):
        first = pl.multiple_of((me ^ k) * step, step)
        cut = pl.ds(first, step)
        pair = (
            pltpu.make_async_copy(feats_hbm.at[:, cut], cuts[k], sems.at[0, k]),
            pltpu.make_async_copy(w_hbm.at[cut, :], w_v.at[pl.ds(k * step, step), :], sems.at[1, k]),
        )
        pair[0].start()
        pair[1].start()
        copies.append(pair)
    projected = jnp.zeros((rows, width), jnp.float32)
    for k in range(parts):
        copies[k][0].wait()
        copies[k][1].wait()
        projected = projected + f32_dot(cuts[k][...], w_v[pl.ds(k * step, step), :], ((1,), (0,)))
    for copy in small:
        copy.wait()
    partners = partners_ref[...]
    logq = -(buckets_ref[...].astype(jnp.float32) + 0.5) / 4.0
    high = (partners >> DIGIT_BITS).astype(jnp.float32)
    low = (partners & (DIGIT - 1)).astype(jnp.float32)
    kinds = lax.broadcasted_iota(jnp.int32, (META, rows), 0)
    meta = jnp.where(kinds == 0, logq, jnp.where(kinds == 1, high, jnp.where(kinds == 2, low, 0.0)))
    msg_ref[pl.ds(rows, META), :] = meta.astype(jnp.bfloat16)
    inv_norm = lax.rsqrt(jnp.sum(projected * projected, axis=1, keepdims=True) + epsilon)
    normed = projected * inv_norm
    normed_ref[...] = normed
    inv_ref[...] = jnp.broadcast_to(inv_norm, inv_ref.shape)
    msg_ref[pl.ds(0, rows), :] = normed.astype(jnp.bfloat16)


def project(feats, tower_w, partners, buckets, parts):
    rows, din = feats.shape
    width = tower_w.shape[1]
    return pl.pallas_call(
        functools.partial(project_kernel, parts),
        out_shape=(
            jax.ShapeDtypeStruct((rows + META, width), jnp.bfloat16),
            jax.ShapeDtypeStruct((rows, width), jnp.float32),
            jax.ShapeDtypeStruct((rows, 128), jnp.float32),
        )
        + (jax.ShapeDtypeStruct((parts // 2, rows, din // parts), feats.dtype),) * 2,
        in_specs=[HBM, HBM, HBM, HBM],
        out_specs=(VMEM,) * 5,
        scratch_shapes=[
            pltpu.VMEM((din, width), jnp.bfloat16),
            pltpu.VMEM((1, rows), jnp.int32),
            pltpu.VMEM((1, rows), jnp.int32),
            pltpu.SemaphoreType.DMA((2, parts)),
            pltpu.SemaphoreType.DMA((2,)),
        ],
        compiler_params=pltpu.CompilerParams(vmem_limit_bytes=VMEM_LIMIT),
        cost_estimate=pl.CostEstimate(
            flops=2 * rows * din * width, bytes_accessed=2 * din * (rows + width), transcendentals=rows
        ),
        name="project",
    )(*(pltpu.with_memory_space_constraint(each, pltpu.HBM) for each in (feats, tower_w, partners, buckets)))


def folded(terms):
    total = terms[:, 0:128]
    for at in range(128, terms.shape[1], 128):
        total = total + terms[:, at:at + 128]
    return total


def rows_to_lanes(sums):
    return jnp.sum(jnp.transpose(sums), axis=0, keepdims=True)


def weight_of(msg_ref, counts_ref, flip):
    rows = msg_ref.shape[0] - META
    meta = msg_ref[pl.ds(rows, META), :].astype(jnp.float32)
    lanes = lax.broadcasted_iota(jnp.int32, (1, rows), 1)
    valid = lanes < counts_ref[lax.axis_index("dp"), lax.axis_index("pool") ^ flip]
    return jnp.where(valid, jnp.exp2(meta[0:1] * -LOG2E), 0.0)


def pair_sums(seen, fresh, counts_ref, msgs, sums_ref, own_ref, sums_out, kept_at):
    rows = own_ref.shape[0] if own_ref is not None else msgs[0].shape[0] - META
    emb = {k: msgs[k][pl.ds(0, rows), :] for k in seen + fresh}
    weight = {k: weight_of(msgs[k], counts_ref, k) for k in seen + fresh}
    sums = {k: sums_ref[k] for k in seen if k}
    own_sums = own_ref[...] if own_ref is not None else jnp.zeros((rows, 128), jnp.float32)
    off_diagonal = lax.broadcasted_iota(jnp.int32, (rows, rows), 0) != lax.broadcasted_iota(
        jnp.int32, (rows, rows), 1
    )

    def powers_of(left, right):
        return jnp.exp2(f32_dot(emb[left], emb[right], ((1,), (1,))) * EXP2_SCALE)

    def down(powers, column):
        return jnp.sum(powers * column, axis=0, keepdims=True)

    own_column = column_of(weight[0])[:, 0:1]
    for k in fresh:
        powers = powers_of(0, k)
        if k == 0:
            powers = jnp.where(off_diagonal, powers, 0.0)
        else:
            sums[k] = down(powers, own_column)
        kept_at(k)[...] = powers
        own_sums = own_sums + folded(powers * weight[k])
    others = [k for k in seen if k]
    for k in fresh:
        if k == 0:
            continue
        column = column_of(weight[k])[:, 0:1]
        mine = folded(jnp.where(off_diagonal, powers_of(k, k), 0.0) * weight[k])
        for other in others:
            powers = powers_of(k, other)
            mine = mine + folded(powers * weight[other])
            sums[other] = sums[other] + down(powers, column)
        sums[k] = sums[k] + rows_to_lanes(mine)
        others.append(k)
    return sums, own_sums, weight, own_column


def pairs_kernel(seen, fresh, *refs):
    known = seen + fresh
    counts_ref, refs = refs[0], refs[1:]
    msgs, refs = dict(zip(known, refs)), refs[len(known):]
    before = {}
    own_ref = None
    if seen:
        sums_ref, own_ref, refs = refs[0], refs[1], refs[2:]
        before = {k: sums_ref[at:at + 1, :] for at, k in enumerate(seen)}
    sums_out, own_out, kept_out = refs
    sums, own_sums, _, _ = pair_sums(
        seen, fresh, counts_ref, msgs, before, own_ref, sums_out, lambda k: kept_out.at[fresh.index(k)]
    )
    own_out[...] = own_sums
    for at, k in enumerate(known):
        sums_out[at:at + 1, :] = sums[k] if k else jnp.zeros_like(sums_out[0:1, :])


def pairs_cost(seen, fresh, rows, width):
    pairs = len(fresh) * len(seen) + len(fresh) * (len(fresh) + 1) // 2
    return pl.CostEstimate(
        flops=2 * pairs * rows * rows * width,
        bytes_accessed=2 * (len(seen) + len(fresh)) * rows * width + 4 * len(fresh) * rows * rows,
        transcendentals=pairs * rows * rows,
    )


def add_pairs(seen, fresh, counts, msgs, state):
    known = seen + fresh
    rows, width = msgs[0].shape[0] - META, msgs[0].shape[1]
    return pl.pallas_call(
        functools.partial(pairs_kernel, seen, fresh),
        out_shape=(
            jax.ShapeDtypeStruct((len(known), rows), jnp.float32),
            jax.ShapeDtypeStruct((rows, 128), jnp.float32),
            jax.ShapeDtypeStruct((len(fresh), rows, rows), jnp.float32),
        ),
        in_specs=[SMEM] + [VMEM] * (len(known) + len(state)),
        out_specs=(VMEM,) * 3,
        compiler_params=pltpu.CompilerParams(vmem_limit_bytes=VMEM_LIMIT),
        cost_estimate=pairs_cost(seen, fresh, rows, width),
        name="add_pairs",
    )(counts, *(msgs[k] for k in known), *state)


def grad_kernel(stages, fresh, *refs):
    seen = [k for stage in stages for k in stage]
    known = seen + fresh
    counts_ref, refs = refs[0], refs[1:]
    msgs, refs = dict(zip(known, refs)), refs[len(known):]
    sums_ref, own_ref, refs = refs[0], refs[1], refs[2:]
    stage_refs, refs = refs[:len(stages)], refs[len(stages):]
    normed_ref, inv_ref, out_ref, kept = refs[-4:]
    rows, width = normed_ref.shape
    before = {k: sums_ref[at:at + 1, :] for at, k in enumerate(seen)}
    sums, own_sums, weight, own_weight = pair_sums(
        seen, fresh, counts_ref, msgs, before, own_ref, None, lambda k: kept.at[fresh.index(k)]
    )
    sums[0] = rows_to_lanes(own_sums)
    places = {k: kept.at[at] for at, k in enumerate(fresh)}
    for stage, ref in zip(stages, stage_refs):
        for at, k in enumerate(stage):
            places[k] = ref.at[at]

    me = lax.axis_index("pool")
    lanes = lax.broadcasted_iota(jnp.int32, (1, rows), 1)
    own_rows = me * rows + lax.broadcasted_iota(jnp.int32, (rows, 1), 0)

    def partner_of(k):
        meta = msgs[k][pl.ds(rows, META), :].astype(jnp.float32)
        return jnp.where(weight[k] > 0.0, meta[1:2] * DIGIT + meta[2:3], -1.0)

    recip = {k: jnp.where(weight[k] > 0.0, 1.0 / sums[k], 0.0) for k in known}
    own_recip = column_of(recip[0])[:, 0:1]
    own_partner = column_of(partner_of(0))[:, 0:1].astype(jnp.int32)
    both = jnp.zeros((2 * rows, width), jnp.float32)
    for k in known:
        columns = (me ^ k) * rows + lanes
        powers = places[k][...]
        along = powers * weight[k] * own_recip - jnp.where(own_partner == columns, 1.0, 0.0)
        across = powers * own_weight * recip[k] - jnp.where(
            partner_of(k).astype(jnp.int32) == own_rows, 1.0, 0.0
        )
        coefficients = jnp.concatenate([along.astype(jnp.bfloat16), across.astype(jnp.bfloat16)], axis=0)
        both = both + f32_dot(coefficients, msgs[k][pl.ds(0, rows), :], ((1,), (0,)))
    grad = both[:rows] + both[rows:]
    normed = normed_ref[...]
    inward = jnp.sum(normed * grad, axis=1, keepdims=True)
    out_ref[0] = ((grad - normed * inward) * inv_ref[:, 0:1]).astype(jnp.bfloat16)


def group_grad(stages, fresh, counts, msgs, state, kept, earlier, normed, inv):
    seen = [k for stage in stages for k in stage]
    known = seen + fresh
    rows, width = normed.shape
    return pl.pallas_call(
        functools.partial(grad_kernel, stages, fresh),
        out_shape=jax.ShapeDtypeStruct((1, rows, width), jnp.bfloat16),
        in_specs=[SMEM] + [VMEM] * (len(known) + len(state) + len(kept) + len(earlier) + 2),
        out_specs=VMEM,
        scratch_shapes=[pltpu.VMEM((len(fresh), rows, rows), jnp.float32)],
        compiler_params=pltpu.CompilerParams(vmem_limit_bytes=VMEM_LIMIT),
        cost_estimate=pairs_cost(seen, fresh, rows, width),
        name="group_grad",
    )(counts, *(msgs[k] for k in known), *state, *kept, *earlier, normed, inv)


def distinct(arrays):
    found = []
    for array in arrays:
        if all(array is not other for other in found):
            found.append(array)
    return found, [next(at for at, other in enumerate(found) if array is other) for array in arrays]


def pack_kernel(places, *refs):
    for at, (array, row) in enumerate(places):
        refs[-1][at] = refs[array][row]


def pack(pieces, earlier=()):
    arrays, which = distinct([array for array, _ in pieces])
    shape = (len(pieces),) + arrays[0].shape[1:]
    return pl.pallas_call(
        functools.partial(pack_kernel, [(at, piece[1]) for at, piece in zip(which, pieces)]),
        out_shape=jax.ShapeDtypeStruct(shape, arrays[0].dtype),
        in_specs=[VMEM] * (len(arrays) + len(earlier)),
        out_specs=VMEM,
        compiler_params=pltpu.CompilerParams(vmem_limit_bytes=VMEM_LIMIT),
        cost_estimate=pl.CostEstimate(flops=0, bytes_accessed=4 * math.prod(shape), transcendentals=0),
        name="pack",
    )(*arrays, *earlier)


def weight_kernel(places, minor, inputs, *refs):
    arrays, outs, total = refs[:inputs], refs[inputs:-1], refs[-1]
    half, piece, _ = outs[0].shape
    me = lax.axis_index("pool")
    result = None
    for array, row, grad_array, grad_row in places:
        term = f32_dot(arrays[array][row], arrays[grad_array][grad_row], ((0,), (0,)))
        result = term if result is None else result + term
    total[...] = result
    for at, out in enumerate(outs):
        near, start = at // 2, half * (1 - at % 2)
        for far in range(half):
            first = pl.multiple_of((me ^ ((start + far) * minor + near)) * piece, piece)
            out[far] = total[pl.ds(first, piece), :].astype(out.dtype)


def weight_grad(blocks, grads, members, minor):
    blocks, grads = sorted(blocks, key=lambda each: each[0]), sorted(grads, key=lambda each: each[0])
    arrays, which = distinct([array for _, array, _ in blocks + grads])
    parts = len(blocks)
    places = [(which[at], blocks[at][2], which[parts + at], grads[at][2]) for at in range(parts)]
    _, rows, cols = blocks[0][1].shape
    width = grads[0][1].shape[2]
    pieces = (members // minor // 2, cols // members, width)
    return pl.pallas_call(
        functools.partial(weight_kernel, places, minor, len(arrays)),
        out_shape=(jax.ShapeDtypeStruct(pieces, jnp.float32),) * 2
        + (jax.ShapeDtypeStruct(pieces, jnp.bfloat16),) * (2 * minor - 2),
        in_specs=[VMEM] * len(arrays),
        out_specs=(VMEM,) * (2 * minor),
        scratch_shapes=[pltpu.VMEM((cols, width), jnp.float32)],
        compiler_params=pltpu.CompilerParams(vmem_limit_bytes=VMEM_LIMIT),
        cost_estimate=pl.CostEstimate(
            flops=2 * parts * rows * cols * width, bytes_accessed=2 * parts * rows * cols, transcendentals=0
        ),
        name="weight_grad",
    )(*arrays)


def add_pieces_kernel(came, own_ref, *refs):
    for far, out in enumerate(refs[came:]):
        total = own_ref[far]
        for ref in refs[:came]:
            total = total + ref[far].astype(jnp.float32)
        out[...] = total.astype(out.dtype)


def add_pieces(own, came, first_type):
    majors, *piece = own.shape
    return pl.pallas_call(
        functools.partial(add_pieces_kernel, len(came)),
        out_shape=(jax.ShapeDtypeStruct(piece, first_type),)
        + (jax.ShapeDtypeStruct(piece, jnp.bfloat16),) * (majors - 1),
        in_specs=[VMEM] * (1 + len(came)),
        out_specs=(VMEM,) * majors,
        compiler_params=pltpu.CompilerParams(vmem_limit_bytes=SMALL_VMEM_LIMIT),
        cost_estimate=pl.CostEstimate(flops=own.size, bytes_accessed=8 * own.size, transcendentals=0),
        name="add_pieces",
    )(own, *came)


def add_all_kernel(*refs):
    total = refs[0][...].astype(jnp.float32)
    for ref in refs[1:-1]:
        total = total + ref[...].astype(jnp.float32)
    refs[-1][...] = total


def add_all(pieces):
    return pl.pallas_call(
        add_all_kernel,
        out_shape=jax.ShapeDtypeStruct(pieces[0].shape, jnp.float32),
        in_specs=[VMEM] * len(pieces),
        out_specs=VMEM,
        compiler_params=pltpu.CompilerParams(vmem_limit_bytes=SMALL_VMEM_LIMIT),
        name="add_all",
    )(*pieces)


def swap(value, axis, flip):
    size = lax.axis_size(axis)
    return lax.ppermute(value, axis, [(at, at ^ flip) for at in range(size)])


def order_kernel(value_ref, *refs):
    refs[-1][...] = value_ref[...]


def after(value, *earlier):
    return pl.pallas_call(
        order_kernel,
        out_shape=jax.ShapeDtypeStruct(value.shape, value.dtype),
        in_specs=[VMEM] * (1 + len(earlier)),
        out_specs=VMEM,
        compiler_params=pltpu.CompilerParams(vmem_limit_bytes=SMALL_VMEM_LIMIT),
        name="after",
    )(value, *earlier)


def per_device(feats, tower_w, partners, popularity_buckets, row_counts):
    members = lax.axis_size("pool")
    parts = lax.axis_size("dp")
    minor = 1 << ((members.bit_length() - 1) // 2)
    msg, normed, inv, near_cuts, far_cuts = project(feats, tower_w, partners[None, :], popularity_buckets[None, :], parts)

    majors = list(range(0, members, minor))
    last = members // 2
    msgs = {0: msg}
    msgs[last] = swap(msg, "pool", last)
    for k in majors[1:]:
        if k < last:
            msgs[k] = swap(msg, "pool", k)
    for near in range(1, minor):
        msgs[near] = swap(msg, "pool", near)
    for far in majors[1:-2]:
        for near in range(1, minor):
            msgs[far + near] = swap(msgs[far], "pool", near)
    relayed = msgs[last]
    for k in majors:
        if k > last:
            msgs[k] = swap(relayed, "pool", k ^ last)
    for near in range(1, minor):
        msgs[last + near] = swap(msgs[last], "pool", near)

    came = swap(far_cuts, "dp", parts // 2)

    state, kept, stages = (), [], []

    def add(fresh):
        nonlocal state
        *state, powers = add_pairs(sum(stages, []), fresh, row_counts, msgs, state)
        kept.append(powers)
        stages.append(fresh)

    add(majors[:-1] + list(range(1, minor)))
    add([far + near for far in majors[1:-2] for near in range(1, minor)])
    msgs3 = after(msgs[majors[-1]], state[1])
    for near in range(1, minor):
        msgs[majors[-1] + near] = swap(msgs3, "pool", near)
    add([majors[-1]])
    add([majors[-2] + near for near in range(1, minor)])
    final = [majors[-1] + near for near in range(1, minor)]
    grad_proj = group_grad(stages, final, row_counts, msgs, state, kept, [], normed, inv)

    bit = parts // 2
    grads = [(0, grad_proj, 0), (bit, swap(grad_proj, "dp", bit), 0)]
    blocks = {k: [(0, near_cuts, k), (bit, came, k)] for k in range(bit)}
    bit //= 2
    while bit:
        moving = [(k ^ bit, source ^ bit, array, at) for k in blocks if k & bit for source, array, at in blocks[k]]
        blocks = {k: blocks[k] for k in blocks if not k & bit}
        passed = swap(pack([each[2:] for each in moving], [grads[-1][1]]), "dp", bit)
        for at, (k, source, _, _) in enumerate(moving):
            blocks[k].append((source, passed, at))
        bit //= 2
    bit = parts // 4
    while bit:
        sent = swap(pack([each[1:] for each in grads]), "dp", bit)
        grads += [(each[0] ^ bit, sent, at) for at, each in enumerate(grads)]
        bit //= 2

    own_far, own_near, *pieces = weight_grad(blocks[0], grads, members, minor)
    far_came = [swap(each, "pool", at + 1) for at, each in enumerate(pieces[0::2])]
    near_came = [swap(each, "pool", at + 1) for at, each in enumerate(pieces[1::2])]
    far_sums = add_pieces(own_far, far_came, jnp.bfloat16)
    total, *near_sums = add_pieces(own_near, near_came, jnp.float32)
    half = members // minor // 2
    far_came = [swap(each, "pool", (half + at) * minor) for at, each in enumerate(far_sums)]
    near_came = [swap(each, "pool", (1 + at) * minor) for at, each in enumerate(near_sums)]
    far_total = add_all(far_came)
    return add_all([total, far_total] + [after(each, far_total) for each in near_came])


def solution(mesh):
    return jax.shard_map(
        per_device,
        mesh=mesh,
        in_specs=(P(("dp", "pool"), None), P(), P(("dp", "pool")), P(("dp", "pool")), P()),
        out_specs=P(("dp", "pool"), None),
        check_vma=False,
    )
```

```python
import functools
import math

import jax
import jax.numpy as jnp
from jax import lax
from jax.experimental import pallas as pl
from jax.experimental.pallas import tpu as pltpu
from jax.sharding import PartitionSpec as P

sharpness_scaler = 0.05
epsilon = 1e-06
META = 16
DIGIT_BITS = 8
DIGIT = 1 << DIGIT_BITS
EXP2_SCALE = math.log2(math.e) / sharpness_scaler
LOG2E = math.log2(math.e)
VMEM_LIMIT = 40 * 1024 * 1024
SMALL_VMEM_LIMIT = 8 * 1024 * 1024

VMEM = pl.BlockSpec(memory_space=pltpu.VMEM)
SMEM = pl.BlockSpec(memory_space=pltpu.SMEM)
HBM = pl.BlockSpec(memory_space=pltpu.HBM)


def f32_dot(left, right, dims):
    return lax.dot_general(left, right, (dims, ((), ())), preferred_element_type=jnp.float32)


def column_of(row):
    return jnp.transpose(jnp.broadcast_to(row, (128, row.shape[1])))


def project_kernel(parts, feats_hbm, w_hbm, partners_hbm, buckets_hbm, msg_ref, normed_ref, inv_ref,
                   near_ref, far_ref, w_v, partners_ref, buckets_ref, sems, small_sems):
    half, rows, step = near_ref.shape
    cuts = [near_ref.at[k] for k in range(half)] + [far_ref.at[k] for k in range(half)]
    width = w_v.shape[1]
    me = lax.axis_index("dp")
    small = (
        pltpu.make_async_copy(partners_hbm, partners_ref, small_sems.at[0]),
        pltpu.make_async_copy(buckets_hbm, buckets_ref, small_sems.at[1]),
    )
    for copy in small:
        copy.start()
    copies = []
    for k in range(parts):
        first = pl.multiple_of((me ^ k) * step, step)
        cut = pl.ds(first, step)
        pair = (
            pltpu.make_async_copy(feats_hbm.at[:, cut], cuts[k], sems.at[0, k]),
            pltpu.make_async_copy(w_hbm.at[cut, :], w_v.at[pl.ds(k * step, step), :], sems.at[1, k]),
        )
        pair[0].start()
        pair[1].start()
        copies.append(pair)
    projected = jnp.zeros((rows, width), jnp.float32)
    for k in range(parts):
        copies[k][0].wait()
        copies[k][1].wait()
        projected = projected + f32_dot(cuts[k][...], w_v[pl.ds(k * step, step), :], ((1,), (0,)))
    for copy in small:
        copy.wait()
    partners = partners_ref[...]
    logq = -(buckets_ref[...].astype(jnp.float32) + 0.5) / 4.0
    high = (partners >> DIGIT_BITS).astype(jnp.float32)
    low = (partners & (DIGIT - 1)).astype(jnp.float32)
    kinds = lax.broadcasted_iota(jnp.int32, (META, rows), 0)
    meta = jnp.where(kinds == 0, logq, jnp.where(kinds == 1, high, jnp.where(kinds == 2, low, 0.0)))
    msg_ref[pl.ds(rows, META), :] = meta.astype(jnp.bfloat16)
    inv_norm = lax.rsqrt(jnp.sum(projected * projected, axis=1, keepdims=True) + epsilon)
    normed = projected * inv_norm
    normed_ref[...] = normed
    inv_ref[...] = jnp.broadcast_to(inv_norm, inv_ref.shape)
    msg_ref[pl.ds(0, rows), :] = normed.astype(jnp.bfloat16)


def project(feats, tower_w, partners, buckets, parts):
    rows, din = feats.shape
    width = tower_w.shape[1]
    return pl.pallas_call(
        functools.partial(project_kernel, parts),
        out_shape=(
            jax.ShapeDtypeStruct((rows + META, width), jnp.bfloat16),
            jax.ShapeDtypeStruct((rows, width), jnp.float32),
            jax.ShapeDtypeStruct((rows, 128), jnp.float32),
        )
        + (jax.ShapeDtypeStruct((parts // 2, rows, din // parts), feats.dtype),) * 2,
        in_specs=[HBM, HBM, HBM, HBM],
        out_specs=(VMEM,) * 5,
        scratch_shapes=[
            pltpu.VMEM((din, width), jnp.bfloat16),
            pltpu.VMEM((1, rows), jnp.int32),
            pltpu.VMEM((1, rows), jnp.int32),
            pltpu.SemaphoreType.DMA((2, parts)),
            pltpu.SemaphoreType.DMA((2,)),
        ],
        compiler_params=pltpu.CompilerParams(vmem_limit_bytes=VMEM_LIMIT),
        cost_estimate=pl.CostEstimate(
            flops=2 * rows * din * width, bytes_accessed=2 * din * (rows + width), transcendentals=rows
        ),
        name="project",
    )(*(pltpu.with_memory_space_constraint(each, pltpu.HBM) for each in (feats, tower_w, partners, buckets)))


def folded(terms):
    total = terms[:, 0:128]
    for at in range(128, terms.shape[1], 128):
        total = total + terms[:, at:at + 128]
    return total


def rows_to_lanes(sums):
    return jnp.sum(jnp.transpose(sums), axis=0, keepdims=True)


def weight_of(msg_ref, counts_ref, flip):
    rows = msg_ref.shape[0] - META
    meta = msg_ref[pl.ds(rows, META), :].astype(jnp.float32)
    lanes = lax.broadcasted_iota(jnp.int32, (1, rows), 1)
    valid = lanes < counts_ref[lax.axis_index("dp"), lax.axis_index("pool") ^ flip]
    return jnp.where(valid, jnp.exp2(meta[0:1] * -LOG2E), 0.0)


def pair_sums(seen, fresh, counts_ref, msgs, sums_ref, own_ref, sums_out, kept_at):
    rows = own_ref.shape[0] if own_ref is not None else msgs[0].shape[0] - META
    emb = {k: msgs[k][pl.ds(0, rows), :] for k in seen + fresh}
    weight = {k: weight_of(msgs[k], counts_ref, k) for k in seen + fresh}
    sums = {k: sums_ref[k] for k in seen if k}
    own_sums = own_ref[...] if own_ref is not None else jnp.zeros((rows, 128), jnp.float32)
    off_diagonal = lax.broadcasted_iota(jnp.int32, (rows, rows), 0) != lax.broadcasted_iota(
        jnp.int32, (rows, rows), 1
    )

    def powers_of(left, right):
        return jnp.exp2(f32_dot(emb[left], emb[right], ((1,), (1,))) * EXP2_SCALE)

    def down(powers, column):
        return jnp.sum(powers * column, axis=0, keepdims=True)

    own_column = column_of(weight[0])[:, 0:1]
    for k in fresh:
        powers = powers_of(0, k)
        if k == 0:
            powers = jnp.where(off_diagonal, powers, 0.0)
        along, across = powers * weight[k], powers * own_column
        kept_at(k)[0] = along
        kept_at(k)[1] = across
        if k:
            sums[k] = jnp.sum(across, axis=0, keepdims=True)
        own_sums = own_sums + folded(along)
    others = [k for k in seen if k]
    for k in fresh:
        if k == 0:
            continue
        column = column_of(weight[k])[:, 0:1]
        mine = folded(jnp.where(off_diagonal, powers_of(k, k), 0.0) * weight[k])
        for other in others:
            powers = powers_of(k, other)
            mine = mine + folded(powers * weight[other])
            sums[other] = sums[other] + down(powers, column)
        sums[k] = sums[k] + rows_to_lanes(mine)
        others.append(k)
    return sums, own_sums, weight


def pairs_kernel(seen, fresh, *refs):
    known = seen + fresh
    counts_ref, refs = refs[0], refs[1:]
    msgs, refs = dict(zip(known, refs)), refs[len(known):]
    before = {}
    own_ref = None
    if seen:
        sums_ref, own_ref, refs = refs[0], refs[1], refs[2:]
        before = {k: sums_ref[at:at + 1, :] for at, k in enumerate(seen)}
    sums_out, own_out, kept_out = refs
    sums, own_sums, _ = pair_sums(
        seen, fresh, counts_ref, msgs, before, own_ref, sums_out, lambda k: kept_out.at[fresh.index(k)]
    )
    own_out[...] = own_sums
    for at, k in enumerate(known):
        sums_out[at:at + 1, :] = sums[k] if k else jnp.zeros_like(sums_out[0:1, :])


def pairs_cost(seen, fresh, rows, width):
    pairs = len(fresh) * len(seen) + len(fresh) * (len(fresh) + 1) // 2
    return pl.CostEstimate(
        flops=2 * pairs * rows * rows * width,
        bytes_accessed=2 * (len(seen) + len(fresh)) * rows * width + 4 * len(fresh) * rows * rows,
        transcendentals=pairs * rows * rows,
    )


def add_pairs(seen, fresh, counts, msgs, state):
    known = seen + fresh
    rows, width = msgs[0].shape[0] - META, msgs[0].shape[1]
    return pl.pallas_call(
        functools.partial(pairs_kernel, seen, fresh),
        out_shape=(
            jax.ShapeDtypeStruct((len(known), rows), jnp.float32),
            jax.ShapeDtypeStruct((rows, 128), jnp.float32),
            jax.ShapeDtypeStruct((len(fresh), 2, rows, rows), jnp.float32),
        ),
        in_specs=[SMEM] + [VMEM] * (len(known) + len(state)),
        out_specs=(VMEM,) * 3,
        compiler_params=pltpu.CompilerParams(vmem_limit_bytes=VMEM_LIMIT),
        cost_estimate=pairs_cost(seen, fresh, rows, width),
        name="add_pairs",
    )(counts, *(msgs[k] for k in known), *state)


def grad_kernel(stages, fresh, *refs):
    seen = [k for stage in stages for k in stage]
    known = seen + fresh
    counts_ref, refs = refs[0], refs[1:]
    msgs, refs = dict(zip(known, refs)), refs[len(known):]
    sums_ref, own_ref, refs = refs[0], refs[1], refs[2:]
    stage_refs, refs = refs[:len(stages)], refs[len(stages):]
    normed_ref, inv_ref, out_ref, kept = refs[-4:]
    rows, width = normed_ref.shape
    before = {k: sums_ref[at:at + 1, :] for at, k in enumerate(seen)}
    sums, own_sums, weight = pair_sums(
        seen, fresh, counts_ref, msgs, before, own_ref, None, lambda k: kept.at[fresh.index(k)]
    )
    sums[0] = rows_to_lanes(own_sums)
    places = {k: kept.at[at] for at, k in enumerate(fresh)}
    for stage, ref in zip(stages, stage_refs):
        for at, k in enumerate(stage):
            places[k] = ref.at[at]

    me = lax.axis_index("pool")
    lanes = lax.broadcasted_iota(jnp.int32, (1, rows), 1)
    own_rows = me * rows + lax.broadcasted_iota(jnp.int32, (rows, 1), 0)

    def partner_of(k):
        meta = msgs[k][pl.ds(rows, META), :].astype(jnp.float32)
        return jnp.where(weight[k] > 0.0, meta[1:2] * DIGIT + meta[2:3], -1.0)

    recip = {k: jnp.where(weight[k] > 0.0, 1.0 / sums[k], 0.0) for k in known}
    own_recip = column_of(recip[0])[:, 0:1]
    own_partner = column_of(partner_of(0))[:, 0:1].astype(jnp.int32)
    both = jnp.zeros((2 * rows, width), jnp.float32)
    for k in known:
        columns = (me ^ k) * rows + lanes
        along = places[k][0] * own_recip - jnp.where(own_partner == columns, 1.0, 0.0)
        across = places[k][1] * recip[k] - jnp.where(
            partner_of(k).astype(jnp.int32) == own_rows, 1.0, 0.0
        )
        coefficients = jnp.concatenate([along.astype(jnp.bfloat16), across.astype(jnp.bfloat16)], axis=0)
        both = both + f32_dot(coefficients, msgs[k][pl.ds(0, rows), :], ((1,), (0,)))
    grad = both[:rows] + both[rows:]
    normed = normed_ref[...]
    inward = jnp.sum(normed * grad, axis=1, keepdims=True)
    out_ref[0] = ((grad - normed * inward) * inv_ref[:, 0:1]).astype(jnp.bfloat16)


def group_grad(stages, fresh, counts, msgs, state, kept, earlier, normed, inv):
    seen = [k for stage in stages for k in stage]
    known = seen + fresh
    rows, width = normed.shape
    return pl.pallas_call(
        functools.partial(grad_kernel, stages, fresh),
        out_shape=jax.ShapeDtypeStruct((1, rows, width), jnp.bfloat16),
        in_specs=[SMEM] + [VMEM] * (len(known) + len(state) + len(kept) + len(earlier) + 2),
        out_specs=VMEM,
        scratch_shapes=[pltpu.VMEM((len(fresh), 2, rows, rows), jnp.float32)],
        compiler_params=pltpu.CompilerParams(vmem_limit_bytes=VMEM_LIMIT),
        cost_estimate=pairs_cost(seen, fresh, rows, width),
        name="group_grad",
    )(counts, *(msgs[k] for k in known), *state, *kept, *earlier, normed, inv)


def distinct(arrays):
    found = []
    for array in arrays:
        if all(array is not other for other in found):
            found.append(array)
    return found, [next(at for at, other in enumerate(found) if array is other) for array in arrays]


def pack_kernel(places, *refs):
    for at, (array, row) in enumerate(places):
        refs[-1][at] = refs[array][row]


def pack(pieces, earlier=()):
    arrays, which = distinct([array for array, _ in pieces])
    shape = (len(pieces),) + arrays[0].shape[1:]
    return pl.pallas_call(
        functools.partial(pack_kernel, [(at, piece[1]) for at, piece in zip(which, pieces)]),
        out_shape=jax.ShapeDtypeStruct(shape, arrays[0].dtype),
        in_specs=[VMEM] * (len(arrays) + len(earlier)),
        out_specs=VMEM,
        compiler_params=pltpu.CompilerParams(vmem_limit_bytes=VMEM_LIMIT),
        cost_estimate=pl.CostEstimate(flops=0, bytes_accessed=4 * math.prod(shape), transcendentals=0),
        name="pack",
    )(*arrays, *earlier)


def weight_kernel(places, minor, inputs, *refs):
    arrays, outs, total = refs[:inputs], refs[inputs:-1], refs[-1]
    half, piece, _ = outs[0].shape
    me = lax.axis_index("pool")
    result = None
    for array, row, grad_array, grad_row in places:
        term = f32_dot(arrays[array][row], arrays[grad_array][grad_row], ((0,), (0,)))
        result = term if result is None else result + term
    total[...] = result
    for at, out in enumerate(outs):
        near, start = at // 2, half * (1 - at % 2)
        for far in range(half):
            first = pl.multiple_of((me ^ ((start + far) * minor + near)) * piece, piece)
            out[far] = total[pl.ds(first, piece), :].astype(out.dtype)


def weight_grad(blocks, grads, members, minor):
    blocks, grads = sorted(blocks, key=lambda each: each[0]), sorted(grads, key=lambda each: each[0])
    arrays, which = distinct([array for _, array, _ in blocks + grads])
    parts = len(blocks)
    places = [(which[at], blocks[at][2], which[parts + at], grads[at][2]) for at in range(parts)]
    _, rows, cols = blocks[0][1].shape
    width = grads[0][1].shape[2]
    pieces = (members // minor // 2, cols // members, width)
    return pl.pallas_call(
        functools.partial(weight_kernel, places, minor, len(arrays)),
        out_shape=(jax.ShapeDtypeStruct(pieces, jnp.float32),) * 2
        + (jax.ShapeDtypeStruct(pieces, jnp.bfloat16),) * (2 * minor - 2),
        in_specs=[VMEM] * len(arrays),
        out_specs=(VMEM,) * (2 * minor),
        scratch_shapes=[pltpu.VMEM((cols, width), jnp.float32)],
        compiler_params=pltpu.CompilerParams(vmem_limit_bytes=VMEM_LIMIT),
        cost_estimate=pl.CostEstimate(
            flops=2 * parts * rows * cols * width, bytes_accessed=2 * parts * rows * cols, transcendentals=0
        ),
        name="weight_grad",
    )(*arrays)


def add_pieces_kernel(came, own_ref, *refs):
    for far, out in enumerate(refs[came:]):
        total = own_ref[far]
        for ref in refs[:came]:
            total = total + ref[far].astype(jnp.float32)
        out[...] = total.astype(out.dtype)


def add_pieces(own, came, first_type):
    majors, *piece = own.shape
    return pl.pallas_call(
        functools.partial(add_pieces_kernel, len(came)),
        out_shape=(jax.ShapeDtypeStruct(piece, first_type),)
        + (jax.ShapeDtypeStruct(piece, jnp.bfloat16),) * (majors - 1),
        in_specs=[VMEM] * (1 + len(came)),
        out_specs=(VMEM,) * majors,
        compiler_params=pltpu.CompilerParams(vmem_limit_bytes=SMALL_VMEM_LIMIT),
        cost_estimate=pl.CostEstimate(flops=own.size, bytes_accessed=8 * own.size, transcendentals=0),
        name="add_pieces",
    )(own, *came)


def add_all_kernel(*refs):
    total = refs[0][...].astype(jnp.float32)
    for ref in refs[1:-1]:
        total = total + ref[...].astype(jnp.float32)
    refs[-1][...] = total


def add_all(pieces):
    return pl.pallas_call(
        add_all_kernel,
        out_shape=jax.ShapeDtypeStruct(pieces[0].shape, jnp.float32),
        in_specs=[VMEM] * len(pieces),
        out_specs=VMEM,
        compiler_params=pltpu.CompilerParams(vmem_limit_bytes=SMALL_VMEM_LIMIT),
        name="add_all",
    )(*pieces)


def swap(value, axis, flip):
    size = lax.axis_size(axis)
    return lax.ppermute(value, axis, [(at, at ^ flip) for at in range(size)])


def order_kernel(value_ref, *refs):
    refs[-1][...] = value_ref[...]


def after(value, *earlier):
    return pl.pallas_call(
        order_kernel,
        out_shape=jax.ShapeDtypeStruct(value.shape, value.dtype),
        in_specs=[VMEM] * (1 + len(earlier)),
        out_specs=VMEM,
        compiler_params=pltpu.CompilerParams(vmem_limit_bytes=SMALL_VMEM_LIMIT),
        name="after",
    )(value, *earlier)


def per_device(feats, tower_w, partners, popularity_buckets, row_counts):
    members = lax.axis_size("pool")
    parts = lax.axis_size("dp")
    minor = 1 << ((members.bit_length() - 1) // 2)
    msg, normed, inv, near_cuts, far_cuts = project(feats, tower_w, partners[None, :], popularity_buckets[None, :], parts)

    majors = list(range(0, members, minor))
    last = members // 2
    msgs = {0: msg}
    msgs[last] = swap(msg, "pool", last)
    for k in majors[1:]:
        if k < last:
            msgs[k] = swap(msg, "pool", k)
    for near in range(1, minor):
        msgs[near] = swap(msg, "pool", near)
    for far in majors[1:-2]:
        for near in range(1, minor):
            msgs[far + near] = swap(msgs[far], "pool", near)
    relayed = msgs[last]
    for k in majors:
        if k > last:
            msgs[k] = swap(relayed, "pool", k ^ last)
    for near in range(1, minor):
        msgs[last + near] = swap(msgs[last], "pool", near)

    came = swap(far_cuts, "dp", parts // 2)

    state, kept, stages = (), [], []

    def add(fresh):
        nonlocal state
        *state, powers = add_pairs(sum(stages, []), fresh, row_counts, msgs, state)
        kept.append(powers)
        stages.append(fresh)

    add(majors[:-1] + list(range(1, minor)))
    add([far + near for far in majors[1:-2] for near in range(1, minor)])
    msgs3 = after(msgs[majors[-1]], state[1])
    for near in range(1, minor):
        msgs[majors[-1] + near] = swap(msgs3, "pool", near)
    add([majors[-1]])
    add([majors[-2] + near for near in range(1, minor)])
    final = [majors[-1] + near for near in range(1, minor)]
    grad_proj = group_grad(stages, final, row_counts, msgs, state, kept, [], normed, inv)

    bit = parts // 2
    grads = [(0, grad_proj, 0), (bit, swap(grad_proj, "dp", bit), 0)]
    blocks = {k: [(0, near_cuts, k), (bit, came, k)] for k in range(bit)}
    bit //= 2
    while bit:
        moving = [(k ^ bit, source ^ bit, array, at) for k in blocks if k & bit for source, array, at in blocks[k]]
        blocks = {k: blocks[k] for k in blocks if not k & bit}
        passed = swap(pack([each[2:] for each in moving], [grads[-1][1]]), "dp", bit)
        for at, (k, source, _, _) in enumerate(moving):
            blocks[k].append((source, passed, at))
        bit //= 2
    bit = parts // 4
    while bit:
        sent = swap(pack([each[1:] for each in grads]), "dp", bit)
        grads += [(each[0] ^ bit, sent, at) for at, each in enumerate(grads)]
        bit //= 2

    own_far, own_near, *pieces = weight_grad(blocks[0], grads, members, minor)
    far_came = [swap(each, "pool", at + 1) for at, each in enumerate(pieces[0::2])]
    near_came = [swap(each, "pool", at + 1) for at, each in enumerate(pieces[1::2])]
    far_sums = add_pieces(own_far, far_came, jnp.bfloat16)
    total, *near_sums = add_pieces(own_near, near_came, jnp.float32)
    half = members // minor // 2
    far_came = [swap(each, "pool", (half + at) * minor) for at, each in enumerate(far_sums)]
    near_came = [swap(each, "pool", (1 + at) * minor) for at, each in enumerate(near_sums)]
    far_total = add_all(far_came)
    return add_all([total, far_total] + [after(each, far_total) for each in near_came])


def solution(mesh):
    return jax.shard_map(
        per_device,
        mesh=mesh,
        in_specs=(P(("dp", "pool"), None), P(), P(("dp", "pool")), P(("dp", "pool")), P()),
        out_specs=P(("dp", "pool"), None),
        check_vma=False,
    )
```

```python
import functools
import math

import jax
import jax.numpy as jnp
from jax import lax
from jax.experimental import pallas as pl
from jax.experimental.pallas import tpu as pltpu
from jax.sharding import PartitionSpec as P

sharpness_scaler = 0.05
epsilon = 1e-06
META = 16
DIGIT_BITS = 8
DIGIT = 1 << DIGIT_BITS
EXP2_SCALE = math.log2(math.e) / sharpness_scaler
LOG2E = math.log2(math.e)
VMEM_LIMIT = 40 * 1024 * 1024
SMALL_VMEM_LIMIT = 8 * 1024 * 1024

VMEM = pl.BlockSpec(memory_space=pltpu.VMEM)
SMEM = pl.BlockSpec(memory_space=pltpu.SMEM)
HBM = pl.BlockSpec(memory_space=pltpu.HBM)


def f32_dot(left, right, dims):
    return lax.dot_general(left, right, (dims, ((), ())), preferred_element_type=jnp.float32)


def column_of(row):
    return jnp.transpose(jnp.broadcast_to(row, (128, row.shape[1])))


def project_kernel(parts, feats_hbm, w_hbm, partners_hbm, buckets_hbm, msg_ref, normed_ref, inv_ref,
                   near_ref, far_ref, w_v, partners_ref, buckets_ref, sems, small_sems):
    half, rows, step = near_ref.shape
    cuts = [near_ref.at[k] for k in range(half)] + [far_ref.at[k] for k in range(half)]
    width = w_v.shape[1]
    me = lax.axis_index("dp")
    small = (
        pltpu.make_async_copy(partners_hbm, partners_ref, small_sems.at[0]),
        pltpu.make_async_copy(buckets_hbm, buckets_ref, small_sems.at[1]),
    )
    for copy in small:
        copy.start()
    w_copy = pltpu.make_async_copy(w_hbm, w_v, small_sems.at[2])
    w_copy.start()
    firsts = [pl.multiple_of((me ^ k) * step, step) for k in range(parts)]
    copies = [
        pltpu.make_async_copy(feats_hbm.at[:, pl.ds(first, step)], cut, sems.at[k])
        for k, (first, cut) in enumerate(zip(firsts, cuts))
    ]
    for copy in copies:
        copy.start()
    w_copy.wait()
    projected = jnp.zeros((rows, width), jnp.float32)
    for copy, first, cut in zip(copies, firsts, cuts):
        copy.wait()
        projected = projected + f32_dot(cut[...], w_v[pl.ds(first, step), :], ((1,), (0,)))
    for copy in small:
        copy.wait()
    partners = partners_ref[...]
    logq = -(buckets_ref[...].astype(jnp.float32) + 0.5) / 4.0
    high = (partners >> DIGIT_BITS).astype(jnp.float32)
    low = (partners & (DIGIT - 1)).astype(jnp.float32)
    kinds = lax.broadcasted_iota(jnp.int32, (META, rows), 0)
    meta = jnp.where(kinds == 0, logq, jnp.where(kinds == 1, high, jnp.where(kinds == 2, low, 0.0)))
    msg_ref[pl.ds(rows, META), :] = meta.astype(jnp.bfloat16)
    inv_norm = lax.rsqrt(jnp.sum(projected * projected, axis=1, keepdims=True) + epsilon)
    normed = projected * inv_norm
    normed_ref[...] = normed
    inv_ref[...] = jnp.broadcast_to(inv_norm, inv_ref.shape)
    msg_ref[pl.ds(0, rows), :] = normed.astype(jnp.bfloat16)


def project(feats, tower_w, partners, buckets, parts):
    rows, din = feats.shape
    width = tower_w.shape[1]
    return pl.pallas_call(
        functools.partial(project_kernel, parts),
        out_shape=(
            jax.ShapeDtypeStruct((rows + META, width), jnp.bfloat16),
            jax.ShapeDtypeStruct((rows, width), jnp.float32),
            jax.ShapeDtypeStruct((rows, 128), jnp.float32),
        )
        + (jax.ShapeDtypeStruct((parts // 2, rows, din // parts), feats.dtype),) * 2,
        in_specs=[HBM, HBM, HBM, HBM],
        out_specs=(VMEM,) * 5,
        scratch_shapes=[
            pltpu.VMEM((din, width), jnp.bfloat16),
            pltpu.VMEM((1, rows), jnp.int32),
            pltpu.VMEM((1, rows), jnp.int32),
            pltpu.SemaphoreType.DMA((parts,)),
            pltpu.SemaphoreType.DMA((3,)),
        ],
        compiler_params=pltpu.CompilerParams(vmem_limit_bytes=VMEM_LIMIT),
        cost_estimate=pl.CostEstimate(
            flops=2 * rows * din * width, bytes_accessed=2 * din * (rows + width), transcendentals=rows
        ),
        name="project",
    )(*(pltpu.with_memory_space_constraint(each, pltpu.HBM) for each in (feats, tower_w, partners, buckets)))


def folded(terms):
    total = terms[:, 0:128]
    for at in range(128, terms.shape[1], 128):
        total = total + terms[:, at:at + 128]
    return total


def rows_to_lanes(sums):
    return jnp.sum(jnp.transpose(sums), axis=0, keepdims=True)


def weight_of(msg_ref, counts_ref, flip):
    rows = msg_ref.shape[0] - META
    meta = msg_ref[pl.ds(rows, META), :].astype(jnp.float32)
    lanes = lax.broadcasted_iota(jnp.int32, (1, rows), 1)
    valid = lanes < counts_ref[lax.axis_index("dp"), lax.axis_index("pool") ^ flip]
    return jnp.where(valid, jnp.exp2(meta[0:1] * -LOG2E), 0.0)


def pair_sums(seen, fresh, counts_ref, msgs, sums_ref, own_ref, sums_out, kept_at):
    rows = own_ref.shape[0] if own_ref is not None else msgs[0].shape[0] - META
    emb = {k: msgs[k][pl.ds(0, rows), :] for k in seen + fresh}
    weight = {k: weight_of(msgs[k], counts_ref, k) for k in seen + fresh}
    sums = {k: sums_ref[k] for k in seen if k}
    own_sums = own_ref[...] if own_ref is not None else jnp.zeros((rows, 128), jnp.float32)
    off_diagonal = lax.broadcasted_iota(jnp.int32, (rows, rows), 0) != lax.broadcasted_iota(
        jnp.int32, (rows, rows), 1
    )

    def powers_of(left, right):
        return jnp.exp2(f32_dot(emb[left], emb[right], ((1,), (1,))) * EXP2_SCALE)

    def down(powers, column):
        return jnp.sum(powers * column, axis=0, keepdims=True)

    own_column = column_of(weight[0])[:, 0:1]
    for k in fresh:
        powers = powers_of(0, k)
        if k == 0:
            powers = jnp.where(off_diagonal, powers, 0.0)
        along, across = powers * weight[k], powers * own_column
        kept_at(k)[0] = along
        kept_at(k)[1] = across
        if k:
            sums[k] = jnp.sum(across, axis=0, keepdims=True)
        own_sums = own_sums + folded(along)
    others = [k for k in seen if k]
    for k in fresh:
        if k == 0:
            continue
        column = column_of(weight[k])[:, 0:1]
        mine = folded(jnp.where(off_diagonal, powers_of(k, k), 0.0) * weight[k])
        for other in others:
            powers = powers_of(k, other)
            mine = mine + folded(powers * weight[other])
            sums[other] = sums[other] + down(powers, column)
        sums[k] = sums[k] + rows_to_lanes(mine)
        others.append(k)
    return sums, own_sums, weight


def pairs_kernel(seen, fresh, *refs):
    known = seen + fresh
    counts_ref, refs = refs[0], refs[1:]
    msgs, refs = dict(zip(known, refs)), refs[len(known):]
    before = {}
    own_ref = None
    if seen:
        sums_ref, own_ref, refs = refs[0], refs[1], refs[2:]
        before = {k: sums_ref[at:at + 1, :] for at, k in enumerate(seen)}
    sums_out, own_out, kept_out = refs
    sums, own_sums, _ = pair_sums(
        seen, fresh, counts_ref, msgs, before, own_ref, sums_out, lambda k: kept_out.at[fresh.index(k)]
    )
    own_out[...] = own_sums
    for at, k in enumerate(known):
        sums_out[at:at + 1, :] = sums[k] if k else jnp.zeros_like(sums_out[0:1, :])


def pairs_cost(seen, fresh, rows, width):
    pairs = len(fresh) * len(seen) + len(fresh) * (len(fresh) + 1) // 2
    return pl.CostEstimate(
        flops=2 * pairs * rows * rows * width,
        bytes_accessed=2 * (len(seen) + len(fresh)) * rows * width + 4 * len(fresh) * rows * rows,
        transcendentals=pairs * rows * rows,
    )


def add_pairs(seen, fresh, counts, msgs, state):
    known = seen + fresh
    rows, width = msgs[0].shape[0] - META, msgs[0].shape[1]
    return pl.pallas_call(
        functools.partial(pairs_kernel, seen, fresh),
        out_shape=(
            jax.ShapeDtypeStruct((len(known), rows), jnp.float32),
            jax.ShapeDtypeStruct((rows, 128), jnp.float32),
            jax.ShapeDtypeStruct((len(fresh), 2, rows, rows), jnp.float32),
        ),
        in_specs=[SMEM] + [VMEM] * (len(known) + len(state)),
        out_specs=(VMEM,) * 3,
        compiler_params=pltpu.CompilerParams(vmem_limit_bytes=VMEM_LIMIT),
        cost_estimate=pairs_cost(seen, fresh, rows, width),
        name="add_pairs",
    )(counts, *(msgs[k] for k in known), *state)


def grad_kernel(stages, fresh, *refs):
    seen = [k for stage in stages for k in stage]
    known = seen + fresh
    counts_ref, refs = refs[0], refs[1:]
    msgs, refs = dict(zip(known, refs)), refs[len(known):]
    sums_ref, own_ref, refs = refs[0], refs[1], refs[2:]
    stage_refs, refs = refs[:len(stages)], refs[len(stages):]
    normed_ref, inv_ref, out_ref, kept = refs[-4:]
    rows, width = normed_ref.shape
    before = {k: sums_ref[at:at + 1, :] for at, k in enumerate(seen)}
    sums, own_sums, weight = pair_sums(
        seen, fresh, counts_ref, msgs, before, own_ref, None, lambda k: kept.at[fresh.index(k)]
    )
    sums[0] = rows_to_lanes(own_sums)
    places = {k: kept.at[at] for at, k in enumerate(fresh)}
    for stage, ref in zip(stages, stage_refs):
        for at, k in enumerate(stage):
            places[k] = ref.at[at]

    me = lax.axis_index("pool")
    lanes = lax.broadcasted_iota(jnp.int32, (1, rows), 1)
    own_rows = me * rows + lax.broadcasted_iota(jnp.int32, (rows, 1), 0)

    def partner_of(k):
        meta = msgs[k][pl.ds(rows, META), :].astype(jnp.float32)
        return jnp.where(weight[k] > 0.0, meta[1:2] * DIGIT + meta[2:3], -1.0)

    recip = {k: jnp.where(weight[k] > 0.0, 1.0 / sums[k], 0.0) for k in known}
    own_recip = column_of(recip[0])[:, 0:1]
    own_partner = column_of(partner_of(0))[:, 0:1].astype(jnp.int32)
    both = jnp.zeros((2 * rows, width), jnp.float32)
    for k in known:
        columns = (me ^ k) * rows + lanes
        along = places[k][0] * own_recip - jnp.where(own_partner == columns, 1.0, 0.0)
        across = places[k][1] * recip[k] - jnp.where(
            partner_of(k).astype(jnp.int32) == own_rows, 1.0, 0.0
        )
        coefficients = jnp.concatenate([along.astype(jnp.bfloat16), across.astype(jnp.bfloat16)], axis=0)
        both = both + f32_dot(coefficients, msgs[k][pl.ds(0, rows), :], ((1,), (0,)))
    grad = both[:rows] + both[rows:]
    normed = normed_ref[...]
    inward = jnp.sum(normed * grad, axis=1, keepdims=True)
    out_ref[0] = ((grad - normed * inward) * inv_ref[:, 0:1]).astype(jnp.bfloat16)


def group_grad(stages, fresh, counts, msgs, state, kept, earlier, normed, inv):
    seen = [k for stage in stages for k in stage]
    known = seen + fresh
    rows, width = normed.shape
    return pl.pallas_call(
        functools.partial(grad_kernel, stages, fresh),
        out_shape=jax.ShapeDtypeStruct((1, rows, width), jnp.bfloat16),
        in_specs=[SMEM] + [VMEM] * (len(known) + len(state) + len(kept) + len(earlier) + 2),
        out_specs=VMEM,
        scratch_shapes=[pltpu.VMEM((len(fresh), 2, rows, rows), jnp.float32)],
        compiler_params=pltpu.CompilerParams(vmem_limit_bytes=VMEM_LIMIT),
        cost_estimate=pairs_cost(seen, fresh, rows, width),
        name="group_grad",
    )(counts, *(msgs[k] for k in known), *state, *kept, *earlier, normed, inv)


def distinct(arrays):
    found = []
    for array in arrays:
        if all(array is not other for other in found):
            found.append(array)
    return found, [next(at for at, other in enumerate(found) if array is other) for array in arrays]


def pack_kernel(places, *refs):
    for at, (array, row) in enumerate(places):
        refs[-1][at] = refs[array][row]


def pack(pieces, earlier=()):
    arrays, which = distinct([array for array, _ in pieces])
    shape = (len(pieces),) + arrays[0].shape[1:]
    return pl.pallas_call(
        functools.partial(pack_kernel, [(at, piece[1]) for at, piece in zip(which, pieces)]),
        out_shape=jax.ShapeDtypeStruct(shape, arrays[0].dtype),
        in_specs=[VMEM] * (len(arrays) + len(earlier)),
        out_specs=VMEM,
        compiler_params=pltpu.CompilerParams(vmem_limit_bytes=VMEM_LIMIT),
        cost_estimate=pl.CostEstimate(flops=0, bytes_accessed=4 * math.prod(shape), transcendentals=0),
        name="pack",
    )(*arrays, *earlier)


def weight_kernel(places, minor, inputs, *refs):
    arrays, outs, total = refs[:inputs], refs[inputs:-1], refs[-1]
    half, piece, _ = outs[0].shape
    me = lax.axis_index("pool")
    result = None
    for array, row, grad_array, grad_row in places:
        term = f32_dot(arrays[array][row], arrays[grad_array][grad_row], ((0,), (0,)))
        result = term if result is None else result + term
    total[...] = result
    for at, out in enumerate(outs):
        near, start = at // 2, half * (1 - at % 2)
        for far in range(half):
            first = pl.multiple_of((me ^ ((start + far) * minor + near)) * piece, piece)
            out[far] = total[pl.ds(first, piece), :].astype(out.dtype)


def weight_grad(blocks, grads, members, minor):
    blocks, grads = sorted(blocks, key=lambda each: each[0]), sorted(grads, key=lambda each: each[0])
    arrays, which = distinct([array for _, array, _ in blocks + grads])
    parts = len(blocks)
    places = [(which[at], blocks[at][2], which[parts + at], grads[at][2]) for at in range(parts)]
    _, rows, cols = blocks[0][1].shape
    width = grads[0][1].shape[2]
    pieces = (members // minor // 2, cols // members, width)
    return pl.pallas_call(
        functools.partial(weight_kernel, places, minor, len(arrays)),
        out_shape=(jax.ShapeDtypeStruct(pieces, jnp.float32),) * 2
        + (jax.ShapeDtypeStruct(pieces, jnp.bfloat16),) * (2 * minor - 2),
        in_specs=[VMEM] * len(arrays),
        out_specs=(VMEM,) * (2 * minor),
        scratch_shapes=[pltpu.VMEM((cols, width), jnp.float32)],
        compiler_params=pltpu.CompilerParams(vmem_limit_bytes=VMEM_LIMIT),
        cost_estimate=pl.CostEstimate(
            flops=2 * parts * rows * cols * width, bytes_accessed=2 * parts * rows * cols, transcendentals=0
        ),
        name="weight_grad",
    )(*arrays)


def add_pieces_kernel(came, own_ref, *refs):
    for far, out in enumerate(refs[came:]):
        total = own_ref[far]
        for ref in refs[:came]:
            total = total + ref[far].astype(jnp.float32)
        out[...] = total.astype(out.dtype)


def add_pieces(own, came, first_type):
    majors, *piece = own.shape
    return pl.pallas_call(
        functools.partial(add_pieces_kernel, len(came)),
        out_shape=(jax.ShapeDtypeStruct(piece, first_type),)
        + (jax.ShapeDtypeStruct(piece, jnp.bfloat16),) * (majors - 1),
        in_specs=[VMEM] * (1 + len(came)),
        out_specs=(VMEM,) * majors,
        compiler_params=pltpu.CompilerParams(vmem_limit_bytes=SMALL_VMEM_LIMIT),
        cost_estimate=pl.CostEstimate(flops=own.size, bytes_accessed=8 * own.size, transcendentals=0),
        name="add_pieces",
    )(own, *came)


def add_all_kernel(*refs):
    total = refs[0][...].astype(jnp.float32)
    for ref in refs[1:-1]:
        total = total + ref[...].astype(jnp.float32)
    refs[-1][...] = total


def add_all(pieces):
    return pl.pallas_call(
        add_all_kernel,
        out_shape=jax.ShapeDtypeStruct(pieces[0].shape, jnp.float32),
        in_specs=[VMEM] * len(pieces),
        out_specs=VMEM,
        compiler_params=pltpu.CompilerParams(vmem_limit_bytes=SMALL_VMEM_LIMIT),
        name="add_all",
    )(*pieces)


def swap(value, axis, flip):
    size = lax.axis_size(axis)
    return lax.ppermute(value, axis, [(at, at ^ flip) for at in range(size)])


def order_kernel(value_ref, *refs):
    refs[-1][...] = value_ref[...]


def after(value, *earlier):
    return pl.pallas_call(
        order_kernel,
        out_shape=jax.ShapeDtypeStruct(value.shape, value.dtype),
        in_specs=[VMEM] * (1 + len(earlier)),
        out_specs=VMEM,
        compiler_params=pltpu.CompilerParams(vmem_limit_bytes=SMALL_VMEM_LIMIT),
        name="after",
    )(value, *earlier)


def per_device(feats, tower_w, partners, popularity_buckets, row_counts):
    members = lax.axis_size("pool")
    parts = lax.axis_size("dp")
    minor = 1 << ((members.bit_length() - 1) // 2)
    msg, normed, inv, near_cuts, far_cuts = project(feats, tower_w, partners[None, :], popularity_buckets[None, :], parts)

    majors = list(range(0, members, minor))
    last = members // 2
    msgs = {0: msg}
    msgs[last] = swap(msg, "pool", last)
    for k in majors[1:]:
        if k < last:
            msgs[k] = swap(msg, "pool", k)
    for near in range(1, minor):
        msgs[near] = swap(msg, "pool", near)
    for far in majors[1:-2]:
        for near in range(1, minor):
            msgs[far + near] = swap(msgs[far], "pool", near)
    relayed = msgs[last]
    for k in majors:
        if k > last:
            msgs[k] = swap(relayed, "pool", k ^ last)
    for near in range(1, minor):
        msgs[last + near] = swap(msgs[last], "pool", near)

    came = swap(far_cuts, "dp", parts // 2)

    state, kept, stages = (), [], []

    def add(fresh):
        nonlocal state
        *state, powers = add_pairs(sum(stages, []), fresh, row_counts, msgs, state)
        kept.append(powers)
        stages.append(fresh)

    add(majors[:-1] + list(range(1, minor)))
    add([far + near for far in majors[1:-2] for near in range(1, minor)])
    msgs3 = after(msgs[majors[-1]], state[1])
    for near in range(1, minor):
        msgs[majors[-1] + near] = swap(msgs3, "pool", near)
    add([majors[-1]])
    add([majors[-2] + near for near in range(1, minor)])
    final = [majors[-1] + near for near in range(1, minor)]
    grad_proj = group_grad(stages, final, row_counts, msgs, state, kept, [], normed, inv)

    bit = parts // 2
    grads = [(0, grad_proj, 0), (bit, swap(grad_proj, "dp", bit), 0)]
    blocks = {k: [(0, near_cuts, k), (bit, came, k)] for k in range(bit)}
    bit //= 2
    while bit:
        moving = [(k ^ bit, source ^ bit, array, at) for k in blocks if k & bit for source, array, at in blocks[k]]
        blocks = {k: blocks[k] for k in blocks if not k & bit}
        passed = swap(pack([each[2:] for each in moving], [grads[-1][1]]), "dp", bit)
        for at, (k, source, _, _) in enumerate(moving):
            blocks[k].append((source, passed, at))
        bit //= 2
    bit = parts // 4
    while bit:
        sent = swap(pack([each[1:] for each in grads]), "dp", bit)
        grads += [(each[0] ^ bit, sent, at) for at, each in enumerate(grads)]
        bit //= 2

    own_far, own_near, *pieces = weight_grad(blocks[0], grads, members, minor)
    far_came = [swap(each, "pool", at + 1) for at, each in enumerate(pieces[0::2])]
    near_came = [swap(each, "pool", at + 1) for at, each in enumerate(pieces[1::2])]
    far_sums = add_pieces(own_far, far_came, jnp.bfloat16)
    total, *near_sums = add_pieces(own_near, near_came, jnp.float32)
    half = members // minor // 2
    far_came = [swap(each, "pool", (half + at) * minor) for at, each in enumerate(far_sums)]
    near_came = [swap(each, "pool", (1 + at) * minor) for at, each in enumerate(near_sums)]
    far_total = add_all(far_came)
    return add_all([total, far_total] + [after(each, far_total) for each in near_came])


def solution(mesh):
    return jax.shard_map(
        per_device,
        mesh=mesh,
        in_specs=(P(("dp", "pool"), None), P(), P(("dp", "pool")), P(("dp", "pool")), P()),
        out_specs=P(("dp", "pool"), None),
        check_vma=False,
    )
```

```python
import functools
import math

import jax
import jax.numpy as jnp
from jax import lax
from jax.experimental import pallas as pl
from jax.experimental.pallas import tpu as pltpu
from jax.sharding import PartitionSpec as P

sharpness_scaler = 0.05
epsilon = 1e-06
META = 16
DIGIT_BITS = 8
DIGIT = 1 << DIGIT_BITS
EXP2_SCALE = math.log2(math.e) / sharpness_scaler
LOG2E = math.log2(math.e)
VMEM_LIMIT = 40 * 1024 * 1024
SMALL_VMEM_LIMIT = 8 * 1024 * 1024

VMEM = pl.BlockSpec(memory_space=pltpu.VMEM)
SMEM = pl.BlockSpec(memory_space=pltpu.SMEM)
HBM = pl.BlockSpec(memory_space=pltpu.HBM)


def f32_dot(left, right, dims):
    return lax.dot_general(left, right, (dims, ((), ())), preferred_element_type=jnp.float32)


def column_of(row):
    return jnp.transpose(jnp.broadcast_to(row, (128, row.shape[1])))


def project_kernel(parts, feats_hbm, w_hbm, partners_hbm, buckets_hbm, msg_ref, normed_ref, inv_ref,
                   near_ref, far_ref, w_v, partners_ref, buckets_ref, sems, small_sems):
    half, rows, step = near_ref.shape
    cuts = [near_ref.at[k] for k in range(half)] + [far_ref.at[k] for k in range(half)]
    width = w_v.shape[1]
    me = lax.axis_index("dp")
    small = (
        pltpu.make_async_copy(partners_hbm, partners_ref, small_sems.at[0]),
        pltpu.make_async_copy(buckets_hbm, buckets_ref, small_sems.at[1]),
    )
    for copy in small:
        copy.start()
    copies = []
    for k in range(parts):
        first = pl.multiple_of((me ^ k) * step, step)
        cut = pl.ds(first, step)
        pair = (
            pltpu.make_async_copy(feats_hbm.at[:, cut], cuts[k], sems.at[0, k]),
            pltpu.make_async_copy(w_hbm.at[cut, :], w_v.at[pl.ds(k * step, step), :], sems.at[1, k]),
        )
        pair[0].start()
        pair[1].start()
        copies.append(pair)
    projected = jnp.zeros((rows, width), jnp.float32)
    for k in range(parts):
        copies[k][0].wait()
        copies[k][1].wait()
        projected = projected + f32_dot(cuts[k][...], w_v[pl.ds(k * step, step), :], ((1,), (0,)))
    for copy in small:
        copy.wait()
    partners = partners_ref[...]
    logq = -(buckets_ref[...].astype(jnp.float32) + 0.5) / 4.0
    high = (partners >> DIGIT_BITS).astype(jnp.float32)
    low = (partners & (DIGIT - 1)).astype(jnp.float32)
    kinds = lax.broadcasted_iota(jnp.int32, (META, rows), 0)
    meta = jnp.where(kinds == 0, logq, jnp.where(kinds == 1, high, jnp.where(kinds == 2, low, 0.0)))
    msg_ref[pl.ds(rows, META), :] = meta.astype(jnp.bfloat16)
    inv_norm = lax.rsqrt(jnp.sum(projected * projected, axis=1, keepdims=True) + epsilon)
    normed = projected * inv_norm
    normed_ref[...] = normed
    inv_ref[...] = jnp.broadcast_to(inv_norm, inv_ref.shape)
    msg_ref[pl.ds(0, rows), :] = normed.astype(jnp.bfloat16)


def project(feats, tower_w, partners, buckets, parts):
    rows, din = feats.shape
    width = tower_w.shape[1]
    return pl.pallas_call(
        functools.partial(project_kernel, parts),
        out_shape=(
            jax.ShapeDtypeStruct((rows + META, width), jnp.bfloat16),
            jax.ShapeDtypeStruct((rows, width), jnp.float32),
            jax.ShapeDtypeStruct((rows, 128), jnp.float32),
        )
        + (jax.ShapeDtypeStruct((parts // 2, rows, din // parts), feats.dtype),) * 2,
        in_specs=[HBM, HBM, HBM, HBM],
        out_specs=(VMEM,) * 5,
        scratch_shapes=[
            pltpu.VMEM((din, width), jnp.bfloat16),
            pltpu.VMEM((1, rows), jnp.int32),
            pltpu.VMEM((1, rows), jnp.int32),
            pltpu.SemaphoreType.DMA((2, parts)),
            pltpu.SemaphoreType.DMA((2,)),
        ],
        compiler_params=pltpu.CompilerParams(vmem_limit_bytes=VMEM_LIMIT),
        cost_estimate=pl.CostEstimate(
            flops=2 * rows * din * width, bytes_accessed=2 * din * (rows + width), transcendentals=rows
        ),
        name="project",
    )(*(pltpu.with_memory_space_constraint(each, pltpu.HBM) for each in (feats, tower_w, partners, buckets)))


def folded(terms):
    total = terms[:, 0:128]
    for at in range(128, terms.shape[1], 128):
        total = total + terms[:, at:at + 128]
    return total


def rows_to_lanes(sums):
    return jnp.sum(jnp.transpose(sums), axis=0, keepdims=True)


def weight_of(msg_ref, counts_ref, flip):
    rows = msg_ref.shape[0] - META
    meta = msg_ref[pl.ds(rows, META), :].astype(jnp.float32)
    lanes = lax.broadcasted_iota(jnp.int32, (1, rows), 1)
    valid = lanes < counts_ref[lax.axis_index("dp"), lax.axis_index("pool") ^ flip]
    return jnp.where(valid, jnp.exp2(meta[0:1] * -LOG2E), 0.0)


def pair_sums(seen, fresh, counts_ref, msgs, sums_ref, own_ref, sums_out, kept_at):
    rows = own_ref.shape[0] if own_ref is not None else msgs[0].shape[0] - META
    emb = {k: msgs[k][pl.ds(0, rows), :] for k in seen + fresh}
    weight = {k: weight_of(msgs[k], counts_ref, k) for k in seen + fresh}
    sums = {k: sums_ref[k] for k in seen if k}
    own_sums = own_ref[...] if own_ref is not None else jnp.zeros((rows, 128), jnp.float32)
    off_diagonal = lax.broadcasted_iota(jnp.int32, (rows, rows), 0) != lax.broadcasted_iota(
        jnp.int32, (rows, rows), 1
    )

    def powers_of(left, right):
        return jnp.exp2(f32_dot(emb[left], emb[right], ((1,), (1,))) * EXP2_SCALE)

    def down(powers, column):
        return jnp.sum(powers * column, axis=0, keepdims=True)

    own_column = column_of(weight[0])[:, 0:1]
    for k in fresh:
        powers = powers_of(0, k)
        if k == 0:
            powers = jnp.where(off_diagonal, powers, 0.0)
        along, across = powers * weight[k], powers * own_column
        kept_at(k)[0] = along
        kept_at(k)[1] = across
        if k:
            sums[k] = jnp.sum(across, axis=0, keepdims=True)
        own_sums = own_sums + folded(along)
    others = [k for k in seen if k]
    for k in fresh:
        if k == 0:
            continue
        column = column_of(weight[k])[:, 0:1]
        mine = folded(jnp.where(off_diagonal, powers_of(k, k), 0.0) * weight[k])
        for other in others:
            powers = powers_of(k, other)
            mine = mine + folded(powers * weight[other])
            sums[other] = sums[other] + down(powers, column)
        sums[k] = sums[k] + rows_to_lanes(mine)
        others.append(k)
    return sums, own_sums, weight


def pairs_kernel(seen, fresh, *refs):
    known = seen + fresh
    counts_ref, refs = refs[0], refs[1:]
    msgs, refs = dict(zip(known, refs)), refs[len(known):]
    before = {}
    own_ref = None
    if seen:
        sums_ref, own_ref, refs = refs[0], refs[1], refs[2:]
        before = {k: sums_ref[at:at + 1, :] for at, k in enumerate(seen)}
    sums_out, own_out, kept_out = refs
    sums, own_sums, _ = pair_sums(
        seen, fresh, counts_ref, msgs, before, own_ref, sums_out, lambda k: kept_out.at[fresh.index(k)]
    )
    own_out[...] = own_sums
    for at, k in enumerate(known):
        sums_out[at:at + 1, :] = sums[k] if k else jnp.zeros_like(sums_out[0:1, :])


def pairs_cost(seen, fresh, rows, width):
    pairs = len(fresh) * len(seen) + len(fresh) * (len(fresh) + 1) // 2
    return pl.CostEstimate(
        flops=2 * pairs * rows * rows * width,
        bytes_accessed=2 * (len(seen) + len(fresh)) * rows * width + 4 * len(fresh) * rows * rows,
        transcendentals=pairs * rows * rows,
    )


def add_pairs(seen, fresh, counts, msgs, state):
    known = seen + fresh
    rows, width = msgs[0].shape[0] - META, msgs[0].shape[1]
    return pl.pallas_call(
        functools.partial(pairs_kernel, seen, fresh),
        out_shape=(
            jax.ShapeDtypeStruct((len(known), rows), jnp.float32),
            jax.ShapeDtypeStruct((rows, 128), jnp.float32),
            jax.ShapeDtypeStruct((len(fresh), 2, rows, rows), jnp.float32),
        ),
        in_specs=[SMEM] + [VMEM] * (len(known) + len(state)),
        out_specs=(VMEM,) * 3,
        compiler_params=pltpu.CompilerParams(vmem_limit_bytes=VMEM_LIMIT),
        cost_estimate=pairs_cost(seen, fresh, rows, width),
        name="add_pairs",
    )(counts, *(msgs[k] for k in known), *state)


def grad_kernel(stages, fresh, *refs):
    seen = [k for stage in stages for k in stage]
    known = seen + fresh
    counts_ref, refs = refs[0], refs[1:]
    msgs, refs = dict(zip(known, refs)), refs[len(known):]
    sums_ref, own_ref, refs = refs[0], refs[1], refs[2:]
    stage_refs, refs = refs[:len(stages)], refs[len(stages):]
    normed_ref, inv_ref, out_ref, kept = refs[-4:]
    rows, width = normed_ref.shape
    before = {k: sums_ref[at:at + 1, :] for at, k in enumerate(seen)}
    sums, own_sums, weight = pair_sums(
        seen, fresh, counts_ref, msgs, before, own_ref, None, lambda k: kept.at[fresh.index(k)]
    )
    sums[0] = rows_to_lanes(own_sums)
    places = {k: kept.at[at] for at, k in enumerate(fresh)}
    for stage, ref in zip(stages, stage_refs):
        for at, k in enumerate(stage):
            places[k] = ref.at[at]

    me = lax.axis_index("pool")
    lanes = lax.broadcasted_iota(jnp.int32, (1, rows), 1)
    own_rows = me * rows + lax.broadcasted_iota(jnp.int32, (rows, 1), 0)

    def partner_of(k):
        meta = msgs[k][pl.ds(rows, META), :].astype(jnp.float32)
        return jnp.where(weight[k] > 0.0, meta[1:2] * DIGIT + meta[2:3], -1.0)

    recip = {k: jnp.where(weight[k] > 0.0, 1.0 / sums[k], 0.0) for k in known}
    own_recip = column_of(recip[0])[:, 0:1]
    own_partner = column_of(partner_of(0))[:, 0:1].astype(jnp.int32)
    both = jnp.zeros((2 * rows, width), jnp.float32)
    for k in known:
        columns = (me ^ k) * rows + lanes
        along = places[k][0] * own_recip - jnp.where(own_partner == columns, 1.0, 0.0)
        across = places[k][1] * recip[k] - jnp.where(
            partner_of(k).astype(jnp.int32) == own_rows, 1.0, 0.0
        )
        coefficients = jnp.concatenate([along.astype(jnp.bfloat16), across.astype(jnp.bfloat16)], axis=0)
        both = both + f32_dot(coefficients, msgs[k][pl.ds(0, rows), :], ((1,), (0,)))
    grad = both[:rows] + both[rows:]
    normed = normed_ref[...]
    inward = jnp.sum(normed * grad, axis=1, keepdims=True)
    out_ref[0] = ((grad - normed * inward) * inv_ref[:, 0:1]).astype(jnp.bfloat16)


def group_grad(stages, fresh, counts, msgs, state, kept, earlier, normed, inv):
    seen = [k for stage in stages for k in stage]
    known = seen + fresh
    rows, width = normed.shape
    return pl.pallas_call(
        functools.partial(grad_kernel, stages, fresh),
        out_shape=jax.ShapeDtypeStruct((1, rows, width), jnp.bfloat16),
        in_specs=[SMEM] + [VMEM] * (len(known) + len(state) + len(kept) + len(earlier) + 2),
        out_specs=VMEM,
        scratch_shapes=[pltpu.VMEM((len(fresh), 2, rows, rows), jnp.float32)],
        compiler_params=pltpu.CompilerParams(vmem_limit_bytes=VMEM_LIMIT),
        cost_estimate=pairs_cost(seen, fresh, rows, width),
        name="group_grad",
    )(counts, *(msgs[k] for k in known), *state, *kept, *earlier, normed, inv)


def distinct(arrays):
    found = []
    for array in arrays:
        if all(array is not other for other in found):
            found.append(array)
    return found, [next(at for at, other in enumerate(found) if array is other) for array in arrays]


def pack_kernel(places, *refs):
    for at, (array, row) in enumerate(places):
        refs[-1][at] = refs[array][row]


def pack(pieces, earlier=()):
    arrays, which = distinct([array for array, _ in pieces])
    shape = (len(pieces),) + arrays[0].shape[1:]
    return pl.pallas_call(
        functools.partial(pack_kernel, [(at, piece[1]) for at, piece in zip(which, pieces)]),
        out_shape=jax.ShapeDtypeStruct(shape, arrays[0].dtype),
        in_specs=[VMEM] * (len(arrays) + len(earlier)),
        out_specs=VMEM,
        compiler_params=pltpu.CompilerParams(vmem_limit_bytes=VMEM_LIMIT),
        cost_estimate=pl.CostEstimate(flops=0, bytes_accessed=4 * math.prod(shape), transcendentals=0),
        name="pack",
    )(*arrays, *earlier)


def weight_kernel(places, minor, inputs, *refs):
    arrays, outs, total = refs[:inputs], refs[inputs:-1], refs[-1]
    half, piece, _ = outs[0].shape
    me = lax.axis_index("pool")
    result = None
    for array, row, grad_array, grad_row in places:
        term = f32_dot(arrays[array][row], arrays[grad_array][grad_row], ((0,), (0,)))
        result = term if result is None else result + term
    total[...] = result
    for at, out in enumerate(outs):
        near, start = at // 2, half * (1 - at % 2)
        for far in range(half):
            first = pl.multiple_of((me ^ ((start + far) * minor + near)) * piece, piece)
            out[far] = total[pl.ds(first, piece), :].astype(out.dtype)


def weight_grad(blocks, grads, members, minor):
    blocks, grads = sorted(blocks, key=lambda each: each[0]), sorted(grads, key=lambda each: each[0])
    arrays, which = distinct([array for _, array, _ in blocks + grads])
    parts = len(blocks)
    places = [(which[at], blocks[at][2], which[parts + at], grads[at][2]) for at in range(parts)]
    _, rows, cols = blocks[0][1].shape
    width = grads[0][1].shape[2]
    pieces = (members // minor // 2, cols // members, width)
    return pl.pallas_call(
        functools.partial(weight_kernel, places, minor, len(arrays)),
        out_shape=(jax.ShapeDtypeStruct(pieces, jnp.float32),) * 2
        + (jax.ShapeDtypeStruct(pieces, jnp.bfloat16),) * (2 * minor - 2),
        in_specs=[VMEM] * len(arrays),
        out_specs=(VMEM,) * (2 * minor),
        scratch_shapes=[pltpu.VMEM((cols, width), jnp.float32)],
        compiler_params=pltpu.CompilerParams(vmem_limit_bytes=VMEM_LIMIT),
        cost_estimate=pl.CostEstimate(
            flops=2 * parts * rows * cols * width, bytes_accessed=2 * parts * rows * cols, transcendentals=0
        ),
        name="weight_grad",
    )(*arrays)


def add_pieces_kernel(came, own_ref, *refs):
    for far, out in enumerate(refs[came:]):
        total = own_ref[far]
        for ref in refs[:came]:
            total = total + ref[far].astype(jnp.float32)
        out[...] = total.astype(out.dtype)


def add_pieces(own, came, first_type):
    majors, *piece = own.shape
    return pl.pallas_call(
        functools.partial(add_pieces_kernel, len(came)),
        out_shape=(jax.ShapeDtypeStruct(piece, first_type),)
        + (jax.ShapeDtypeStruct(piece, jnp.bfloat16),) * (majors - 1),
        in_specs=[VMEM] * (1 + len(came)),
        out_specs=(VMEM,) * majors,
        compiler_params=pltpu.CompilerParams(vmem_limit_bytes=SMALL_VMEM_LIMIT),
        cost_estimate=pl.CostEstimate(flops=own.size, bytes_accessed=8 * own.size, transcendentals=0),
        name="add_pieces",
    )(own, *came)


def add_all_kernel(*refs):
    total = refs[0][...].astype(jnp.float32)
    for ref in refs[1:-1]:
        total = total + ref[...].astype(jnp.float32)
    refs[-1][...] = total


def add_all(pieces):
    return pl.pallas_call(
        add_all_kernel,
        out_shape=jax.ShapeDtypeStruct(pieces[0].shape, jnp.float32),
        in_specs=[VMEM] * len(pieces),
        out_specs=VMEM,
        compiler_params=pltpu.CompilerParams(vmem_limit_bytes=SMALL_VMEM_LIMIT),
        name="add_all",
    )(*pieces)


def swap(value, axis, flip):
    size = lax.axis_size(axis)
    return lax.ppermute(value, axis, [(at, at ^ flip) for at in range(size)])


def order_kernel(value_ref, *refs):
    refs[-1][...] = value_ref[...]


def after(value, *earlier):
    return pl.pallas_call(
        order_kernel,
        out_shape=jax.ShapeDtypeStruct(value.shape, value.dtype),
        in_specs=[VMEM] * (1 + len(earlier)),
        out_specs=VMEM,
        compiler_params=pltpu.CompilerParams(vmem_limit_bytes=SMALL_VMEM_LIMIT),
        name="after",
    )(value, *earlier)


def per_device(feats, tower_w, partners, popularity_buckets, row_counts):
    members = lax.axis_size("pool")
    parts = lax.axis_size("dp")
    minor = 1 << ((members.bit_length() - 1) // 2)
    msg, normed, inv, near_cuts, far_cuts = project(feats, tower_w, partners[None, :], popularity_buckets[None, :], parts)

    majors = list(range(0, members, minor))
    last = members // 2
    msgs = {0: msg}
    msgs[last] = swap(msg, "pool", last)
    for k in majors[1:]:
        if k < last:
            msgs[k] = swap(msg, "pool", k)
    for near in range(1, minor):
        msgs[near] = swap(msg, "pool", near)
    for far in majors[1:-2]:
        for near in range(1, minor):
            msgs[far + near] = swap(msgs[far], "pool", near)
    relayed = msgs[last]
    for k in majors:
        if k > last:
            msgs[k] = swap(relayed, "pool", k ^ last)
    for near in range(1, minor):
        msgs[last + near] = swap(msgs[last], "pool", near)

    came = swap(far_cuts, "dp", parts // 2)

    state, kept, stages = (), [], []

    def add(fresh):
        nonlocal state
        *state, powers = add_pairs(sum(stages, []), fresh, row_counts, msgs, state)
        kept.append(powers)
        stages.append(fresh)

    add(majors[:-1] + list(range(1, minor)))
    add([far + near for far in majors[1:-2] for near in range(1, minor)])
    msgs3 = after(msgs[majors[-1]], state[1])
    for near in range(1, minor):
        msgs[majors[-1] + near] = swap(msgs3, "pool", near)
    add([majors[-1]])
    add([majors[-2] + near for near in range(1, minor)])
    final = [majors[-1] + near for near in range(1, minor)]
    grad_proj = group_grad(stages, final, row_counts, msgs, state, kept, [], normed, inv)

    bit = parts // 2
    grads = [(0, grad_proj, 0), (bit, swap(grad_proj, "dp", bit), 0)]
    blocks = {k: [(0, near_cuts, k), (bit, came, k)] for k in range(bit)}
    bit //= 2
    while bit:
        moving = [(k ^ bit, source ^ bit, array, at) for k in blocks if k & bit for source, array, at in blocks[k]]
        blocks = {k: blocks[k] for k in blocks if not k & bit}
        passed = swap(pack([each[2:] for each in moving], [grads[-1][1]]), "dp", bit)
        for at, (k, source, _, _) in enumerate(moving):
            blocks[k].append((source, passed, at))
        bit //= 2
    bit = parts // 4
    while bit:
        sent = swap(pack([each[1:] for each in grads]), "dp", bit)
        grads += [(each[0] ^ bit, sent, at) for at, each in enumerate(grads)]
        bit //= 2

    own_far, own_near, *pieces = weight_grad(blocks[0], grads, members, minor)
    far_came = [swap(each, "pool", at + 1) for at, each in enumerate(pieces[0::2])]
    near_came = [swap(each, "pool", at + 1) for at, each in enumerate(pieces[1::2])]
    far_sums = add_pieces(own_far, far_came, jnp.bfloat16)
    total, *near_sums = add_pieces(own_near, near_came, jnp.float32)
    half = members // minor // 2
    far_came = [swap(far_sums[at], "pool", (half + at) * minor) for at in reversed(range(half))]
    near_came = [swap(each, "pool", (1 + at) * minor) for at, each in enumerate(near_sums)]
    far_total = add_all(far_came)
    return add_all([total, far_total] + [after(each, far_total) for each in near_came])


def solution(mesh):
    return jax.shard_map(
        per_device,
        mesh=mesh,
        in_specs=(P(("dp", "pool"), None), P(), P(("dp", "pool")), P(("dp", "pool")), P()),
        out_specs=P(("dp", "pool"), None),
        check_vma=False,
    )
```
